512 devices in a mesh: gx: 8 (over z_lo, core), gy: 16 (over z_hi, y), orb: 4 (over x).
Axes of the slice: x: 4, y: 8, z: 8 (z_hi: 2, z_lo: 4; z = z_hi * 4 + z_lo), core: 2. Of those that a mesh axis runs over, the one named last changes fastest.
Arguments:
- orbitals: float32 [16, 96, 256, 128], P('orb', 'gx', 'gy'), may hold values from -1800 to 1800
- potential: float32 [96, 256, 128], P('gx', 'gy'), may hold values from -2 to 0
- kinetic_mu: float32 [96, 256, 128], P('gx', 'gy'), may hold values from 0.2 to 1
- projectors: float32 [1024, 8, 512], P(('gx', 'gy')), may hold values from -4 to 4
- strengths: float32 [1024, 8], P(('gx', 'gy')), may hold values from -4 to 8
- box_offsets: int32 [1024, 3], P(('gx', 'gy')), may hold values from 0 to 120, as said below
- block_counts: int32 [128], P(('gx', 'gy')), may hold values from 1 to 8, as said below
Outputs:
- orthonormal: float32 [16, 96, 256, 128], P('orb', 'gx', 'gy')
The draws below stay inside these ranges and needn't reach their ends.
Inputs may be any that keep to these rules, and one draw needn't show every extreme that they name: `box_offsets`: column 0 lies in 2 to 14, column 1 in 2 to 18, column 2 in 0 to 120. `block_counts`: some tile has all 8 slots live, and some tile only one.
All inputs are finite; a program needn't handle non-finite values.
Results may differ from the reference program's by a relative error of at most 0.0003.
Values sent between devices are 32-bit elements; how exact they have to be, the bound alone decides.
No kernel may reach another device: no remote copies, remote signals or barrier semaphores. Data moves between devices by JAX's collectives and lax.ppermute only.
A program may use at most 64 MiB of HBM per device.

```python
import math
from functools import partial
import jax
import jax.numpy as jnp
from jax import lax

NORB = 16
CX = 12
CY = 16
NZ = 128
NA_DEV = 8
STEPS = 3
NPROJ = 8
BOX_EDGE = 8
HALO = 6
NX = 96
NY = 256
TILES = 128
SLOTS = 1024
N_GY = 16


def draw_orbitals(key, part):
    key = jax.random.fold_in(key, 11)
    base_key, orbital_key, cell_key = jax.random.split(key, 3)
    shape = (NORB, NX, NY, NZ)
    orbital_scale = 10.0 ** jax.random.uniform(orbital_key, (NORB, 1, 1, 1), jnp.float32)
    cell_scale = 10.0 ** jax.random.uniform(cell_key, (1, NX, NY, NZ), jnp.float32)
    x_ramp = (3.0 ** (jnp.arange(NX, dtype=jnp.float32) / max(NX - 1, 1))).reshape(1, NX, 1, 1)
    base_draw = jnp.clip(jax.random.normal(base_key, shape, jnp.float32), -6.0, 6.0)
    return (base_draw * orbital_scale * cell_scale * x_ramp).astype(jnp.float32)


def draw_box_offsets(key, part):
    key = jax.random.fold_in(key, 23)
    first_key, second_key, third_key = jax.random.split(key, 3)
    along_x = jax.random.randint(first_key, (SLOTS,), 2, CX + 3)
    along_y = jax.random.randint(second_key, (SLOTS,), 2, CY + 3)
    along_z = jax.random.randint(third_key, (SLOTS,), 0, NZ - BOX_EDGE + 1)
    within = jnp.arange(SLOTS, dtype=jnp.int32) % NA_DEV
    along_x = jnp.where(within == 0, 2, jnp.where(within == 1, CX + 2, along_x))
    along_y = jnp.where(within == 0, CY + 2, jnp.where(within == 1, 2, along_y))
    return jnp.stack([along_x, along_y, along_z], axis=1).astype(jnp.int32)


def draw_block_counts(key, part):
    key = jax.random.fold_in(key, 37)
    count_key, full_key = jax.random.split(key, 2)
    counts = jax.random.randint(count_key, (TILES,), 1, NA_DEV + 1)
    chosen = jax.random.randint(full_key, (), 0, TILES)
    sparse = (chosen + TILES // 2) % TILES
    tile_ids = jnp.arange(TILES)
    counts = jnp.where(tile_ids == chosen, NA_DEV, counts)
    counts = jnp.where(tile_ids == sparse, 1, counts)
    return counts.astype(jnp.int32)


def levels(own_key, shape, cuts, low, top_value):
    gain, own = 1.0, jax.random.fold_in(own_key, 6)
    for axis_at, shards_of in cuts:
        steps = jnp.exp(jax.random.uniform(jax.random.fold_in(own, axis_at), (shards_of,), jnp.float32, low / len(cuts), top_value / len(cuts)))
        gain = gain * jnp.repeat(steps, shape[axis_at] // shards_of).reshape([-1 if axis == axis_at else 1 for axis in range(len(shape))])
    return gain


def gaussian(key, shape, scale, most, shards=(), kind=jnp.bfloat16):
    level = levels(key, shape, shards, -0.22, 0.18) if shards else 1.0
    values = jax.random.normal(key, shape, jnp.float32) * scale * level
    return jnp.minimum(jnp.maximum(values, -most), most).astype(kind)


def setup_inputs(seed: int = 0) -> dict:
    keys = jax.random.split(jax.random.key(seed), 8)
    orbitals = draw_orbitals(jax.random.fold_in(keys[7], 71), 0)
    potential = jnp.clip(-2.0 + 2.0 * jax.random.uniform(keys[1], (NX, NY, NZ), jnp.float32) ** levels(keys[1], (NX, NY, NZ), ((0, 8), (1, 16)), -0.2, 0.2), -2.0, 0.0)
    kinetic_mu = jnp.clip(jnp.exp(math.log(1.0) - 1.609438 * jax.random.uniform(keys[2], (NX, NY, NZ), jnp.float32) ** levels(keys[2], (NX, NY, NZ), ((0, 8), (1, 16)), -0.2, 0.2)), 0.2, 1.0)
    projectors = gaussian(keys[3], (SLOTS, NPROJ, BOX_EDGE * BOX_EDGE * BOX_EDGE), 1.0, 4.0, ((0, 128),), jnp.float32)
    strengths = jnp.clip(-4.0 + 12.0 * jax.random.uniform(keys[4], (SLOTS, NPROJ), jnp.float32) ** levels(keys[4], (SLOTS, NPROJ), ((0, 128),), -0.2, 0.2), -4.0, 8.0)
    box_offsets = draw_box_offsets(jax.random.fold_in(keys[7], 71), 0)
    block_counts = draw_block_counts(jax.random.fold_in(keys[7], 71), 0)
    return {"orbitals": orbitals, "potential": potential, "kinetic_mu": kinetic_mu, "projectors": projectors, "strengths": strengths, "box_offsets": box_offsets, "block_counts": block_counts}


first_coefs = (6.0 / 7.0, -15.0 / 56.0, 5.0 / 63.0, -1.0 / 56.0, 2.0 / 825.0, -1.0 / 5544.0)
second_coefs = (12.0 / 7.0, -15.0 / 56.0, 10.0 / 189.0, -1.0 / 112.0, 2.0 / 1925.0, -1.0 / 16632.0)
center_coef = -5369.0 / 1800.0
filter_center = 13.5
filter_half = 10.5

def neighbour(extended, direction, offset):
    leading = extended.ndim - 3
    starts = [0] * extended.ndim
    limits = list(extended.shape)
    for dim_index in range(3):
        starts[leading + dim_index] = HALO
        limits[leading + dim_index] = extended.shape[leading + dim_index] - HALO
    starts[leading + direction] += offset
    limits[leading + direction] += offset
    return lax.slice(extended, starts, limits)

def pad_depth(padded):
    return jnp.pad(padded, [(0, 0)] * (padded.ndim - 1) + [(HALO, HALO)])

def gradient(extended):
    result = []
    for direction in range(3):
        summed = first_coefs[0] * (neighbour(extended, direction, 1) - neighbour(extended, direction, -1))
        for offset in range(2, HALO + 1):
            summed = summed + first_coefs[offset - 1] * (neighbour(extended, direction, offset) - neighbour(extended, direction, -offset))
        result.append(summed)
    return result

def laplacian(extended):
    summed = 3.0 * center_coef * neighbour(extended, 0, 0)
    for direction in range(3):
        for offset in range(1, HALO + 1):
            summed = summed + second_coefs[offset - 1] * (neighbour(extended, direction, offset) + neighbour(extended, direction, -offset))
    return summed

def local_terms(padded, grad_mu, kinetic_mu, potential):
    extended = pad_depth(padded)
    laplace = laplacian(extended)
    slopes = gradient(extended)
    cross_term = grad_mu[0] * slopes[0] + grad_mu[1] * slopes[1] + grad_mu[2] * slopes[2]
    return -0.5 * (1.0 + kinetic_mu) * laplace - 0.5 * cross_term + potential * neighbour(extended, 0, 0)

def chebyshev(start, hamiltonian):
    previous = start
    current = (hamiltonian(start) - filter_center * start) / filter_half
    for repeat in range(STEPS - 1):
        following = 2.0 * (hamiltonian(current) - filter_center * current) / filter_half - previous
        previous, current = (current, following)
    return current

def add_atom(slot_index, accumulated, padded, projectors, strengths, box_offsets, block_counts):
    norm_scale = BOX_EDGE ** (-1.5)
    tile_index = slot_index // NA_DEV
    start_x = (tile_index // N_GY * CX + box_offsets[slot_index, 0]).astype(jnp.int32)
    start_y = (tile_index % N_GY * CY + box_offsets[slot_index, 1]).astype(jnp.int32)
    start_z = box_offsets[slot_index, 2].astype(jnp.int32)
    is_live = (slot_index % NA_DEV < block_counts[tile_index]).astype(jnp.float32)
    starts = (start_x, start_y, start_z)
    extent = (BOX_EDGE, BOX_EDGE, BOX_EDGE)
    support = lax.dynamic_slice(padded, starts, extent).reshape(-1)
    table = projectors[slot_index]
    coeffs = jnp.dot(table, support, precision=lax.Precision.HIGHEST) * norm_scale
    weights = coeffs * strengths[slot_index] * is_live
    addition = (jnp.dot(weights, table, precision=lax.Precision.HIGHEST) * norm_scale).reshape(extent)
    current = lax.dynamic_slice(accumulated, starts, extent)
    return lax.dynamic_update_slice(accumulated, current + addition, starts)

def reference(orbitals, potential, kinetic_mu, projectors, strengths, box_offsets, block_counts):
    plane = ((HALO, HALO), (HALO, HALO), (0, 0))
    grad_mu = gradient(pad_depth(jnp.pad(kinetic_mu, plane)))

    def hamiltonian(field):
        padded = jnp.pad(field, plane)
        local = local_terms(padded, grad_mu, kinetic_mu, potential)
        stepper = partial(add_atom, padded=padded, projectors=projectors, strengths=strengths, box_offsets=box_offsets, block_counts=block_counts)
        accumulated = lax.fori_loop(0, SLOTS, stepper, jnp.zeros_like(padded))
        return local + accumulated[HALO:-HALO, HALO:-HALO, :]

    def filter_orbital(field):
        return chebyshev(field, hamiltonian)
    filtered = lax.map(filter_orbital, orbitals)
    flattened = filtered.reshape(NORB, -1)
    correlation = jnp.dot(flattened, flattened.T, precision=lax.Precision.HIGHEST) / (NX * NY * NZ)
    cholesky_factor = jnp.linalg.cholesky(correlation)
    inverse = jax.scipy.linalg.solve_triangular(cholesky_factor, jnp.eye(NORB, dtype=jnp.float32), lower=True)
    return jnp.dot(inverse, flattened, precision=lax.Precision.HIGHEST).reshape(filtered.shape)
```

```python
import functools

import jax
import jax.numpy as jnp
import ml_dtypes
import numpy as np
from jax import lax
from jax.experimental import pallas as pl
from jax.experimental.pallas import tpu as pltpu
from jax.sharding import PartitionSpec as P

CX, CY, NZ, ORB = 12, 16, 128, 4
HALO = 6
TILES = 96
XH = HALO * 8
YH = CX * 3
STEPS = 3

first_coefs = (6.0 / 7.0, -15.0 / 56.0, 5.0 / 63.0, -1.0 / 56.0, 2.0 / 825.0, -1.0 / 5544.0)
second_coefs = (12.0 / 7.0, -15.0 / 56.0, 10.0 / 189.0, -1.0 / 112.0, 2.0 / 1925.0, -1.0 / 16632.0)
center_coef = -5369.0 / 1800.0
filter_center = 13.5
filter_half = 10.5

F32, BF16 = jnp.float32, jnp.bfloat16
VMEM = pl.BlockSpec(memory_space=pltpu.VMEM)
SMEM = pl.BlockSpec(memory_space=pltpu.SMEM)
ANY = pl.BlockSpec(memory_space=pl.ANY)
LIMIT = 50 * 1024 * 1024


def derivative_table():
    table = np.zeros((NZ, 2 * NZ), np.float64)
    for z in range(NZ):
        table[z, NZ + z] = 3.0 * center_coef
        for k in range(1, HALO + 1):
            if z + k < NZ:
                table[z + k, z] = first_coefs[k - 1]
                table[z + k, NZ + z] = second_coefs[k - 1]
            if z - k >= 0:
                table[z - k, z] = -first_coefs[k - 1]
                table[z - k, NZ + z] = second_coefs[k - 1]
    high = table.astype(ml_dtypes.bfloat16)
    low = (table - high.astype(np.float64)).astype(ml_dtypes.bfloat16)
    return np.concatenate([high, low], axis=0)


def group_table():
    table = np.zeros((8 * 128, 128), np.float32)
    for p in range(8):
        for slot in range(16):
            for k in range(8):
                table[p * 128 + slot * 8 + k, slot * 8 + p] = 1.0
    return table.astype(ml_dtypes.bfloat16)


def split(a):
    high = a.astype(BF16)
    return high, (a - high.astype(F32)).astype(BF16)


def mm(a, b):
    return jnp.dot(a, b, preferred_element_type=F32)


def mm_t(a, b):
    return lax.dot_general(a, b, (((1,), (1,)), ((), ())), preferred_element_type=F32)


def pick(a, table):
    high, low = split(a)
    return mm(high, table) + mm(low, table)


def pick_t(a, table):
    high, low = split(a)
    return mm_t(high, table) + mm_t(low, table)


def get(ref, tile):
    return ref[pl.ds(tile * 8, 8), :]


def put(ref, tile, value):
    ref[pl.ds(tile * 8, 8), :] = value


def get_at(ref, tile):
    return ref[pl.ds(pl.multiple_of(tile * 8, 8), 8), :]


def iotas():
    return (
        lax.broadcasted_iota(jnp.int32, (8, 128), 0),
        lax.broadcasted_iota(jnp.int32, (8, 128), 1),
    )


def row(value, index):
    return jnp.broadcast_to(value[index : index + 1, :], (8, 128))


def pack_rims(y_ref, hi_ref, lo_ref, low):
    for x in range(CX):
        for m in range(3):
            put(hi_ref, x * 3 + m, jnp.where(low, pltpu.roll(get(y_ref, x * 8 + 2 + m), 4, 0), get(y_ref, x * 8 + 5 + m)))
            put(lo_ref, x * 3 + m, jnp.where(low, get(y_ref, x * 8 + m), pltpu.roll(get(y_ref, x * 8 + 3 + m), 4, 0)))


def prep_kernel(offs, strg, cnt, orb, mu, proj, y_ref, t_ref, meta_ref, xr_ref, xl_ref, yh_ref, yl_ref):
    sub, lane = iotas()
    low = sub < 4
    left_half = lane < 64
    for x in range(CX):
        for o in range(ORB):
            for h in range(2):
                y_ref[pl.ds(x * 64 + 4 * h + o, 8, stride=8), :] = orb[o, x, 8 * h : 8 * h + 8, :]
    group = lane // 8
    place = lane % 8
    meta = jnp.zeros((8, 128), F32)
    for s in range(8):
        for column in range(3):
            value = offs[s, column].astype(F32)
            meta = jnp.where((group == s) & (sub == column), value, meta)
        alive = jnp.where(s < cnt[0], 1.0, 0.0).astype(F32)
        for p in range(8):
            weight = strg[s, p] * alive * (1.0 / (512.0 * filter_half))
            meta = jnp.where((lane == s * 8 + p) & (sub == 3), weight, meta)
    del place
    meta_ref[...] = meta
    for i in range(8):
        for j in range(8):
            start = (i % 2) * 64 + j * 8
            total = jnp.zeros((8, 128), F32)
            for s in range(8):
                source = proj[s, :, 128 * (i // 2) : 128 * (i // 2) + 128]
                shift = (s * 8 - start) % 128
                moved = pltpu.roll(source, shift, 1) if shift else source
                total = jnp.where(group == s, moved, total)
            put(t_ref, i * 8 + j, total)
    for q in range(XH):
        put(xr_ref, q, get(y_ref, XH + q))
        put(xl_ref, q, get(y_ref, q))
    for x in range(HALO):
        for h in range(2):
            put(xr_ref, XH + 2 * x + h, mu[CX - HALO + x, 8 * h : 8 * h + 8, :])
            put(xl_ref, XH + 2 * x + h, mu[x, 8 * h : 8 * h + 8, :])
    base = XH + 2 * HALO
    for i in range(2):
        for j in range(8):
            for ref, first in ((xr_ref, 4), (xl_ref, 0)):
                one = get(t_ref, (first + i) * 8 + j)
                two = pltpu.roll(get(t_ref, (first + 2 + i) * 8 + j), 64, 1)
                put(ref, base + i * 8 + j, jnp.where(left_half, one, two))
    put(xr_ref, base + 16, meta)
    put(xl_ref, base + 16, meta)
    pack_rims(y_ref, yh_ref, yl_ref, low)
    for x in range(CX):
        put(yh_ref, YH + x, mu[x, 8:16, :])
        put(yl_ref, YH + x, mu[x, 0:8, :])


FIRST_X = XH + 2 * HALO + 17
FIRST_Y = YH + CX


def widen_kernel(t_ref, meta_ref, fl_ref, fr_ref, t2_ref, m_ref, hi_ref, lo_ref):
    _, lane = iotas()
    left_half = lane < 64
    base = XH + 2 * HALO
    for i in range(8):
        for j in range(8):
            if i >= 4:
                other = get(fl_ref, base + (i % 2) * 8 + j)
                other = other if i >= 6 else pltpu.roll(other, 64, 1)
            else:
                other = get(fr_ref, base + (i % 2) * 8 + j)
                other = other if i >= 2 else pltpu.roll(other, 64, 1)
            both = jnp.where(left_half, get(t_ref, i * 8 + j), other)
            put(t2_ref, i * 8 + j, both)
            if j >= 4:
                put(hi_ref, i * 4 + j - 4, both)
            else:
                put(lo_ref, i * 4 + j, both)
    meta = meta_ref[...]
    for side, ref in enumerate((fl_ref, fr_ref)):
        both = jnp.where(left_half, meta, pltpu.roll(get(ref, base + 16), 64, 1))
        put(m_ref, side, both)
        put(hi_ref, 32 + side, both)
        put(lo_ref, 32 + side, both)


def coef_kernel(mu, pot, fl_ref, fr_ref, flo_ref, fhi_ref, dz_ref, out_ref, ex, ey):
    sub, _ = iotas()
    low = sub < 4

    def two(a, ia, b, ib):
        return jnp.where(low, row(a, ia), row(b, ib))

    for x in range(CX + 2 * HALO):
        if x < HALO:
            a, b = get(fl_ref, XH + 2 * x), get(fl_ref, XH + 2 * x + 1)
        elif x < HALO + CX:
            a, b = mu[x - HALO, 0:8, :], mu[x - HALO, 8:16, :]
        else:
            a, b = get(fr_ref, XH + 2 * (x - HALO - CX)), get(fr_ref, XH + 2 * (x - HALO - CX) + 1)
        for yl in range(8):
            put(ex, x * 8 + yl, two(a, yl, b, yl))
    for x in range(CX):
        parts = [get(flo_ref, YH + x), mu[x, 0:8, :], mu[x, 8:16, :], get(fhi_ref, YH + x)]
        for n in range(20):
            y = n - HALO
            put(ey, x * 20 + n, two(parts[(y + 8) // 8], y % 8, parts[(y + 16) // 8], y % 8))
    field = ex[XH * 8 : (XH + TILES) * 8, :]
    high, rest = split(field)
    zd = mm(high, dz_ref[0:NZ, 0:NZ]) + mm(rest, dz_ref[0:NZ, 0:NZ]) + mm(high, dz_ref[NZ : 2 * NZ, 0:NZ])
    out_ref[3 * 768 : 4 * 768, :] = zd * (-0.5 / filter_half)

    def body(x, carry):
        va, vb = pot[x, 0:8, :], pot[x, 8:16, :]
        for yl in range(8):
            gx = jnp.zeros((8, 128), F32)
            gy = jnp.zeros((8, 128), F32)
            for k in range(1, HALO + 1):
                gx += first_coefs[k - 1] * (get_at(ex, (x + HALO + k) * 8 + yl) - get_at(ex, (x + HALO - k) * 8 + yl))
                gy += first_coefs[k - 1] * (
                    get_at(ey, x * 20 + HALO + yl + k) - get_at(ey, x * 20 + HALO + yl - k)
                )
            r = x * 8 + yl
            center = get_at(ex, (x + HALO) * 8 + yl)

            def store(which, value):
                out_ref[pl.ds(pl.multiple_of((which * TILES + r) * 8, 8), 8), :] = value

            store(0, (1.0 + center) * (-0.5 / filter_half))
            store(1, gx * (-0.5 / filter_half))
            store(2, gy * (-0.5 / filter_half))
            store(4, (two(va, yl, vb, yl) - filter_center) * (1.0 / filter_half))
        return carry

    lax.fori_loop(0, CX, body, 0)


def block_tiles(xt, yq):
    return [(4 * xt + a) * 8 + 4 * yq for a in range(4)]


def side_of(xt):
    return 1 if xt == 2 else 0


def partial_coeffs(y_ref, q_ref, s_ref, g_ref, z_ref, acc):
    left_half = lax.broadcasted_iota(jnp.int32, (8, 1024), 1) % 128 < 64
    own = None
    ends = {}
    rims = [None, None]
    corners = {}
    for xt in range(3):
        for yq in range(2):
            b = xt * 2 + yq
            field = jnp.concatenate([y_ref[t * 8 : t * 8 + 32, :] for t in block_tiles(xt, yq)], axis=0)
            table = s_ref[(side_of(xt) * 2 + yq) * 128 : (side_of(xt) * 2 + yq) * 128 + 128, :]
            seen = pick(field, table).reshape(16, 8, 256)
            sums = []
            for p in range(8):
                base = (b * 8 + p) * 128
                product = seen * q_ref[base : base + 128, :].reshape(16, 8, 256)
                total = jnp.sum(product, axis=0)
                sums.append(total + pltpu.roll(total, 4, 0))
            col_a = jnp.concatenate([t[:, :128] for t in sums], axis=1)
            col_b = jnp.concatenate([t[:, 128:] for t in sums], axis=1)
            own = col_a if own is None else own + col_a
            rims[yq] = col_b if rims[yq] is None else rims[yq] + col_b
            if xt != 1:
                ends[xt] = ends[xt] + col_a if xt in ends else col_a
                corners[(xt, yq)] = col_b
    for side, xt in enumerate((0, 2)):
        acc[side * 24 : side * 24 + 8, :] = jnp.where(left_half, own, ends[xt])
        for yq in range(2):
            at = side * 24 + 8 + yq * 8
            acc[at : at + 8, :] = jnp.where(left_half, rims[yq], corners[(xt, yq)])
    z_ref[...] = pick(acc[...], g_ref[...])


def send_coeffs(z_ref, xr_ref, xl_ref, base):
    for t in range(3):
        put(xr_ref, base + t, pltpu.roll(get(z_ref, 3 + t), 64, 1))
        put(xl_ref, base + t, pltpu.roll(get(z_ref, t), 64, 1))


def build_kernel(t2_ref, m_ref, lo_ref, hi_ref, y_ref, g_ref, q_ref, s_ref, w_ref, z_ref, xr_ref, xl_ref, tx, acc):
    sub, lane = iotas()
    low = sub < 4
    right_half = lane >= 64
    metas = [get(m_ref, 0), get(lo_ref, 32), get(hi_ref, 32), get(m_ref, 1), get(lo_ref, 33), get(hi_ref, 33)]
    for t in range(6):
        put(w_ref, t, row(metas[t], 3))
    zi = lax.broadcasted_iota(jnp.int32, (128, 128), 0)
    for side in range(2):
        for yq in range(2):
            for col, t in enumerate((side * 3, side * 3 + 1 + yq)):
                place = metas[t][2:3, :].astype(jnp.int32) + lane[0:1, :] % 8
                base = (side * 2 + yq) * 128
                hot = jnp.where(zi == jnp.broadcast_to(place, (128, 128)), 1.0, 0.0).astype(BF16)
                s_ref[base : base + 128, col * 128 : col * 128 + 128] = hot

    def table(col, i, j):
        if col == 0:
            return get(t2_ref, i * 8 + j)
        return get(lo_ref, i * 4 + j - 4) if j >= 4 else get(hi_ref, i * 4 + j)

    zero = jnp.zeros((8, 128), F32)
    for xt in range(3):
        shift = (-12.0, 1000.0, 12.0)[xt]
        for col in range(2):
            for yq in range(2):
                b = xt * 2 + yq
                t = side_of(xt) * 3 + (0 if col == 0 else 1 + yq)
                x0 = row(metas[t], 0) - 6.0 + jnp.where(right_half, shift, 0.0)
                y0 = row(metas[t], 1) - 6.0
                if col == 1:
                    y0 = y0 + (16.0 if yq == 1 else -16.0)
                js = range(8) if col == 0 else (range(0, 4) if yq == 1 else range(4, 8))
                if col == 1 or yq == 0:
                    for a in range(4):
                        for j in js:
                            moved = zero
                            for i in range(8):
                                moved = jnp.where(x0 == float(4 * xt + a - i), table(col, i, j), moved)
                            put(tx, a * 8 + j, moved)
                for a in range(4):
                    for c in range(4):
                        rows = []
                        for h in range(2):
                            y = 8 * h + 4 * yq + c
                            moved = zero
                            if col == 0 or h == yq:
                                for j in js:
                                    moved = jnp.where(y0 == float(y - j), get(tx, a * 8 + j), moved)
                            rows.append(moved)
                        for p in range(8):
                            base = ((b * 8 + p) * 16 + a * 4 + c) * 8
                            value = jnp.where(low, row(rows[0], p), row(rows[1], p))
                            q_ref[base : base + 8, col * 128 : col * 128 + 128] = value
    partial_coeffs(y_ref, q_ref, s_ref, g_ref, z_ref, acc)
    send_coeffs(z_ref, xr_ref, xl_ref, 0)


def fold_kernel(z_ref, fl_ref, fr_ref, out_ref, hi_ref, lo_ref):
    _, lane = iotas()
    left_half = lane < 64
    tiles = []
    for side in range(2):
        near, far = (fl_ref, fr_ref) if side == 0 else (fr_ref, fl_ref)
        for t in range(3):
            tiles.append(get(z_ref, side * 3 + t) + get(near, t) + jnp.where(left_half, get(far, t), 0.0))
    for t in range(6):
        put(out_ref, t, tiles[t])
    for side in range(2):
        put(hi_ref, side * 2, tiles[side * 3 + 2])
        put(hi_ref, side * 2 + 1, tiles[side * 3])
        put(lo_ref, side * 2, tiles[side * 3 + 1])
        put(lo_ref, side * 2 + 1, tiles[side * 3])


def step_kernel(
    step, y_ref, prev_ref, fl_ref, fr_ref, plo_ref, phi_ref, coef_ref, q_hbm, s_ref, w_ref, z_ref, clo_ref, chi_ref,
    dz_ref, g_ref, *rest
):
    last = step == STEPS
    if last:
        new_ref, q_ref, ex, ey, zd, acc, wp, sem = rest
    else:
        new_ref, xr_ref, xl_ref, yh_ref, yl_ref, zn_ref, q_ref, ex, ey, zd, acc, wp, sem = rest
    copy = pltpu.make_async_copy(q_hbm, q_ref, sem)
    copy.start()
    sub, _ = iotas()
    low = sub < 4
    scale = 1.0 if step == 1 else 2.0

    high, rest_part = split(y_ref[...])
    zd[...] = mm(high, dz_ref[0:NZ, :]) + mm(rest_part, dz_ref[0:NZ, :]) + mm(high, dz_ref[NZ : 2 * NZ, :])

    ex[0 : XH * 8, :] = fl_ref[0 : XH * 8, :]
    ex[XH * 8 : (XH + TILES) * 8, :] = y_ref[...]
    ex[(XH + TILES) * 8 : (2 * XH + TILES) * 8, :] = fr_ref[0 : XH * 8, :]
    for x in range(CX):
        for yl in range(8):
            put(ey, x * 20 + HALO + yl, get(y_ref, x * 8 + yl))
        for m in range(HALO):
            rim = get(plo_ref, x * 3 + m) if m < 3 else pltpu.roll(get(plo_ref, x * 3 + m - 3), 4, 0)
            put(ey, x * 20 + m, jnp.where(low, rim, pltpu.roll(get(y_ref, x * 8 + 2 + m), 4, 0)))
            rim = pltpu.roll(get(phi_ref, x * 3 + m), 4, 0) if m < 3 else get(phi_ref, x * 3 + m - 3)
            put(ey, x * 20 + HALO + 8 + m, jnp.where(low, pltpu.roll(get(y_ref, x * 8 + m), 4, 0), rim))

    def body(x, carry):
        for yl in range(8):
            r = x * 8 + yl
            center = get_at(y_ref, r)
            gx = gy = lap = None
            for k in range(1, HALO + 1):
                xp, xm = get_at(ex, (x + HALO + k) * 8 + yl), get_at(ex, (x + HALO - k) * 8 + yl)
                yp, ym = get_at(ey, x * 20 + HALO + yl + k), get_at(ey, x * 20 + HALO + yl - k)
                tx = first_coefs[k - 1] * (xp - xm)
                ty = first_coefs[k - 1] * (yp - ym)
                tl = second_coefs[k - 1] * ((xp + xm) + (yp + ym))
                gx, gy, lap = (tx, ty, tl) if k == 1 else (gx + tx, gy + ty, lap + tl)
            at = pl.ds(pl.multiple_of(r * 8, 8), 8)
            total = get_at(coef_ref, r) * (lap + zd[at, NZ:])
            total += get_at(coef_ref, TILES + r) * gx
            total += get_at(coef_ref, 2 * TILES + r) * gy
            total += get_at(coef_ref, 3 * TILES + r) * zd[at, :NZ]
            total += get_at(coef_ref, 4 * TILES + r) * center
            new_ref[at, :] = total if step == 1 else 2.0 * total - get_at(prev_ref, r)
        return carry

    lax.fori_loop(0, CX, body, 0)

    tiles = []
    for side in range(2):
        own, lo, hi = (get(z_ref, side * 3 + t) for t in range(3))
        tiles.append(own + get(clo_ref, side * 2) + get(chi_ref, side * 2))
        tiles.append(lo + get(clo_ref, side * 2 + 1))
        tiles.append(hi + get(chi_ref, side * 2 + 1))
    weights = jnp.concatenate(tiles, axis=0) * w_ref[...] * scale
    wp[...] = pick_t(weights, g_ref[...])

    copy.wait()
    for xt in range(3):
        for yq in range(2):
            b = xt * 2 + yq
            ta, tb = side_of(xt) * 3, side_of(xt) * 3 + 1 + yq
            total = None
            for p in range(8):
                weight = jnp.concatenate(
                    [wp[t * 8 : t * 8 + 8, p * 128 : p * 128 + 128] for t in (ta, tb)], axis=1
                )
                base = (b * 8 + p) * 128
                term = weight[None] * q_ref[base : base + 128, :].reshape(16, 8, 256)
                total = term if total is None else total + term
            table = s_ref[(side_of(xt) * 2 + yq) * 128 : (side_of(xt) * 2 + yq) * 128 + 128, :]
            spread = pick_t(total.reshape(128, 256), table)
            for a, t in enumerate(block_tiles(xt, yq)):
                new_ref[t * 8 : t * 8 + 32, :] += spread[a * 32 : a * 32 + 32, :]

    if not last:
        for q in range(XH):
            put(xr_ref, q, get(new_ref, XH + q))
            put(xl_ref, q, get(new_ref, q))
        pack_rims(new_ref, yh_ref, yl_ref, low)
        partial_coeffs(new_ref, q_ref, s_ref, g_ref, zn_ref, acc)
        send_coeffs(zn_ref, xr_ref, xl_ref, XH)


def gram_kernel(order, a0, a1, a2, a3, out_ref, held):
    for n, ref in enumerate((a0, a1, a2, a3)):
        held[order[n]] = ref[...]

    def body(x, total):
        at = pl.ds(pl.multiple_of(x * 64, 64), 64)
        field = jnp.concatenate([held[d, at, :] for d in range(4)], axis=0)
        high, low = split(field)
        return total + (mm_t(high, high) + mm_t(high, low) + mm_t(low, high))

    total = lax.fori_loop(0, CX, body, jnp.zeros((256, 256), F32))
    rows = lax.broadcasted_iota(jnp.int32, (256, 256), 0)
    columns = lax.broadcasted_iota(jnp.int32, (256, 256), 1)
    total = jnp.where((rows % 64) // 4 == (columns % 64) // 4, total, 0.0)
    orbital = lax.broadcasted_iota(jnp.int32, (16, 256), 0)
    held_at = lax.broadcasted_iota(jnp.int32, (16, 256), 1)
    hot = jnp.where(orbital == held_at // 64 * 4 + held_at % 4, 1.0, 0.0).astype(F32)
    first = jnp.dot(hot, total, precision=lax.Precision.HIGHEST, preferred_element_type=F32)
    small = lax.dot_general(
        first, hot, (((1,), (1,)), ((), ())), precision=lax.Precision.HIGHEST, preferred_element_type=F32
    )
    out_ref[...] = jnp.zeros((16, 128), F32)
    out_ref[:, 0:16] = small


def rotate_kernel(cells, order, corr_ref, a0, a1, a2, a3, out_ref, flat):
    lane = lax.broadcasted_iota(jnp.int32, (16, 128), 1)
    rows = lax.broadcasted_iota(jnp.int32, (16, 128), 0)
    work = jnp.where(lane < 16, corr_ref[...] * (1.0 / cells), jnp.where(lane == rows + 16, 1.0, 0.0))
    pivots = jnp.ones((16, 128), F32)
    for k in range(16):
        pivot_row = jnp.broadcast_to(work[k : k + 1, :], (16, 128))
        pivot = jnp.broadcast_to(pivot_row[:, k : k + 1], (16, 128))
        column = jnp.broadcast_to(work[:, k : k + 1], (16, 128))
        pivots = jnp.where(rows == k, pivot, pivots)
        work = jnp.where(rows > k, work - column / pivot * pivot_row, work)
    inverse = (work / jnp.sqrt(pivots))[:, 16:32]
    me = order[0]
    own_row = lax.broadcasted_iota(jnp.int32, (64, 16), 0)
    orbital = lax.broadcasted_iota(jnp.int32, (64, 16), 1)
    left = jnp.where(orbital == me * 4 + own_row % 4, 1.0, 0.0).astype(F32)
    orbital = lax.broadcasted_iota(jnp.int32, (16, 256), 0)
    held_at = lax.broadcasted_iota(jnp.int32, (16, 256), 1)
    device = held_at // 64
    owner = jnp.where(device == 0, order[0], jnp.where(device == 1, order[1], jnp.where(device == 2, order[2], order[3])))
    right = jnp.where(orbital == owner * 4 + held_at % 4, 1.0, 0.0).astype(F32)
    exact = functools.partial(jnp.dot, precision=lax.Precision.HIGHEST, preferred_element_type=F32)
    mixing = exact(exact(left, inverse), right)
    at_row = lax.broadcasted_iota(jnp.int32, (64, 256), 0)
    at_column = lax.broadcasted_iota(jnp.int32, (64, 256), 1)
    mixing = jnp.where(at_row // 4 == at_column % 64 // 4, mixing, 0.0)
    mix_high, mix_low = split(mixing)
    for x in range(CX):
        field = jnp.concatenate([ref[x * 64 : x * 64 + 64, :] for ref in (a0, a1, a2, a3)], axis=0)
        high, low = split(field)
        flat[x * 64 : x * 64 + 64, :] = mm(mix_high, high) + mm(mix_high, low) + mm(mix_low, high)
    for o in range(ORB):
        for x in range(CX):
            for h in range(2):
                out_ref[o, x, 8 * h : 8 * h + 8, :] = flat[pl.ds(x * 64 + 4 * h + o, 8, stride=8), :]


def kernel_call(body, outs, ins, scratch=(), name=None):
    return pl.pallas_call(
        body,
        out_shape=[jax.ShapeDtypeStruct(shape, dtype) for shape, dtype in outs],
        in_specs=ins,
        out_specs=[VMEM] * len(outs),
        scratch_shapes=list(scratch),
        compiler_params=pltpu.CompilerParams(vmem_limit_bytes=LIMIT),
        name=name,
    )


def blocks(count, columns=128, dtype=F32):
    return (count * 8, columns), dtype


def beside(low_value, high_value, axis):
    count = lax.axis_size(axis)
    up = [(i, i + 1) for i in range(count - 1)]
    down = [(i + 1, i) for i in range(count - 1)]
    return lax.ppermute(low_value, axis, up), lax.ppermute(high_value, axis, down)


def fold(z, from_left, from_right, tile):
    block = pl.BlockSpec((24, 128), lambda i: (tile // 3, 0))
    whole = lambda rows: pl.BlockSpec((rows, 128), lambda i: (0, 0))
    return pl.pallas_call(
        fold_kernel,
        grid=(1,),
        out_shape=[jax.ShapeDtypeStruct((rows, 128), F32) for rows in (48, 32, 32)],
        in_specs=[whole(48), block, block],
        out_specs=[whole(48), whole(32), whole(32)],
        name="fold_coeffs",
    )(z, from_left, from_right)


def shards(orbitals, potential, kinetic_mu, projectors, strengths, box_offsets, block_counts):
    dz = jnp.asarray(derivative_table())
    groups = jnp.asarray(group_table())
    y, t, meta, xr, xl, yh, yl = kernel_call(
        prep_kernel,
        [blocks(TILES), blocks(64), blocks(1), blocks(FIRST_X), blocks(FIRST_X), blocks(FIRST_Y), blocks(FIRST_Y)],
        [SMEM, SMEM, SMEM, VMEM, VMEM, VMEM],
        name="prepare",
    )(box_offsets, strengths, block_counts, orbitals, kinetic_mu, projectors)
    from_left, from_right = beside(xr, xl, "gx")
    from_lo, from_hi = beside(yh, yl, "gy")
    t2, metas, hi2, lo2 = kernel_call(
        widen_kernel, [blocks(64), blocks(2), blocks(34), blocks(34)], [VMEM] * 4, name="widen"
    )(t, meta, from_left, from_right)
    from_lo2, from_hi2 = beside(hi2, lo2, "gy")
    (coefs,) = kernel_call(
        coef_kernel,
        [blocks(5 * TILES)],
        [VMEM] * 7,
        [pltpu.VMEM(((TILES + 2 * XH) * 8, 128), F32), pltpu.VMEM((CX * 20 * 8, 128), F32)],
        name="coefficients",
    )(kinetic_mu, potential, from_left, from_right, from_lo, from_hi, dz)
    q, s, w, z, zr, zl = kernel_call(
        build_kernel,
        [
            blocks(6 * 8 * 16, 256),
            ((4 * 128, 256), BF16),
            blocks(6),
            blocks(6),
            blocks(3),
            blocks(3),
        ],
        [VMEM] * 6,
        [pltpu.VMEM((32 * 8, 128), F32), pltpu.VMEM((48, 1024), F32)],
        name="build",
    )(t2, metas, from_lo2, from_hi2, y, groups)
    z_left, z_right = beside(zr, zl, "gx")
    z, z_hi, z_lo = fold(z, z_left, z_right, 0)
    c_lo, c_hi = beside(z_hi, z_lo, "gy")

    previous = y
    for step in range(1, STEPS + 1):
        last = step == STEPS
        outs = [blocks(TILES)]
        if not last:
            outs += [blocks(XH + 3), blocks(XH + 3), blocks(YH), blocks(YH), blocks(6)]
        result = kernel_call(
            functools.partial(step_kernel, step),
            outs,
            [VMEM] * 7 + [ANY] + [VMEM] * 7,
            [
                pltpu.VMEM((6 * 8 * 16 * 8, 256), F32),
                pltpu.VMEM(((TILES + 2 * XH) * 8, 128), F32),
                pltpu.VMEM((CX * 20 * 8, 128), F32),
                pltpu.VMEM((TILES * 8, 256), F32),
                pltpu.VMEM((48, 1024), F32),
                pltpu.VMEM((48, 1024), F32),
                pltpu.SemaphoreType.DMA,
            ],
            name="step",
        )(y, previous, from_left, from_right, from_lo, from_hi, coefs, q, s, w, z, c_lo, c_hi, dz, groups)
        previous = y
        if last:
            (y,) = result
        else:
            y, xr, xl, yh, yl, z = result
            from_left, from_right = beside(xr, xl, "gx")
            from_lo, from_hi = beside(yh, yl, "gy")
            z, z_hi, z_lo = fold(z, from_left, from_right, XH)
            c_lo, c_hi = beside(z_hi, z_lo, "gy")

    count = lax.axis_size("orb")
    me = lax.axis_index("orb")
    up = [(i, (i + 1) % count) for i in range(count)]
    down = [(i, (i - 1) % count) for i in range(count)]
    below = lax.ppermute(y, "orb", up)
    above = lax.ppermute(y, "orb", down)
    half = TILES * 4
    across_a = lax.ppermute(below[:half], "orb", up)
    across_b = lax.ppermute(above[half:], "orb", down)
    across = jnp.concatenate([across_a, across_b], axis=0)
    order = jnp.stack([me, (me + count - 1) % count, (me + 1) % count, (me + 2) % count]).astype(jnp.int32)
    (corr,) = kernel_call(
        gram_kernel,
        [((16, 128), F32)],
        [SMEM] + [VMEM] * 4,
        [pltpu.VMEM((4, TILES * 8, 128), F32)],
        name="gram",
    )(order, y, below, above, across)
    for axis in ("gx", "gy"):
        size = lax.axis_size(axis)
        stride = 1
        while stride < size:
            corr = corr + lax.ppermute(corr, axis, [(i, i ^ stride) for i in range(size)])
            stride *= 2
    cells = CX * CY * NZ * lax.axis_size("gx") * lax.axis_size("gy")
    (result,) = kernel_call(
        functools.partial(rotate_kernel, cells),
        [((ORB, CX, CY, NZ), F32)],
        [SMEM] + [VMEM] * 5,
        [pltpu.VMEM((TILES * 8, 128), F32)],
        name="rotate",
    )(order, corr, y, below, above, across)
    return result


def solution(mesh):
    in_specs = (
        P("orb", "gx", "gy", None),
        P("gx", "gy", None),
        P("gx", "gy", None),
        P(("gx", "gy"), None, None),
        P(("gx", "gy"), None),
        P(("gx", "gy"), None),
        P(("gx", "gy")),
    )
    out_specs = P("orb", "gx", "gy", None)
    return jax.shard_map(shards, mesh=mesh, in_specs=in_specs, out_specs=out_specs, check_vma=False)
```

```python
import functools

import jax
import jax.numpy as jnp
import ml_dtypes
import numpy as np
from jax import lax
from jax.experimental import pallas as pl
from jax.experimental.pallas import tpu as pltpu
from jax.sharding import PartitionSpec as P

CX, CY, NZ, ORB = 12, 16, 128, 4
HALO = 6
TILES = 96
XH = HALO * 8
YH = CX * 3
STEPS = 3

first_coefs = (6.0 / 7.0, -15.0 / 56.0, 5.0 / 63.0, -1.0 / 56.0, 2.0 / 825.0, -1.0 / 5544.0)
second_coefs = (12.0 / 7.0, -15.0 / 56.0, 10.0 / 189.0, -1.0 / 112.0, 2.0 / 1925.0, -1.0 / 16632.0)
center_coef = -5369.0 / 1800.0
filter_center = 13.5
filter_half = 10.5

F32, BF16 = jnp.float32, jnp.bfloat16
VMEM = pl.BlockSpec(memory_space=pltpu.VMEM)
SMEM = pl.BlockSpec(memory_space=pltpu.SMEM)
LIMIT = 24 * 1024 * 1024


def derivative_table():
    table = np.zeros((NZ, 2 * NZ), np.float64)
    for z in range(NZ):
        table[z, NZ + z] = 3.0 * center_coef
        for k in range(1, HALO + 1):
            if z + k < NZ:
                table[z + k, z] = first_coefs[k - 1]
                table[z + k, NZ + z] = second_coefs[k - 1]
            if z - k >= 0:
                table[z - k, z] = -first_coefs[k - 1]
                table[z - k, NZ + z] = second_coefs[k - 1]
    high = table.astype(ml_dtypes.bfloat16)
    low = (table - high.astype(np.float64)).astype(ml_dtypes.bfloat16)
    return np.concatenate([high, low], axis=0)


def group_table():
    table = np.zeros((8 * 128, 128), np.float32)
    for p in range(8):
        for slot in range(16):
            for k in range(8):
                table[p * 128 + slot * 8 + k, slot * 8 + p] = 1.0
    return table.astype(ml_dtypes.bfloat16)


def split(a):
    high = a.astype(BF16)
    return high, (a - high.astype(F32)).astype(BF16)


def mm(a, b):
    return jnp.dot(a, b, preferred_element_type=F32)


def mm_t(a, b):
    return lax.dot_general(a, b, (((1,), (1,)), ((), ())), preferred_element_type=F32)


def pick(a, table):
    high, low = split(a)
    return mm(high, table) + mm(low, table)


def pick_t(a, table):
    high, low = split(a)
    return mm_t(high, table) + mm_t(low, table)


def get(ref, tile):
    return ref[pl.ds(tile * 8, 8), :]


def put(ref, tile, value):
    ref[pl.ds(tile * 8, 8), :] = value


def get_at(ref, tile):
    return ref[pl.ds(pl.multiple_of(tile * 8, 8), 8), :]


def iotas():
    return (
        lax.broadcasted_iota(jnp.int32, (8, 128), 0),
        lax.broadcasted_iota(jnp.int32, (8, 128), 1),
    )


def row(value, index):
    return jnp.broadcast_to(value[index : index + 1, :], (8, 128))


def pack_rims(y_ref, hi_ref, lo_ref, low):
    for x in range(CX):
        for m in range(3):
            put(hi_ref, x * 3 + m, jnp.where(low, pltpu.roll(get(y_ref, x * 8 + 2 + m), 4, 0), get(y_ref, x * 8 + 5 + m)))
            put(lo_ref, x * 3 + m, jnp.where(low, get(y_ref, x * 8 + m), pltpu.roll(get(y_ref, x * 8 + 3 + m), 4, 0)))


def prep_kernel(offs, strg, cnt, orb, mu, proj, y_ref, t_ref, meta_ref, xr_ref, xl_ref, yh_ref, yl_ref):
    sub, lane = iotas()
    low = sub < 4
    left_half = lane < 64
    for x in range(CX):
        for o in range(ORB):
            for h in range(2):
                y_ref[pl.ds(x * 64 + 4 * h + o, 8, stride=8), :] = orb[o, x, 8 * h : 8 * h + 8, :]
    group = lane // 8
    place = lane % 8
    meta = jnp.zeros((8, 128), F32)
    for s in range(8):
        for column in range(3):
            value = offs[s, column].astype(F32)
            meta = jnp.where((group == s) & (sub == column), value, meta)
        alive = jnp.where(s < cnt[0], 1.0, 0.0).astype(F32)
        for p in range(8):
            weight = strg[s, p] * alive * (1.0 / (512.0 * filter_half))
            meta = jnp.where((lane == s * 8 + p) & (sub == 3), weight, meta)
    del place
    meta_ref[...] = meta
    for i in range(8):
        for j in range(8):
            start = (i % 2) * 64 + j * 8
            total = jnp.zeros((8, 128), F32)
            for s in range(8):
                source = proj[s, :, 128 * (i // 2) : 128 * (i // 2) + 128]
                shift = (s * 8 - start) % 128
                moved = pltpu.roll(source, shift, 1) if shift else source
                total = jnp.where(group == s, moved, total)
            put(t_ref, i * 8 + j, total)
    for q in range(XH):
        put(xr_ref, q, get(y_ref, XH + q))
        put(xl_ref, q, get(y_ref, q))
    for x in range(HALO):
        for h in range(2):
            put(xr_ref, XH + 2 * x + h, mu[CX - HALO + x, 8 * h : 8 * h + 8, :])
            put(xl_ref, XH + 2 * x + h, mu[x, 8 * h : 8 * h + 8, :])
    base = XH + 2 * HALO
    for i in range(2):
        for j in range(8):
            for ref, first in ((xr_ref, 4), (xl_ref, 0)):
                one = get(t_ref, (first + i) * 8 + j)
                two = pltpu.roll(get(t_ref, (first + 2 + i) * 8 + j), 64, 1)
                put(ref, base + i * 8 + j, jnp.where(left_half, one, two))
    put(xr_ref, base + 16, meta)
    put(xl_ref, base + 16, meta)
    pack_rims(y_ref, yh_ref, yl_ref, low)
    for x in range(CX):
        put(yh_ref, YH + x, mu[x, 8:16, :])
        put(yl_ref, YH + x, mu[x, 0:8, :])


FIRST_X = XH + 2 * HALO + 17
FIRST_Y = YH + CX


def widen_kernel(t_ref, meta_ref, fl_ref, fr_ref, t2_ref, m_ref, hi_ref, lo_ref):
    _, lane = iotas()
    left_half = lane < 64
    base = XH + 2 * HALO
    for i in range(8):
        for j in range(8):
            if i >= 4:
                other = get(fl_ref, base + (i % 2) * 8 + j)
                other = other if i >= 6 else pltpu.roll(other, 64, 1)
            else:
                other = get(fr_ref, base + (i % 2) * 8 + j)
                other = other if i >= 2 else pltpu.roll(other, 64, 1)
            both = jnp.where(left_half, get(t_ref, i * 8 + j), other)
            put(t2_ref, i * 8 + j, both)
            if j >= 4:
                put(hi_ref, i * 4 + j - 4, both)
            else:
                put(lo_ref, i * 4 + j, both)
    meta = meta_ref[...]
    for side, ref in enumerate((fl_ref, fr_ref)):
        both = jnp.where(left_half, meta, pltpu.roll(get(ref, base + 16), 64, 1))
        put(m_ref, side, both)
        put(hi_ref, 32 + side, both)
        put(lo_ref, 32 + side, both)


def coef_kernel(mu, pot, fl_ref, fr_ref, flo_ref, fhi_ref, dz_ref, out_ref, ex, ey):
    sub, _ = iotas()
    low = sub < 4

    def two(a, ia, b, ib):
        return jnp.where(low, row(a, ia), row(b, ib))

    for x in range(CX + 2 * HALO):
        if x < HALO:
            a, b = get(fl_ref, XH + 2 * x), get(fl_ref, XH + 2 * x + 1)
        elif x < HALO + CX:
            a, b = mu[x - HALO, 0:8, :], mu[x - HALO, 8:16, :]
        else:
            a, b = get(fr_ref, XH + 2 * (x - HALO - CX)), get(fr_ref, XH + 2 * (x - HALO - CX) + 1)
        for yl in range(8):
            put(ex, x * 8 + yl, two(a, yl, b, yl))
    for x in range(CX):
        parts = [get(flo_ref, YH + x), mu[x, 0:8, :], mu[x, 8:16, :], get(fhi_ref, YH + x)]
        for n in range(20):
            y = n - HALO
            put(ey, x * 20 + n, two(parts[(y + 8) // 8], y % 8, parts[(y + 16) // 8], y % 8))
    field = ex[XH * 8 : (XH + TILES) * 8, :]
    high, rest = split(field)
    zd = mm(high, dz_ref[0:NZ, 0:NZ]) + mm(rest, dz_ref[0:NZ, 0:NZ]) + mm(high, dz_ref[NZ : 2 * NZ, 0:NZ])
    out_ref[3 * 768 : 4 * 768, :] = zd * (-0.5 / filter_half)

    def body(x, carry):
        va, vb = pot[x, 0:8, :], pot[x, 8:16, :]
        for yl in range(8):
            gx = jnp.zeros((8, 128), F32)
            gy = jnp.zeros((8, 128), F32)
            for k in range(1, HALO + 1):
                gx += first_coefs[k - 1] * (get_at(ex, (x + HALO + k) * 8 + yl) - get_at(ex, (x + HALO - k) * 8 + yl))
                gy += first_coefs[k - 1] * (
                    get_at(ey, x * 20 + HALO + yl + k) - get_at(ey, x * 20 + HALO + yl - k)
                )
            r = x * 8 + yl
            center = get_at(ex, (x + HALO) * 8 + yl)

            def store(which, value):
                out_ref[pl.ds(pl.multiple_of((which * TILES + r) * 8, 8), 8), :] = value

            store(0, (1.0 + center) * (-0.5 / filter_half))
            store(1, gx * (-0.5 / filter_half))
            store(2, gy * (-0.5 / filter_half))
            store(4, (two(va, yl, vb, yl) - filter_center) * (1.0 / filter_half))
        return carry

    lax.fori_loop(0, CX, body, 0)


def block_tiles(xt, yq):
    return [(4 * xt + a) * 8 + 4 * yq for a in range(4)]


def side_of(xt):
    return 1 if xt == 2 else 0


def partial_coeffs(y_ref, q_ref, s_ref, g_ref, z_ref, acc):
    left_half = lax.broadcasted_iota(jnp.int32, (8, 1024), 1) % 128 < 64
    own = None
    ends = {}
    rims = [None, None]
    corners = {}
    for xt in range(3):
        for yq in range(2):
            b = xt * 2 + yq
            field = jnp.concatenate([y_ref[t * 8 : t * 8 + 32, :] for t in block_tiles(xt, yq)], axis=0)
            table = s_ref[(side_of(xt) * 2 + yq) * 128 : (side_of(xt) * 2 + yq) * 128 + 128, :]
            seen = pick(field, table).reshape(16, 8, 256)
            sums = []
            for p in range(8):
                base = (b * 8 + p) * 128
                product = seen * q_ref[base : base + 128, :].reshape(16, 8, 256)
                total = jnp.sum(product, axis=0)
                sums.append(total + pltpu.roll(total, 4, 0))
            col_a = jnp.concatenate([t[:, :128] for t in sums], axis=1)
            col_b = jnp.concatenate([t[:, 128:] for t in sums], axis=1)
            own = col_a if own is None else own + col_a
            rims[yq] = col_b if rims[yq] is None else rims[yq] + col_b
            if xt != 1:
                ends[xt] = ends[xt] + col_a if xt in ends else col_a
                corners[(xt, yq)] = col_b
    for side, xt in enumerate((0, 2)):
        acc[side * 24 : side * 24 + 8, :] = jnp.where(left_half, own, ends[xt])
        for yq in range(2):
            at = side * 24 + 8 + yq * 8
            acc[at : at + 8, :] = jnp.where(left_half, rims[yq], corners[(xt, yq)])
    z_ref[...] = pick(acc[...], g_ref[...])


def send_coeffs(z_ref, xr_ref, xl_ref, base):
    for t in range(3):
        put(xr_ref, base + t, pltpu.roll(get(z_ref, 3 + t), 64, 1))
        put(xl_ref, base + t, pltpu.roll(get(z_ref, t), 64, 1))


def build_kernel(t2_ref, m_ref, lo_ref, hi_ref, y_ref, g_ref, q_ref, s_ref, w_ref, z_ref, xr_ref, xl_ref, tx, acc):
    sub, lane = iotas()
    low = sub < 4
    right_half = lane >= 64
    metas = [get(m_ref, 0), get(lo_ref, 32), get(hi_ref, 32), get(m_ref, 1), get(lo_ref, 33), get(hi_ref, 33)]
    for t in range(6):
        put(w_ref, t, row(metas[t], 3))
    zi = lax.broadcasted_iota(jnp.int32, (128, 128), 0)
    for side in range(2):
        for yq in range(2):
            for col, t in enumerate((side * 3, side * 3 + 1 + yq)):
                place = metas[t][2:3, :].astype(jnp.int32) + lane[0:1, :] % 8
                base = (side * 2 + yq) * 128
                hot = jnp.where(zi == jnp.broadcast_to(place, (128, 128)), 1.0, 0.0).astype(BF16)
                s_ref[base : base + 128, col * 128 : col * 128 + 128] = hot

    def table(col, i, j):
        if col == 0:
            return get(t2_ref, i * 8 + j)
        return get(lo_ref, i * 4 + j - 4) if j >= 4 else get(hi_ref, i * 4 + j)

    zero = jnp.zeros((8, 128), F32)
    for xt in range(3):
        shift = (-12.0, 1000.0, 12.0)[xt]
        for col in range(2):
            for yq in range(2):
                b = xt * 2 + yq
                t = side_of(xt) * 3 + (0 if col == 0 else 1 + yq)
                x0 = row(metas[t], 0) - 6.0 + jnp.where(right_half, shift, 0.0)
                y0 = row(metas[t], 1) - 6.0
                if col == 1:
                    y0 = y0 + (16.0 if yq == 1 else -16.0)
                js = range(8) if col == 0 else (range(0, 4) if yq == 1 else range(4, 8))
                if col == 1 or yq == 0:
                    for a in range(4):
                        for j in js:
                            moved = zero
                            for i in range(8):
                                moved = jnp.where(x0 == float(4 * xt + a - i), table(col, i, j), moved)
                            put(tx, a * 8 + j, moved)
                for a in range(4):
                    for c in range(4):
                        rows = []
                        for h in range(2):
                            y = 8 * h + 4 * yq + c
                            moved = zero
                            if col == 0 or h == yq:
                                for j in js:
                                    moved = jnp.where(y0 == float(y - j), get(tx, a * 8 + j), moved)
                            rows.append(moved)
                        for p in range(8):
                            base = ((b * 8 + p) * 16 + a * 4 + c) * 8
                            value = jnp.where(low, row(rows[0], p), row(rows[1], p))
                            q_ref[base : base + 8, col * 128 : col * 128 + 128] = value
    partial_coeffs(y_ref, q_ref, s_ref, g_ref, z_ref, acc)
    send_coeffs(z_ref, xr_ref, xl_ref, 0)


def fold_kernel(base, z_ref, fl_ref, fr_ref, out_ref, hi_ref, lo_ref):
    _, lane = iotas()
    left_half = lane < 64
    tiles = []
    for side in range(2):
        near, far = (fl_ref, fr_ref) if side == 0 else (fr_ref, fl_ref)
        for t in range(3):
            tiles.append(get(z_ref, side * 3 + t) + get(near, base + t) + jnp.where(left_half, get(far, base + t), 0.0))
    for t in range(6):
        put(out_ref, t, tiles[t])
    for side in range(2):
        put(hi_ref, side * 2, tiles[side * 3 + 2])
        put(hi_ref, side * 2 + 1, tiles[side * 3])
        put(lo_ref, side * 2, tiles[side * 3 + 1])
        put(lo_ref, side * 2 + 1, tiles[side * 3])


def step_kernel(
    step, y_ref, prev_ref, fl_ref, fr_ref, plo_ref, phi_ref, coef_ref, q_ref, s_ref, w_ref, z_ref, clo_ref, chi_ref,
    dz_ref, g_ref, *rest
):
    last = step == STEPS
    if last:
        new_ref, ex, ey, zd, acc, wp = rest
    else:
        new_ref, xr_ref, xl_ref, yh_ref, yl_ref, zn_ref, ex, ey, zd, acc, wp = rest
    sub, _ = iotas()
    low = sub < 4
    scale = 1.0 if step == 1 else 2.0

    high, rest_part = split(y_ref[...])
    zd[...] = mm(high, dz_ref[0:NZ, :]) + mm(rest_part, dz_ref[0:NZ, :]) + mm(high, dz_ref[NZ : 2 * NZ, :])

    ex[0 : XH * 8, :] = fl_ref[0 : XH * 8, :]
    ex[XH * 8 : (XH + TILES) * 8, :] = y_ref[...]
    ex[(XH + TILES) * 8 : (2 * XH + TILES) * 8, :] = fr_ref[0 : XH * 8, :]
    for x in range(CX):
        for yl in range(8):
            put(ey, x * 20 + HALO + yl, get(y_ref, x * 8 + yl))
        for m in range(HALO):
            rim = get(plo_ref, x * 3 + m) if m < 3 else pltpu.roll(get(plo_ref, x * 3 + m - 3), 4, 0)
            put(ey, x * 20 + m, jnp.where(low, rim, pltpu.roll(get(y_ref, x * 8 + 2 + m), 4, 0)))
            rim = pltpu.roll(get(phi_ref, x * 3 + m), 4, 0) if m < 3 else get(phi_ref, x * 3 + m - 3)
            put(ey, x * 20 + HALO + 8 + m, jnp.where(low, pltpu.roll(get(y_ref, x * 8 + m), 4, 0), rim))

    def body(x, carry):
        for yl in range(8):
            r = x * 8 + yl
            center = get_at(y_ref, r)
            gx = gy = lap = None
            for k in range(1, HALO + 1):
                xp, xm = get_at(ex, (x + HALO + k) * 8 + yl), get_at(ex, (x + HALO - k) * 8 + yl)
                yp, ym = get_at(ey, x * 20 + HALO + yl + k), get_at(ey, x * 20 + HALO + yl - k)
                tx = first_coefs[k - 1] * (xp - xm)
                ty = first_coefs[k - 1] * (yp - ym)
                tl = second_coefs[k - 1] * ((xp + xm) + (yp + ym))
                gx, gy, lap = (tx, ty, tl) if k == 1 else (gx + tx, gy + ty, lap + tl)
            at = pl.ds(pl.multiple_of(r * 8, 8), 8)
            total = get_at(coef_ref, r) * (lap + zd[at, NZ:])
            total += get_at(coef_ref, TILES + r) * gx
            total += get_at(coef_ref, 2 * TILES + r) * gy
            total += get_at(coef_ref, 3 * TILES + r) * zd[at, :NZ]
            total += get_at(coef_ref, 4 * TILES + r) * center
            new_ref[at, :] = total if step == 1 else 2.0 * total - get_at(prev_ref, r)
        return carry

    lax.fori_loop(0, CX, body, 0)

    tiles = []
    for side in range(2):
        own, lo, hi = (get(z_ref, side * 3 + t) for t in range(3))
        tiles.append(own + get(clo_ref, side * 2) + get(chi_ref, side * 2))
        tiles.append(lo + get(clo_ref, side * 2 + 1))
        tiles.append(hi + get(chi_ref, side * 2 + 1))
    weights = jnp.concatenate(tiles, axis=0) * w_ref[...] * scale
    wp[...] = pick_t(weights, g_ref[...])

    for xt in range(3):
        for yq in range(2):
            b = xt * 2 + yq
            ta, tb = side_of(xt) * 3, side_of(xt) * 3 + 1 + yq
            total = None
            for p in range(8):
                weight = jnp.concatenate(
                    [wp[t * 8 : t * 8 + 8, p * 128 : p * 128 + 128] for t in (ta, tb)], axis=1
                )
                base = (b * 8 + p) * 128
                term = weight[None] * q_ref[base : base + 128, :].reshape(16, 8, 256)
                total = term if total is None else total + term
            table = s_ref[(side_of(xt) * 2 + yq) * 128 : (side_of(xt) * 2 + yq) * 128 + 128, :]
            spread = pick_t(total.reshape(128, 256), table)
            for a, t in enumerate(block_tiles(xt, yq)):
                new_ref[t * 8 : t * 8 + 32, :] += spread[a * 32 : a * 32 + 32, :]

    if not last:
        for q in range(XH):
            put(xr_ref, q, get(new_ref, XH + q))
            put(xl_ref, q, get(new_ref, q))
        pack_rims(new_ref, yh_ref, yl_ref, low)
        partial_coeffs(new_ref, q_ref, s_ref, g_ref, zn_ref, acc)
        send_coeffs(zn_ref, xr_ref, xl_ref, XH)


def gram_kernel(parts_ref, out_ref):
    total = jnp.zeros((256, 256), F32)
    for x in range(CX // 4):
        field = jnp.concatenate([parts_ref[d, x * 64 : x * 64 + 64, :] for d in range(4)], axis=0)
        high, low = split(field)
        total = total + (mm_t(high, high) + mm_t(high, low) + mm_t(low, high))
    rows = lax.broadcasted_iota(jnp.int32, (256, 256), 0)
    columns = lax.broadcasted_iota(jnp.int32, (256, 256), 1)
    total = jnp.where((rows % 64) // 4 == (columns % 64) // 4, total, 0.0)
    orbital = lax.broadcasted_iota(jnp.int32, (16, 256), 0)
    held_at = lax.broadcasted_iota(jnp.int32, (16, 256), 1)
    hot = jnp.where(orbital == held_at // 64 * 4 + held_at % 4, 1.0, 0.0).astype(F32)
    first = jnp.dot(hot, total, precision=lax.Precision.HIGHEST, preferred_element_type=F32)
    small = lax.dot_general(
        first, hot, (((1,), (1,)), ((), ())), precision=lax.Precision.HIGHEST, preferred_element_type=F32
    )
    out_ref[...] = jnp.zeros((8, 128), F32)
    out_ref[:, 0:16] = small[0:8]
    out_ref[:, 16:32] = small[8:16]


def rotate_kernel(cells, order, corr_ref, a0, a1, a2, a3, out_ref, flat):
    lane = lax.broadcasted_iota(jnp.int32, (16, 128), 1)
    rows = lax.broadcasted_iota(jnp.int32, (16, 128), 0)
    packed = corr_ref[...]
    whole = jnp.concatenate([packed, pltpu.roll(packed, 112, 1)], axis=0)
    work = jnp.where(lane < 16, whole * (1.0 / cells), jnp.where(lane == rows + 16, 1.0, 0.0))
    pivots = jnp.ones((16, 128), F32)
    for k in range(16):
        pivot_row = jnp.broadcast_to(work[k : k + 1, :], (16, 128))
        pivot = jnp.broadcast_to(pivot_row[:, k : k + 1], (16, 128))
        column = jnp.broadcast_to(work[:, k : k + 1], (16, 128))
        pivots = jnp.where(rows == k, pivot, pivots)
        work = jnp.where(rows > k, work - column / pivot * pivot_row, work)
    inverse = (work / jnp.sqrt(pivots))[:, 16:32]
    me = order[0]
    own_row = lax.broadcasted_iota(jnp.int32, (64, 16), 0)
    orbital = lax.broadcasted_iota(jnp.int32, (64, 16), 1)
    left = jnp.where(orbital == me * 4 + own_row % 4, 1.0, 0.0).astype(F32)
    orbital = lax.broadcasted_iota(jnp.int32, (16, 256), 0)
    held_at = lax.broadcasted_iota(jnp.int32, (16, 256), 1)
    device = held_at // 64
    owner = jnp.where(device == 0, order[0], jnp.where(device == 1, order[1], jnp.where(device == 2, order[2], order[3])))
    right = jnp.where(orbital == owner * 4 + held_at % 4, 1.0, 0.0).astype(F32)
    exact = functools.partial(jnp.dot, precision=lax.Precision.HIGHEST, preferred_element_type=F32)
    mixing = exact(exact(left, inverse), right)
    at_row = lax.broadcasted_iota(jnp.int32, (64, 256), 0)
    at_column = lax.broadcasted_iota(jnp.int32, (64, 256), 1)
    mixing = jnp.where(at_row // 4 == at_column % 64 // 4, mixing, 0.0)
    mix_high, mix_low = split(mixing)
    for x in range(CX):
        field = jnp.concatenate([ref[x * 64 : x * 64 + 64, :] for ref in (a0, a1, a2, a3)], axis=0)
        high, low = split(field)
        flat[x * 64 : x * 64 + 64, :] = mm(mix_high, high) + mm(mix_high, low) + mm(mix_low, high)
    for o in range(ORB):
        for x in range(CX):
            for h in range(2):
                out_ref[o, x, 8 * h : 8 * h + 8, :] = flat[pl.ds(x * 64 + 4 * h + o, 8, stride=8), :]


def kernel_call(body, outs, ins, scratch=(), name=None):
    return pl.pallas_call(
        body,
        out_shape=[jax.ShapeDtypeStruct(shape, dtype) for shape, dtype in outs],
        in_specs=ins,
        out_specs=[VMEM] * len(outs),
        scratch_shapes=list(scratch),
        compiler_params=pltpu.CompilerParams(vmem_limit_bytes=LIMIT),
        name=name,
    )


def blocks(count, columns=128, dtype=F32):
    return (count * 8, columns), dtype


def beside(low_value, high_value, axis):
    count = lax.axis_size(axis)
    up = [(i, i + 1) for i in range(count - 1)]
    down = [(i + 1, i) for i in range(count - 1)]
    return lax.ppermute(low_value, axis, up), lax.ppermute(high_value, axis, down)


def fold(z, from_left, from_right, tile):
    return kernel_call(
        functools.partial(fold_kernel, tile), [blocks(6), blocks(4), blocks(4)], [VMEM] * 3, name="fold_coeffs"
    )(z, from_left, from_right)


def shards(orbitals, potential, kinetic_mu, projectors, strengths, box_offsets, block_counts):
    dz = jnp.asarray(derivative_table())
    groups = jnp.asarray(group_table())
    y, t, meta, xr, xl, yh, yl = kernel_call(
        prep_kernel,
        [blocks(TILES), blocks(64), blocks(1), blocks(FIRST_X), blocks(FIRST_X), blocks(FIRST_Y), blocks(FIRST_Y)],
        [SMEM, SMEM, SMEM, VMEM, VMEM, VMEM],
        name="prepare",
    )(box_offsets, strengths, block_counts, orbitals, kinetic_mu, projectors)
    from_left, from_right = beside(xr, xl, "gx")
    from_lo, from_hi = beside(yh, yl, "gy")
    t2, metas, hi2, lo2 = kernel_call(
        widen_kernel, [blocks(64), blocks(2), blocks(34), blocks(34)], [VMEM] * 4, name="widen"
    )(t, meta, from_left, from_right)
    from_lo2, from_hi2 = beside(hi2, lo2, "gy")
    (coefs,) = kernel_call(
        coef_kernel,
        [blocks(5 * TILES)],
        [VMEM] * 7,
        [pltpu.VMEM(((TILES + 2 * XH) * 8, 128), F32), pltpu.VMEM((CX * 20 * 8, 128), F32)],
        name="coefficients",
    )(kinetic_mu, potential, from_left, from_right, from_lo, from_hi, dz)
    q, s, w, z, zr, zl = kernel_call(
        build_kernel,
        [
            blocks(6 * 8 * 16, 256),
            ((4 * 128, 256), BF16),
            blocks(6),
            blocks(6),
            blocks(3),
            blocks(3),
        ],
        [VMEM] * 6,
        [pltpu.VMEM((32 * 8, 128), F32), pltpu.VMEM((48, 1024), F32)],
        name="build",
    )(t2, metas, from_lo2, from_hi2, y, groups)
    z_left, z_right = beside(zr, zl, "gx")
    z, z_hi, z_lo = fold(z, z_left, z_right, 0)
    c_lo, c_hi = beside(z_hi, z_lo, "gy")

    previous = y
    for step in range(1, STEPS + 1):
        last = step == STEPS
        outs = [blocks(TILES)]
        if not last:
            outs += [blocks(XH + 3), blocks(XH + 3), blocks(YH), blocks(YH), blocks(6)]
        result = kernel_call(
            functools.partial(step_kernel, step),
            outs,
            [VMEM] * 15,
            [
                pltpu.VMEM(((TILES + 2 * XH) * 8, 128), F32),
                pltpu.VMEM((CX * 20 * 8, 128), F32),
                pltpu.VMEM((TILES * 8, 256), F32),
                pltpu.VMEM((48, 1024), F32),
                pltpu.VMEM((48, 1024), F32),
            ],
            name="step",
        )(y, previous, from_left, from_right, from_lo, from_hi, coefs, q, s, w, z, c_lo, c_hi, dz, groups)
        previous = y
        if last:
            (y,) = result
        else:
            y, xr, xl, yh, yl, z = result
            from_left, from_right = beside(xr, xl, "gx")
            from_lo, from_hi = beside(yh, yl, "gy")
            z, z_hi, z_lo = fold(z, from_left, from_right, XH)
            c_lo, c_hi = beside(z_hi, z_lo, "gy")

    count = lax.axis_size("orb")
    me = lax.axis_index("orb")
    up = [(i, (i + 1) % count) for i in range(count)]
    down = [(i, (i - 1) % count) for i in range(count)]
    parts = lax.all_to_all(y.reshape(count, -1, NZ), "orb", 0, 0, tiled=True)
    y, parts = lax.optimization_barrier((y, parts))
    (corr,) = kernel_call(gram_kernel, [blocks(1)], [VMEM], name="gram")(parts)
    below = lax.ppermute(y, "orb", up)
    above = lax.ppermute(y, "orb", down)
    half = TILES * 4
    across_a = lax.ppermute(below[:half], "orb", up)
    across_b = lax.ppermute(above[half:], "orb", down)
    across = jnp.concatenate([across_a, across_b], axis=0)
    order = jnp.stack([me, (me + count - 1) % count, (me + 1) % count, (me + 2) % count]).astype(jnp.int32)
    for axis in ("orb", "gx", "gy"):
        size = lax.axis_size(axis)
        copies = jnp.broadcast_to(corr[None], (size, 8, 128))
        corr = jnp.sum(lax.all_to_all(copies, axis, 0, 0, tiled=True), axis=0)
    cells = CX * CY * NZ * lax.axis_size("gx") * lax.axis_size("gy")
    (result,) = kernel_call(
        functools.partial(rotate_kernel, cells),
        [((ORB, CX, CY, NZ), F32)],
        [SMEM] + [VMEM] * 5,
        [pltpu.VMEM((TILES * 8, 128), F32)],
        name="rotate",
    )(order, corr, y, below, above, across)
    return result


def solution(mesh):
    in_specs = (
        P("orb", "gx", "gy", None),
        P("gx", "gy", None),
        P("gx", "gy", None),
        P(("gx", "gy"), None, None),
        P(("gx", "gy"), None),
        P(("gx", "gy"), None),
        P(("gx", "gy")),
    )
    out_specs = P("orb", "gx", "gy", None)
    return jax.shard_map(shards, mesh=mesh, in_specs=in_specs, out_specs=out_specs, check_vma=False)
```

```python
import functools

import jax
import jax.numpy as jnp
import ml_dtypes
import numpy as np
from jax import lax
from jax.experimental import pallas as pl
from jax.experimental.pallas import tpu as pltpu
from jax.sharding import PartitionSpec as P

CX, CY, NZ, ORB = 12, 16, 128, 4
HALO = 6
TILES = 96
XH = HALO * 8
YH = CX * 3
STEPS = 3

first_coefs = (6.0 / 7.0, -15.0 / 56.0, 5.0 / 63.0, -1.0 / 56.0, 2.0 / 825.0, -1.0 / 5544.0)
second_coefs = (12.0 / 7.0, -15.0 / 56.0, 10.0 / 189.0, -1.0 / 112.0, 2.0 / 1925.0, -1.0 / 16632.0)
center_coef = -5369.0 / 1800.0
filter_center = 13.5
filter_half = 10.5

F32, BF16 = jnp.float32, jnp.bfloat16
VMEM = pl.BlockSpec(memory_space=pltpu.VMEM)
SMEM = pl.BlockSpec(memory_space=pltpu.SMEM)
LIMIT = 24 * 1024 * 1024


def derivative_table():
    table = np.zeros((NZ, 2 * NZ), np.float64)
    for z in range(NZ):
        table[z, NZ + z] = 3.0 * center_coef
        for k in range(1, HALO + 1):
            if z + k < NZ:
                table[z + k, z] = first_coefs[k - 1]
                table[z + k, NZ + z] = second_coefs[k - 1]
            if z - k >= 0:
                table[z - k, z] = -first_coefs[k - 1]
                table[z - k, NZ + z] = second_coefs[k - 1]
    high = table.astype(ml_dtypes.bfloat16)
    low = (table - high.astype(np.float64)).astype(ml_dtypes.bfloat16)
    return np.concatenate([high, low], axis=0)


def split(a):
    high = a.astype(BF16)
    return high, (a - high.astype(F32)).astype(BF16)


def mm(a, b):
    return jnp.dot(a, b, preferred_element_type=F32)


def mm_t(a, b):
    return lax.dot_general(a, b, (((1,), (1,)), ((), ())), preferred_element_type=F32)


def pick(a, table):
    high, low = split(a)
    return mm(high, table) + mm(low, table)


def pick_t(a, table):
    high, low = split(a)
    return mm_t(high, table) + mm_t(low, table)


def get(ref, tile):
    return ref[pl.ds(tile * 8, 8), :]


def put(ref, tile, value):
    ref[pl.ds(tile * 8, 8), :] = value


def get_at(ref, tile):
    return ref[pl.ds(pl.multiple_of(tile * 8, 8), 8), :]


def iotas():
    return (
        lax.broadcasted_iota(jnp.int32, (8, 128), 0),
        lax.broadcasted_iota(jnp.int32, (8, 128), 1),
    )


def row(value, index):
    return jnp.broadcast_to(value[index : index + 1, :], (8, 128))


def pack_rims(y_ref, hi_ref, lo_ref, low):
    for x in range(CX):
        for m in range(3):
            put(hi_ref, x * 3 + m, jnp.where(low, pltpu.roll(get(y_ref, x * 8 + 2 + m), 4, 0), get(y_ref, x * 8 + 5 + m)))
            put(lo_ref, x * 3 + m, jnp.where(low, get(y_ref, x * 8 + m), pltpu.roll(get(y_ref, x * 8 + 3 + m), 4, 0)))


def put_seam(refs, count, tile, value):
    half = count // 2
    put(refs[tile // half], tile % half, value)


def get_seam(refs, count, tile):
    half = count // 2
    return get(refs[tile // half], tile % half)


def prep_kernel(
    flags, offs, strg, cnt, orb, mu, proj,
    y_ref, t_ref, meta_ref, xr_ref, xl_ref, yh_ref, yl_ref, sa_ref, sb_ref, mu_out, g_ref
):
    mu_out[...] = mu[...]
    at_row = lax.broadcasted_iota(jnp.int32, (1024, 128), 0)
    at_column = lax.broadcasted_iota(jnp.int32, (1024, 128), 1)
    same = (at_row % 128 // 8 == at_column // 8) & (at_row // 128 == at_column % 8)
    g_ref[...] = jnp.where(same, 1.0, 0.0).astype(BF16)
    sub, lane = iotas()
    above_seam = flags[0] == 1
    low = sub < 4
    left_half = lane < 64
    for x in range(CX):
        for o in range(ORB):
            for h in range(2):
                y_ref[pl.ds(x * 64 + 4 * h + o, 8, stride=8), :] = orb[o, x, 8 * h : 8 * h + 8, :]
    group = lane // 8
    meta = jnp.zeros((8, 128), F32)
    for s in range(8):
        for column in range(3):
            value = offs[column, s].astype(F32)
            meta = jnp.where((group == s) & (sub == column), value, meta)
        alive = jnp.where(s < cnt[0], 1.0, 0.0).astype(F32)
        for p in range(8):
            weight = strg[s, p] * alive * (1.0 / (512.0 * filter_half))
            meta = jnp.where((lane == s * 8 + p) & (sub == 3), weight, meta)
    meta_ref[...] = meta
    for i in range(8):
        for j in range(8):
            start = (i % 2) * 64 + j * 8
            total = jnp.zeros((8, 128), F32)
            for s in range(8):
                source = proj[s, :, 128 * (i // 2) : 128 * (i // 2) + 128]
                shift = (s * 8 - start) % 128
                moved = pltpu.roll(source, shift, 1) if shift else source
                total = jnp.where(group == s, moved, total)
            put(t_ref, i * 8 + j, total)
    for q in range(XH):
        put(xr_ref, q, get(y_ref, XH + q))
        put(xl_ref, q, get(y_ref, q))
    for x in range(HALO):
        for h in range(2):
            put(xr_ref, XH + 2 * x + h, mu[CX - HALO + x, 8 * h : 8 * h + 8, :])
            put(xl_ref, XH + 2 * x + h, mu[x, 8 * h : 8 * h + 8, :])
    base = XH + 2 * HALO
    for i in range(2):
        for j in range(8):
            for ref, first in ((xr_ref, 4), (xl_ref, 0)):
                one = get(t_ref, (first + i) * 8 + j)
                two = pltpu.roll(get(t_ref, (first + 2 + i) * 8 + j), 64, 1)
                put(ref, base + i * 8 + j, jnp.where(left_half, one, two))
    put(xr_ref, base + 16, meta)
    put(xl_ref, base + 16, meta)
    pack_rims(y_ref, yh_ref, yl_ref, low)
    for x in range(CX):
        put(yh_ref, YH + x, mu[x, 8:16, :])
        put(yl_ref, YH + x, mu[x, 0:8, :])
    pick_seam(yh_ref, yl_ref, (sa_ref, sb_ref), FIRST_Y, above_seam)


def pick_seam(hi_ref, lo_ref, seams, count, above_seam):
    for t in range(count):
        put_seam(seams, count, t, jnp.where(above_seam, get(lo_ref, t), get(hi_ref, t)))


FIRST_X = XH + 2 * HALO + 17
FIRST_Y = YH + CX


def widen_kernel(flags, t_ref, meta_ref, fl_ref, fr_ref, t2_ref, m_ref, hi_ref, lo_ref, sa_ref, sb_ref):
    _, lane = iotas()
    left_half = lane < 64
    base = XH + 2 * HALO
    for i in range(8):
        for j in range(8):
            if i >= 4:
                other = get(fl_ref, base + (i % 2) * 8 + j)
                other = other if i >= 6 else pltpu.roll(other, 64, 1)
            else:
                other = get(fr_ref, base + (i % 2) * 8 + j)
                other = other if i >= 2 else pltpu.roll(other, 64, 1)
            both = jnp.where(left_half, get(t_ref, i * 8 + j), other)
            put(t2_ref, i * 8 + j, both)
            if j >= 4:
                put(hi_ref, i * 4 + j - 4, both)
            else:
                put(lo_ref, i * 4 + j, both)
    meta = meta_ref[...]
    for side, ref in enumerate((fl_ref, fr_ref)):
        both = jnp.where(left_half, meta, pltpu.roll(get(ref, base + 16), 64, 1))
        put(m_ref, side, both)
        put(hi_ref, 32 + side, both)
        put(lo_ref, 32 + side, both)
    pick_seam(hi_ref, lo_ref, (sa_ref, sb_ref), 34, flags[0] == 1)


def coef_kernel(flags, mu, pot, fl_ref, fr_ref, flo_ref, fhi_ref, sa_ref, sb_ref, dz_ref, out_ref, ex, ey):
    sub, _ = iotas()
    low = sub < 4

    def two(a, ia, b, ib):
        return jnp.where(low, row(a, ia), row(b, ib))

    for x in range(CX + 2 * HALO):
        if x < HALO:
            a, b = get(fl_ref, XH + 2 * x), get(fl_ref, XH + 2 * x + 1)
        elif x < HALO + CX:
            a, b = mu[x - HALO, 0:8, :], mu[x - HALO, 8:16, :]
        else:
            a, b = get(fr_ref, XH + 2 * (x - HALO - CX)), get(fr_ref, XH + 2 * (x - HALO - CX) + 1)
        for yl in range(8):
            put(ex, x * 8 + yl, two(a, yl, b, yl))
    for x in range(CX):
        rim = get_seam((sa_ref, sb_ref), FIRST_Y, YH + x)
        lo_rim = jnp.where(flags[0] == 1, rim, get(flo_ref, YH + x))
        hi_rim = jnp.where(flags[1] == 1, rim, get(fhi_ref, YH + x))
        parts = [lo_rim, mu[x, 0:8, :], mu[x, 8:16, :], hi_rim]
        for n in range(20):
            y = n - HALO
            put(ey, x * 20 + n, two(parts[(y + 8) // 8], y % 8, parts[(y + 16) // 8], y % 8))
    field = ex[XH * 8 : (XH + TILES) * 8, :]
    high, rest = split(field)
    zd = mm(high, dz_ref[0:NZ, 0:NZ]) + mm(rest, dz_ref[0:NZ, 0:NZ]) + mm(high, dz_ref[NZ : 2 * NZ, 0:NZ])
    out_ref[3 * 768 : 4 * 768, :] = zd * (-0.5 / filter_half)

    def body(x, carry):
        va, vb = pot[x, 0:8, :], pot[x, 8:16, :]
        for yl in range(8):
            gx = jnp.zeros((8, 128), F32)
            gy = jnp.zeros((8, 128), F32)
            for k in range(1, HALO + 1):
                gx += first_coefs[k - 1] * (get_at(ex, (x + HALO + k) * 8 + yl) - get_at(ex, (x + HALO - k) * 8 + yl))
                gy += first_coefs[k - 1] * (
                    get_at(ey, x * 20 + HALO + yl + k) - get_at(ey, x * 20 + HALO + yl - k)
                )
            r = x * 8 + yl
            center = get_at(ex, (x + HALO) * 8 + yl)

            def store(which, value):
                out_ref[pl.ds(pl.multiple_of((which * TILES + r) * 8, 8), 8), :] = value

            store(0, (1.0 + center) * (-0.5 / filter_half))
            store(1, gx * (-0.5 / filter_half))
            store(2, gy * (-0.5 / filter_half))
            store(4, (two(va, yl, vb, yl) - filter_center) * (1.0 / filter_half))
        return carry

    lax.fori_loop(0, CX, body, 0)


def block_tiles(xt, yq):
    return [(4 * xt + a) * 8 + 4 * yq for a in range(4)]


def side_of(xt):
    return 1 if xt == 2 else 0


def partial_coeffs(y_ref, q_ref, s_ref, g_ref, z_ref, acc):
    left_half = lax.broadcasted_iota(jnp.int32, (8, 1024), 1) % 128 < 64
    own = None
    ends = {}
    rims = [None, None]
    corners = {}
    for xt in range(3):
        for yq in range(2):
            b = xt * 2 + yq
            field = jnp.concatenate([y_ref[t * 8 : t * 8 + 32, :] for t in block_tiles(xt, yq)], axis=0)
            table = s_ref[(side_of(xt) * 2 + yq) * 128 : (side_of(xt) * 2 + yq) * 128 + 128, :]
            seen = pick(field, table).reshape(16, 8, 256)
            sums = []
            for p in range(8):
                base = (b * 8 + p) * 128
                product = seen * q_ref[base : base + 128, :].reshape(16, 8, 256)
                total = jnp.sum(product, axis=0)
                sums.append(total + pltpu.roll(total, 4, 0))
            col_a = jnp.concatenate([t[:, :128] for t in sums], axis=1)
            col_b = jnp.concatenate([t[:, 128:] for t in sums], axis=1)
            own = col_a if own is None else own + col_a
            rims[yq] = col_b if rims[yq] is None else rims[yq] + col_b
            if xt != 1:
                ends[xt] = ends[xt] + col_a if xt in ends else col_a
                corners[(xt, yq)] = col_b
    for side, xt in enumerate((0, 2)):
        acc[side * 24 : side * 24 + 8, :] = jnp.where(left_half, own, ends[xt])
        for yq in range(2):
            at = side * 24 + 8 + yq * 8
            acc[at : at + 8, :] = jnp.where(left_half, rims[yq], corners[(xt, yq)])
    z_ref[...] = pick(acc[...], g_ref[...])


def send_coeffs(z_ref, xr_ref, xl_ref, base):
    for t in range(3):
        put(xr_ref, base + t, pltpu.roll(get(z_ref, 3 + t), 64, 1))
        put(xl_ref, base + t, pltpu.roll(get(z_ref, t), 64, 1))


def build_kernel(
    flags, t2_ref, m_ref, lo_in, hi_in, sa_ref, sb_ref, y_ref, g_ref,
    q_ref, s_ref, w_ref, z_ref, xr_ref, xl_ref, tx, acc, lo_ref, hi_ref
):
    for t in range(34):
        seam = get_seam((sa_ref, sb_ref), 34, t)
        put(lo_ref, t, jnp.where(flags[0] == 1, seam, get(lo_in, t)))
        put(hi_ref, t, jnp.where(flags[1] == 1, seam, get(hi_in, t)))
    sub, lane = iotas()
    low = sub < 4
    right_half = lane >= 64
    metas = [get(m_ref, 0), get(lo_ref, 32), get(hi_ref, 32), get(m_ref, 1), get(lo_ref, 33), get(hi_ref, 33)]
    for t in range(6):
        put(w_ref, t, row(metas[t], 3))
    zi = lax.broadcasted_iota(jnp.int32, (128, 128), 0)
    for side in range(2):
        for yq in range(2):
            for col, t in enumerate((side * 3, side * 3 + 1 + yq)):
                place = metas[t][2:3, :].astype(jnp.int32) + lane[0:1, :] % 8
                base = (side * 2 + yq) * 128
                hot = jnp.where(zi == jnp.broadcast_to(place, (128, 128)), 1.0, 0.0).astype(BF16)
                s_ref[base : base + 128, col * 128 : col * 128 + 128] = hot

    def table(col, i, j):
        if col == 0:
            return get(t2_ref, i * 8 + j)
        return get(lo_ref, i * 4 + j - 4) if j >= 4 else get(hi_ref, i * 4 + j)

    zero = jnp.zeros((8, 128), F32)
    for xt in range(3):
        shift = (-12.0, 1000.0, 12.0)[xt]
        for col in range(2):
            for yq in range(2):
                b = xt * 2 + yq
                t = side_of(xt) * 3 + (0 if col == 0 else 1 + yq)
                x0 = row(metas[t], 0) - 6.0 + jnp.where(right_half, shift, 0.0)
                y0 = row(metas[t], 1) - 6.0
                if col == 1:
                    y0 = y0 + (16.0 if yq == 1 else -16.0)
                js = range(8) if col == 0 else (range(0, 4) if yq == 1 else range(4, 8))
                if col == 1 or yq == 0:
                    for a in range(4):
                        for j in js:
                            moved = zero
                            for i in range(8):
                                moved = jnp.where(x0 == float(4 * xt + a - i), table(col, i, j), moved)
                            put(tx, a * 8 + j, moved)
                for a in range(4):
                    for c in range(4):
                        rows = []
                        for h in range(2):
                            y = 8 * h + 4 * yq + c
                            moved = zero
                            if col == 0 or h == yq:
                                for j in js:
                                    moved = jnp.where(y0 == float(y - j), get(tx, a * 8 + j), moved)
                            rows.append(moved)
                        for p in range(8):
                            base = ((b * 8 + p) * 16 + a * 4 + c) * 8
                            value = jnp.where(low, row(rows[0], p), row(rows[1], p))
                            q_ref[base : base + 8, col * 128 : col * 128 + 128] = value
    partial_coeffs(y_ref, q_ref, s_ref, g_ref, z_ref, acc)
    send_coeffs(z_ref, xr_ref, xl_ref, 0)


def fold_kernel(base, z_ref, fl_ref, fr_ref, out_ref, hi_ref, lo_ref):
    _, lane = iotas()
    left_half = lane < 64
    tiles = []
    for side in range(2):
        near, far = (fl_ref, fr_ref) if side == 0 else (fr_ref, fl_ref)
        for t in range(3):
            tiles.append(get(z_ref, side * 3 + t) + get(near, base + t) + jnp.where(left_half, get(far, base + t), 0.0))
    for t in range(6):
        put(out_ref, t, tiles[t])
    for side in range(2):
        put(hi_ref, side * 2, tiles[side * 3 + 2])
        put(hi_ref, side * 2 + 1, tiles[side * 3])
        put(lo_ref, side * 2, tiles[side * 3 + 1])
        put(lo_ref, side * 2 + 1, tiles[side * 3])


def step_kernel(
    step, seam_count, flags, y_ref, prev_ref, fl_ref, fr_ref, plo_ref, phi_ref, sa_ref, sb_ref, coef_ref, q_ref, s_ref, w_ref, z_ref, clo_ref, chi_ref,
    dz_ref, g_ref, *rest
):
    last = step == STEPS
    if last:
        new_ref, ex, ey, zd, acc, wp = rest
    else:
        new_ref, xr_ref, xl_ref, yh_ref, yl_ref, na_ref, nb_ref, zn_ref, ex, ey, zd, acc, wp = rest
    sub, _ = iotas()
    low = sub < 4
    scale = 1.0 if step == 1 else 2.0

    high, rest_part = split(y_ref[...])
    zd[...] = mm(high, dz_ref[0:NZ, :]) + mm(rest_part, dz_ref[0:NZ, :]) + mm(high, dz_ref[NZ : 2 * NZ, :])

    ex[0 : XH * 8, :] = fl_ref[0 : XH * 8, :]
    ex[XH * 8 : (XH + TILES) * 8, :] = y_ref[...]
    ex[(XH + TILES) * 8 : (2 * XH + TILES) * 8, :] = fr_ref[0 : XH * 8, :]
    for x in range(CX):
        for yl in range(8):
            put(ey, x * 20 + HALO + yl, get(y_ref, x * 8 + yl))
        lo_rims, hi_rims = [], []
        for m in range(3):
            seam = get_seam((sa_ref, sb_ref), seam_count, x * 3 + m)
            lo_rims.append(jnp.where(flags[0] == 1, seam, get(plo_ref, x * 3 + m)))
            hi_rims.append(jnp.where(flags[1] == 1, seam, get(phi_ref, x * 3 + m)))
        for m in range(HALO):
            rim = lo_rims[m] if m < 3 else pltpu.roll(lo_rims[m - 3], 4, 0)
            put(ey, x * 20 + m, jnp.where(low, rim, pltpu.roll(get(y_ref, x * 8 + 2 + m), 4, 0)))
            rim = pltpu.roll(hi_rims[m], 4, 0) if m < 3 else hi_rims[m - 3]
            put(ey, x * 20 + HALO + 8 + m, jnp.where(low, pltpu.roll(get(y_ref, x * 8 + m), 4, 0), rim))

    def body(x, carry):
        for yl in range(8):
            r = x * 8 + yl
            center = get_at(y_ref, r)
            gx = gy = lap = None
            for k in range(1, HALO + 1):
                xp, xm = get_at(ex, (x + HALO + k) * 8 + yl), get_at(ex, (x + HALO - k) * 8 + yl)
                yp, ym = get_at(ey, x * 20 + HALO + yl + k), get_at(ey, x * 20 + HALO + yl - k)
                tx = first_coefs[k - 1] * (xp - xm)
                ty = first_coefs[k - 1] * (yp - ym)
                tl = second_coefs[k - 1] * ((xp + xm) + (yp + ym))
                gx, gy, lap = (tx, ty, tl) if k == 1 else (gx + tx, gy + ty, lap + tl)
            at = pl.ds(pl.multiple_of(r * 8, 8), 8)
            total = get_at(coef_ref, r) * (lap + zd[at, NZ:])
            total += get_at(coef_ref, TILES + r) * gx
            total += get_at(coef_ref, 2 * TILES + r) * gy
            total += get_at(coef_ref, 3 * TILES + r) * zd[at, :NZ]
            total += get_at(coef_ref, 4 * TILES + r) * center
            new_ref[at, :] = total if step == 1 else 2.0 * total - get_at(prev_ref, r)
        return carry

    lax.fori_loop(0, CX, body, 0)

    tiles = []
    for side in range(2):
        own, lo, hi = (get(z_ref, side * 3 + t) for t in range(3))
        tiles.append(own + get(clo_ref, side * 2) + get(chi_ref, side * 2))
        tiles.append(lo + get(clo_ref, side * 2 + 1))
        tiles.append(hi + get(chi_ref, side * 2 + 1))
    weights = jnp.concatenate(tiles, axis=0) * w_ref[...] * scale
    wp[...] = pick_t(weights, g_ref[...])

    for xt in range(3):
        for yq in range(2):
            b = xt * 2 + yq
            ta, tb = side_of(xt) * 3, side_of(xt) * 3 + 1 + yq
            total = None
            for p in range(8):
                weight = jnp.concatenate(
                    [wp[t * 8 : t * 8 + 8, p * 128 : p * 128 + 128] for t in (ta, tb)], axis=1
                )
                base = (b * 8 + p) * 128
                term = weight[None] * q_ref[base : base + 128, :].reshape(16, 8, 256)
                total = term if total is None else total + term
            table = s_ref[(side_of(xt) * 2 + yq) * 128 : (side_of(xt) * 2 + yq) * 128 + 128, :]
            spread = pick_t(total.reshape(128, 256), table)
            for a, t in enumerate(block_tiles(xt, yq)):
                new_ref[t * 8 : t * 8 + 32, :] += spread[a * 32 : a * 32 + 32, :]

    if not last:
        for q in range(XH):
            put(xr_ref, q, get(new_ref, XH + q))
            put(xl_ref, q, get(new_ref, q))
        pack_rims(new_ref, yh_ref, yl_ref, low)
        pick_seam(yh_ref, yl_ref, (na_ref, nb_ref), YH, flags[0] == 1)
        partial_coeffs(new_ref, q_ref, s_ref, g_ref, zn_ref, acc)
        send_coeffs(zn_ref, xr_ref, xl_ref, XH)


def gram_kernel(parts_ref, out_ref):
    total = jnp.zeros((256, 256), F32)
    for x in range(CX // 4):
        field = jnp.concatenate([parts_ref[d, x * 64 : x * 64 + 64, :] for d in range(4)], axis=0)
        high, low = split(field)
        total = total + (mm_t(high, high) + mm_t(high, low) + mm_t(low, high))
    rows = lax.broadcasted_iota(jnp.int32, (256, 256), 0)
    columns = lax.broadcasted_iota(jnp.int32, (256, 256), 1)
    total = jnp.where((rows % 64) // 4 == (columns % 64) // 4, total, 0.0)
    orbital = lax.broadcasted_iota(jnp.int32, (16, 256), 0)
    held_at = lax.broadcasted_iota(jnp.int32, (16, 256), 1)
    hot = jnp.where(orbital == held_at // 64 * 4 + held_at % 4, 1.0, 0.0).astype(F32)
    first = jnp.dot(hot, total, precision=lax.Precision.HIGHEST, preferred_element_type=F32)
    small = lax.dot_general(
        first, hot, (((1,), (1,)), ((), ())), precision=lax.Precision.HIGHEST, preferred_element_type=F32
    )
    out_ref[...] = jnp.zeros((8, 128), F32)
    out_ref[:, 0:16] = small[0:8]
    out_ref[:, 16:32] = small[8:16]


def rotate_kernel(cells, order, corr_ref, a0, a1, a2, a3, out_ref, flat):
    lane = lax.broadcasted_iota(jnp.int32, (16, 128), 1)
    rows = lax.broadcasted_iota(jnp.int32, (16, 128), 0)
    packed = corr_ref[...]
    whole = jnp.concatenate([packed, pltpu.roll(packed, 112, 1)], axis=0)
    work = jnp.where(lane < 16, whole * (1.0 / cells), jnp.where(lane == rows + 16, 1.0, 0.0))
    pivots = jnp.ones((16, 128), F32)
    for k in range(16):
        pivot_row = jnp.broadcast_to(work[k : k + 1, :], (16, 128))
        pivot = jnp.broadcast_to(pivot_row[:, k : k + 1], (16, 128))
        column = jnp.broadcast_to(work[:, k : k + 1], (16, 128))
        pivots = jnp.where(rows == k, pivot, pivots)
        work = jnp.where(rows > k, work - column / pivot * pivot_row, work)
    inverse = (work / jnp.sqrt(pivots))[:, 16:32]
    me = order[0]
    own_row = lax.broadcasted_iota(jnp.int32, (64, 16), 0)
    orbital = lax.broadcasted_iota(jnp.int32, (64, 16), 1)
    left = jnp.where(orbital == me * 4 + own_row % 4, 1.0, 0.0).astype(F32)
    orbital = lax.broadcasted_iota(jnp.int32, (16, 256), 0)
    held_at = lax.broadcasted_iota(jnp.int32, (16, 256), 1)
    device = held_at // 64
    owner = jnp.where(device == 0, order[0], jnp.where(device == 1, order[1], jnp.where(device == 2, order[2], order[3])))
    right = jnp.where(orbital == owner * 4 + held_at % 4, 1.0, 0.0).astype(F32)
    exact = functools.partial(jnp.dot, precision=lax.Precision.HIGHEST, preferred_element_type=F32)
    mixing = exact(exact(left, inverse), right)
    at_row = lax.broadcasted_iota(jnp.int32, (64, 256), 0)
    at_column = lax.broadcasted_iota(jnp.int32, (64, 256), 1)
    mixing = jnp.where(at_row // 4 == at_column % 64 // 4, mixing, 0.0)
    mix_high, mix_low = split(mixing)
    for x in range(CX):
        field = jnp.concatenate([ref[x * 64 : x * 64 + 64, :] for ref in (a0, a1, a2, a3)], axis=0)
        high, low = split(field)
        flat[x * 64 : x * 64 + 64, :] = mm(mix_high, high) + mm(mix_high, low) + mm(mix_low, high)
    for o in range(ORB):
        for x in range(CX):
            for h in range(2):
                out_ref[o, x, 8 * h : 8 * h + 8, :] = flat[pl.ds(x * 64 + 4 * h + o, 8, stride=8), :]


def kernel_call(body, outs, ins, scratch=(), name=None):
    return pl.pallas_call(
        body,
        out_shape=[jax.ShapeDtypeStruct(shape, dtype) for shape, dtype in outs],
        in_specs=ins,
        out_specs=[VMEM] * len(outs),
        scratch_shapes=list(scratch),
        compiler_params=pltpu.CompilerParams(vmem_limit_bytes=LIMIT),
        name=name,
    )


def blocks(count, columns=128, dtype=F32):
    return (count * 8, columns), dtype


def beside(low_value, high_value, axis):
    count = lax.axis_size(axis)
    up = [(i, i + 1) for i in range(count - 1)]
    down = [(i + 1, i) for i in range(count - 1)]
    return lax.ppermute(low_value, axis, up), lax.ppermute(high_value, axis, down)


def across_seam(part_a, part_b):
    size, depth = lax.axis_size("gy"), lax.axis_size("gx") // 2
    half = size // 2

    def index(z, core, y):
        z = z % (2 * depth)
        return (z % depth * 2 + core) * size + z // depth * half + y

    first, second = [], []
    for z in range(2 * depth):
        for core in range(2):
            own, other = (half - 1, 0) if z < depth else (0, half - 1)
            stop = index(z - depth // 2, core, own)
            first.append((index(z, core, own), stop))
            second.append((stop, index(z + depth, core, other)))
    stopped = lax.ppermute(part_b, ("gx", "gy"), first)
    straight = lax.ppermute(part_a, "gy", [(half - 1, half), (half, half - 1)])
    return straight, lax.ppermute(stopped, ("gx", "gy"), second)


def beside_in_half(low_value, high_value, axis):
    count = lax.axis_size(axis)
    steps = [i for i in range(count - 1) if i != count // 2 - 1]
    up, down = [(i, i + 1) for i in steps], [(i + 1, i) for i in steps]
    return lax.ppermute(low_value, axis, up), lax.ppermute(high_value, axis, down)


def spread_sum(value, axis):
    copies = jnp.broadcast_to(value[None], (lax.axis_size(axis),) + value.shape)
    return jnp.sum(lax.all_to_all(copies, axis, 0, 0, tiled=True), axis=0)


def fold(z, from_left, from_right, tile):
    return kernel_call(
        functools.partial(fold_kernel, tile), [blocks(6), blocks(4), blocks(4)], [VMEM] * 3, name="fold_coeffs"
    )(z, from_left, from_right)


def shards(orbitals, potential, kinetic_mu, projectors, strengths, box_offsets, block_counts):
    dz = jnp.asarray(derivative_table())
    row_at, rows = lax.axis_index("gy"), lax.axis_size("gy")
    flags = jnp.stack([row_at == rows // 2, row_at == rows // 2 - 1]).astype(jnp.int32)
    y, t, meta, xr, xl, yh, yl, sa, sb, mu, groups = kernel_call(
        prep_kernel,
        [blocks(TILES), blocks(64), blocks(1), blocks(FIRST_X), blocks(FIRST_X), blocks(FIRST_Y), blocks(FIRST_Y)]
        + [blocks(FIRST_Y // 2), blocks(FIRST_Y // 2), ((CX, CY, NZ), F32), ((1024, 128), BF16)],
        [SMEM] * 4 + [VMEM] * 3,
        name="prepare",
    )(flags, box_offsets.T, strengths, block_counts, orbitals, kinetic_mu, projectors)
    seam_a, seam_b = across_seam(sa, sb)
    from_left, from_right = beside(xr, xl, "gx")
    from_lo, from_hi = beside_in_half(yh, yl, "gy")
    t2, metas, hi2, lo2, sa2, sb2 = kernel_call(
        widen_kernel,
        [blocks(64), blocks(2), blocks(34), blocks(34), blocks(17), blocks(17)],
        [SMEM] + [VMEM] * 4,
        name="widen",
    )(flags, t, meta, from_left, from_right)
    seam_a2, seam_b2 = across_seam(sa2, sb2)
    from_lo2, from_hi2 = beside_in_half(hi2, lo2, "gy")
    (coefs,) = kernel_call(
        coef_kernel,
        [blocks(5 * TILES)],
        [SMEM] + [VMEM] * 9,
        [pltpu.VMEM(((TILES + 2 * XH) * 8, 128), F32), pltpu.VMEM((CX * 20 * 8, 128), F32)],
        name="coefficients",
    )(flags, mu, potential, from_left, from_right, from_lo, from_hi, seam_a, seam_b, dz)
    q, s, w, z, zr, zl = kernel_call(
        build_kernel,
        [blocks(6 * 8 * 16, 256), ((4 * 128, 256), BF16), blocks(6), blocks(6), blocks(3), blocks(3)],
        [SMEM] + [VMEM] * 8,
        [
            pltpu.VMEM((32 * 8, 128), F32),
            pltpu.VMEM((48, 1024), F32),
            pltpu.VMEM((34 * 8, 128), F32),
            pltpu.VMEM((34 * 8, 128), F32),
        ],
        name="build",
    )(flags, t2, metas, from_lo2, from_hi2, seam_a2, seam_b2, y, groups)
    z_left, z_right = beside(zr, zl, "gx")
    z, z_hi, z_lo = fold(z, z_left, z_right, 0)
    c_lo, c_hi = beside(z_hi, z_lo, "gy")

    previous = y
    for step in range(1, STEPS + 1):
        last = step == STEPS
        outs = [blocks(TILES)]
        if not last:
            outs += [blocks(XH + 3), blocks(XH + 3), blocks(YH), blocks(YH), blocks(YH // 2), blocks(YH // 2), blocks(6)]
        result = kernel_call(
            functools.partial(step_kernel, step, FIRST_Y if step == 1 else YH),
            outs,
            [SMEM] + [VMEM] * 17,
            [
                pltpu.VMEM(((TILES + 2 * XH) * 8, 128), F32),
                pltpu.VMEM((CX * 20 * 8, 128), F32),
                pltpu.VMEM((TILES * 8, 256), F32),
                pltpu.VMEM((48, 1024), F32),
                pltpu.VMEM((48, 1024), F32),
            ],
            name="step",
        )(
            flags, y, previous, from_left, from_right, from_lo, from_hi, seam_a, seam_b,
            coefs, q, s, w, z, c_lo, c_hi, dz, groups,
        )
        previous = y
        if last:
            (y,) = result
        else:
            y, xr, xl, yh, yl, sa, sb, z = result
            seam_a, seam_b = across_seam(sa, sb)
            from_left, from_right = beside(xr, xl, "gx")
            from_lo, from_hi = beside_in_half(yh, yl, "gy")
            z, z_hi, z_lo = fold(z, from_left, from_right, XH)
            c_lo, c_hi = beside(z_hi, z_lo, "gy")

    count = lax.axis_size("orb")
    me = lax.axis_index("orb")
    up = [(i, (i + 1) % count) for i in range(count)]
    down = [(i, (i - 1) % count) for i in range(count)]
    parts = lax.all_to_all(y.reshape(count, -1, NZ), "orb", 0, 0, tiled=True)
    (corr,) = kernel_call(gram_kernel, [blocks(1)], [VMEM], name="gram")(parts)
    y, corr = lax.optimization_barrier((y, corr))
    below = lax.ppermute(y, "orb", up)
    above = lax.ppermute(y, "orb", down)
    corr = spread_sum(corr, "gy")
    below, above, corr = lax.optimization_barrier((below, above, corr))
    half = TILES * 4
    across_a = lax.ppermute(below[:half], "orb", up)
    across_b = lax.ppermute(above[half:], "orb", down)
    corr = spread_sum(spread_sum(corr, "gx"), "orb")
    across = jnp.concatenate([across_a, across_b], axis=0)
    order = jnp.stack([me, (me + count - 1) % count, (me + 1) % count, (me + 2) % count]).astype(jnp.int32)
    cells = CX * CY * NZ * lax.axis_size("gx") * lax.axis_size("gy")
    (result,) = kernel_call(
        functools.partial(rotate_kernel, cells),
        [((ORB, CX, CY, NZ), F32)],
        [SMEM] + [VMEM] * 5,
        [pltpu.VMEM((TILES * 8, 128), F32)],
        name="rotate",
    )(order, corr, y, below, above, across)
    return result


def solution(mesh):
    in_specs = (
        P("orb", "gx", "gy", None),
        P("gx", "gy", None),
        P("gx", "gy", None),
        P(("gx", "gy"), None, None),
        P(("gx", "gy"), None),
        P(("gx", "gy"), None),
        P(("gx", "gy")),
    )
    out_specs = P("orb", "gx", "gy", None)
    return jax.shard_map(shards, mesh=mesh, in_specs=in_specs, out_specs=out_specs, check_vma=False)
```

```python
import functools

import jax
import jax.numpy as jnp
import ml_dtypes
import numpy as np
from jax import lax
from jax.experimental import pallas as pl
from jax.experimental.pallas import tpu as pltpu
from jax.sharding import PartitionSpec as P

CX, CY, NZ, ORB = 12, 16, 128, 4
HALO = 6
TILES = 96
XH = HALO * 8
YH = CX * 3
STEPS = 3

first_coefs = (6.0 / 7.0, -15.0 / 56.0, 5.0 / 63.0, -1.0 / 56.0, 2.0 / 825.0, -1.0 / 5544.0)
second_coefs = (12.0 / 7.0, -15.0 / 56.0, 10.0 / 189.0, -1.0 / 112.0, 2.0 / 1925.0, -1.0 / 16632.0)
center_coef = -5369.0 / 1800.0
filter_center = 13.5
filter_half = 10.5

F32, BF16 = jnp.float32, jnp.bfloat16
VMEM = pl.BlockSpec(memory_space=pltpu.VMEM)
SMEM = pl.BlockSpec(memory_space=pltpu.SMEM)
LIMIT = 24 * 1024 * 1024


def derivative_table():
    table = np.zeros((NZ, 2 * NZ), np.float64)
    for z in range(NZ):
        table[z, NZ + z] = 3.0 * center_coef
        for k in range(1, HALO + 1):
            if z + k < NZ:
                table[z + k, z] = first_coefs[k - 1]
                table[z + k, NZ + z] = second_coefs[k - 1]
            if z - k >= 0:
                table[z - k, z] = -first_coefs[k - 1]
                table[z - k, NZ + z] = second_coefs[k - 1]
    high = table.astype(ml_dtypes.bfloat16)
    low = (table - high.astype(np.float64)).astype(ml_dtypes.bfloat16)
    return np.concatenate([high, low], axis=0)


def split(a):
    high = a.astype(BF16)
    return high, (a - high.astype(F32)).astype(BF16)


def mm(a, b):
    return jnp.dot(a, b, preferred_element_type=F32)


def mm_t(a, b):
    return lax.dot_general(a, b, (((1,), (1,)), ((), ())), preferred_element_type=F32)


def pick(a, table):
    high, low = split(a)
    return mm(high, table) + mm(low, table)


def pick_t(a, table):
    high, low = split(a)
    return mm_t(high, table) + mm_t(low, table)


def get(ref, tile):
    return ref[pl.ds(tile * 8, 8), :]


def put(ref, tile, value):
    ref[pl.ds(tile * 8, 8), :] = value


def get_at(ref, tile):
    return ref[pl.ds(pl.multiple_of(tile * 8, 8), 8), :]


def iotas():
    return (
        lax.broadcasted_iota(jnp.int32, (8, 128), 0),
        lax.broadcasted_iota(jnp.int32, (8, 128), 1),
    )


def row(value, index):
    return jnp.broadcast_to(value[index : index + 1, :], (8, 128))


def pack_rims(y_ref, hi_ref, lo_ref, low):
    for x in range(CX):
        for m in range(3):
            put(hi_ref, x * 3 + m, jnp.where(low, pltpu.roll(get(y_ref, x * 8 + 2 + m), 4, 0), get(y_ref, x * 8 + 5 + m)))
            put(lo_ref, x * 3 + m, jnp.where(low, get(y_ref, x * 8 + m), pltpu.roll(get(y_ref, x * 8 + 3 + m), 4, 0)))


def sides(odd, even_op, odd_op):
    return jnp.where(odd, even_op, odd_op), jnp.where(odd, odd_op, even_op)


def send(flag, below, above, even_ref, odd_ref, tiles, base=0):
    even_from = jnp.where(flag == 1, 0, 1)
    for t in range(tiles):
        one, two = get(below, t), get(above, t)
        put(even_ref, base + t, jnp.where(even_from == 0, one, two))
        put(odd_ref, base + t, jnp.where(even_from == 0, two, one))


def take(flag, even_ref, odd_ref, target, rows, low_at, high_at):
    even_at = pl.multiple_of(jnp.where(flag == 1, low_at, high_at), 8)
    odd_at = pl.multiple_of(jnp.where(flag == 1, high_at, low_at), 8)
    target[pl.ds(even_at, rows), :] = even_ref[0:rows, :]
    target[pl.ds(odd_at, rows), :] = odd_ref[0:rows, :]


def give_ends(flag, y_ref, even_ref, odd_ref):
    rows = XH * 8
    even_at = pl.multiple_of(jnp.where(flag == 1, 0, rows), 8)
    odd_at = pl.multiple_of(jnp.where(flag == 1, rows, 0), 8)
    even_ref[0:rows, :] = y_ref[pl.ds(even_at, rows), :]
    odd_ref[0:rows, :] = y_ref[pl.ds(odd_at, rows), :]


def prep_kernel(
    flags, offs, strg, cnt, orb, mu, proj,
    y_ref, t_ref, meta_ref, xe_ref, xo_ref, ye_ref, yo_ref, mu_out, g_ref, xr_ref, xl_ref, yh_ref, yl_ref
):
    mu_out[...] = mu[...]
    at_row = lax.broadcasted_iota(jnp.int32, (1024, 128), 0)
    at_column = lax.broadcasted_iota(jnp.int32, (1024, 128), 1)
    same = (at_row % 128 // 8 == at_column // 8) & (at_row // 128 == at_column % 8)
    g_ref[...] = jnp.where(same, 1.0, 0.0).astype(BF16)
    sub, lane = iotas()
    low = sub < 4
    left_half = lane < 64
    for x in range(CX):
        for o in range(ORB):
            for h in range(2):
                y_ref[pl.ds(x * 64 + 4 * h + o, 8, stride=8), :] = orb[o, x, 8 * h : 8 * h + 8, :]
    group = lane // 8
    meta = jnp.zeros((8, 128), F32)
    for s in range(8):
        for column in range(3):
            value = offs[column, s].astype(F32)
            meta = jnp.where((group == s) & (sub == column), value, meta)
        alive = jnp.where(s < cnt[0], 1.0, 0.0).astype(F32)
        for p in range(8):
            weight = strg[s, p] * alive * (1.0 / (512.0 * filter_half))
            meta = jnp.where((lane == s * 8 + p) & (sub == 3), weight, meta)
    meta_ref[...] = meta
    for i in range(8):
        for j in range(8):
            start = (i % 2) * 64 + j * 8
            total = jnp.zeros((8, 128), F32)
            for s in range(8):
                source = proj[s, :, 128 * (i // 2) : 128 * (i // 2) + 128]
                shift = (s * 8 - start) % 128
                moved = pltpu.roll(source, shift, 1) if shift else source
                total = jnp.where(group == s, moved, total)
            put(t_ref, i * 8 + j, total)
    give_ends(flags[0], y_ref, xe_ref, xo_ref)
    for x in range(HALO):
        for h in range(2):
            put(xr_ref, 2 * x + h, mu[CX - HALO + x, 8 * h : 8 * h + 8, :])
            put(xl_ref, 2 * x + h, mu[x, 8 * h : 8 * h + 8, :])
    base = 2 * HALO
    for i in range(2):
        for j in range(8):
            for ref, first in ((xr_ref, 4), (xl_ref, 0)):
                one = get(t_ref, (first + i) * 8 + j)
                two = pltpu.roll(get(t_ref, (first + 2 + i) * 8 + j), 64, 1)
                put(ref, base + i * 8 + j, jnp.where(left_half, one, two))
    put(xr_ref, base + 16, meta)
    put(xl_ref, base + 16, meta)
    pack_rims(y_ref, yh_ref, yl_ref, low)
    for x in range(CX):
        put(yh_ref, YH + x, mu[x, 8:16, :])
        put(yl_ref, YH + x, mu[x, 0:8, :])
    send(flags[0], xl_ref, xr_ref, xe_ref, xo_ref, 2 * HALO + 17, XH)
    send(flags[1], yl_ref, yh_ref, ye_ref, yo_ref, FIRST_Y)


FIRST_X = XH + 2 * HALO + 17
FIRST_Y = YH + CX


def widen_kernel(flags, t_ref, meta_ref, xe_ref, xo_ref, t2_ref, m_ref, ye_ref, yo_ref, fl_ref, fr_ref, hi_ref, lo_ref):
    _, lane = iotas()
    left_half = lane < 64
    base = 0
    for t in range(17):
        left, right = sides(flags[0] == 1, get(xe_ref, XH + 2 * HALO + t), get(xo_ref, XH + 2 * HALO + t))
        put(fl_ref, t, left)
        put(fr_ref, t, right)
    for i in range(8):
        for j in range(8):
            if i >= 4:
                other = get(fl_ref, base + (i % 2) * 8 + j)
                other = other if i >= 6 else pltpu.roll(other, 64, 1)
            else:
                other = get(fr_ref, base + (i % 2) * 8 + j)
                other = other if i >= 2 else pltpu.roll(other, 64, 1)
            both = jnp.where(left_half, get(t_ref, i * 8 + j), other)
            put(t2_ref, i * 8 + j, both)
            if j >= 4:
                put(hi_ref, i * 4 + j - 4, both)
            else:
                put(lo_ref, i * 4 + j, both)
    meta = meta_ref[...]
    for side, ref in enumerate((fl_ref, fr_ref)):
        both = jnp.where(left_half, meta, pltpu.roll(get(ref, base + 16), 64, 1))
        put(m_ref, side, both)
        put(hi_ref, 32 + side, both)
        put(lo_ref, 32 + side, both)
    send(flags[1], lo_ref, hi_ref, ye_ref, yo_ref, 34)


def coef_kernel(flags, mu, pot, xe_ref, xo_ref, ye_ref, yo_ref, dz_ref, out_ref, ex, ey):
    sub, _ = iotas()
    low = sub < 4

    def two(a, ia, b, ib):
        return jnp.where(low, row(a, ia), row(b, ib))

    ends = [sides(flags[0] == 1, get(xe_ref, XH + t), get(xo_ref, XH + t)) for t in range(2 * HALO)]
    for x in range(CX + 2 * HALO):
        if x < HALO:
            a, b = ends[2 * x][0], ends[2 * x + 1][0]
        elif x < HALO + CX:
            a, b = mu[x - HALO, 0:8, :], mu[x - HALO, 8:16, :]
        else:
            a, b = ends[2 * (x - HALO - CX)][1], ends[2 * (x - HALO - CX) + 1][1]
        for yl in range(8):
            put(ex, x * 8 + yl, two(a, yl, b, yl))
    for x in range(CX):
        lo_rim, hi_rim = sides(flags[1] == 1, get(ye_ref, YH + x), get(yo_ref, YH + x))
        parts = [lo_rim, mu[x, 0:8, :], mu[x, 8:16, :], hi_rim]
        for n in range(20):
            y = n - HALO
            put(ey, x * 20 + n, two(parts[(y + 8) // 8], y % 8, parts[(y + 16) // 8], y % 8))
    field = ex[XH * 8 : (XH + TILES) * 8, :]
    high, rest = split(field)
    zd = mm(high, dz_ref[0:NZ, 0:NZ]) + mm(rest, dz_ref[0:NZ, 0:NZ]) + mm(high, dz_ref[NZ : 2 * NZ, 0:NZ])
    out_ref[3 * 768 : 4 * 768, :] = zd * (-0.5 / filter_half)

    def body(x, carry):
        va, vb = pot[x, 0:8, :], pot[x, 8:16, :]
        for yl in range(8):
            gx = jnp.zeros((8, 128), F32)
            gy = jnp.zeros((8, 128), F32)
            for k in range(1, HALO + 1):
                gx += first_coefs[k - 1] * (get_at(ex, (x + HALO + k) * 8 + yl) - get_at(ex, (x + HALO - k) * 8 + yl))
                gy += first_coefs[k - 1] * (
                    get_at(ey, x * 20 + HALO + yl + k) - get_at(ey, x * 20 + HALO + yl - k)
                )
            r = x * 8 + yl
            center = get_at(ex, (x + HALO) * 8 + yl)

            def store(which, value):
                out_ref[pl.ds(pl.multiple_of((which * TILES + r) * 8, 8), 8), :] = value

            store(0, (1.0 + center) * (-0.5 / filter_half))
            store(1, gx * (-0.5 / filter_half))
            store(2, gy * (-0.5 / filter_half))
            store(4, (two(va, yl, vb, yl) - filter_center) * (1.0 / filter_half))
        return carry

    lax.fori_loop(0, CX, body, 0)


def block_tiles(xt, yq):
    return [(4 * xt + a) * 8 + 4 * yq for a in range(4)]


def side_of(xt):
    return 1 if xt == 2 else 0


def partial_coeffs(y_ref, q_ref, s_ref, g_ref, z_ref, acc):
    left_half = lax.broadcasted_iota(jnp.int32, (8, 1024), 1) % 128 < 64
    own = None
    ends = {}
    rims = [None, None]
    corners = {}
    for xt in range(3):
        for yq in range(2):
            b = xt * 2 + yq
            field = jnp.concatenate([y_ref[t * 8 : t * 8 + 32, :] for t in block_tiles(xt, yq)], axis=0)
            table = s_ref[(side_of(xt) * 2 + yq) * 128 : (side_of(xt) * 2 + yq) * 128 + 128, :]
            seen = pick(field, table).reshape(16, 8, 256)
            sums = []
            for p in range(8):
                base = (b * 8 + p) * 128
                product = seen * q_ref[base : base + 128, :].reshape(16, 8, 256)
                total = jnp.sum(product, axis=0)
                sums.append(total + pltpu.roll(total, 4, 0))
            col_a = jnp.concatenate([t[:, :128] for t in sums], axis=1)
            col_b = jnp.concatenate([t[:, 128:] for t in sums], axis=1)
            own = col_a if own is None else own + col_a
            rims[yq] = col_b if rims[yq] is None else rims[yq] + col_b
            if xt != 1:
                ends[xt] = ends[xt] + col_a if xt in ends else col_a
                corners[(xt, yq)] = col_b
    for side, xt in enumerate((0, 2)):
        acc[side * 24 : side * 24 + 8, :] = jnp.where(left_half, own, ends[xt])
        for yq in range(2):
            at = side * 24 + 8 + yq * 8
            acc[at : at + 8, :] = jnp.where(left_half, rims[yq], corners[(xt, yq)])
    z_ref[...] = pick(acc[...], g_ref[...])


def send_coeffs(flag, z_ref, xe_ref, xo_ref, base):
    for t in range(3):
        left, right = pltpu.roll(get(z_ref, t), 64, 1), pltpu.roll(get(z_ref, 3 + t), 64, 1)
        put(xe_ref, base + t, jnp.where(flag == 1, left, right))
        put(xo_ref, base + t, jnp.where(flag == 1, right, left))


def build_kernel(
    flags, t2_ref, m_ref, ye_ref, yo_ref, y_ref, g_ref,
    q_ref, s_ref, w_ref, z_ref, xe_ref, xo_ref, tx, acc, lo_ref, hi_ref
):
    for t in range(34):
        lo, hi = sides(flags[1] == 1, get(ye_ref, t), get(yo_ref, t))
        put(lo_ref, t, lo)
        put(hi_ref, t, hi)
    sub, lane = iotas()
    low = sub < 4
    right_half = lane >= 64
    metas = [get(m_ref, 0), get(lo_ref, 32), get(hi_ref, 32), get(m_ref, 1), get(lo_ref, 33), get(hi_ref, 33)]
    for t in range(6):
        put(w_ref, t, row(metas[t], 3))
    zi = lax.broadcasted_iota(jnp.int32, (128, 128), 0)
    for side in range(2):
        for yq in range(2):
            for col, t in enumerate((side * 3, side * 3 + 1 + yq)):
                place = metas[t][2:3, :].astype(jnp.int32) + lane[0:1, :] % 8
                base = (side * 2 + yq) * 128
                hot = jnp.where(zi == jnp.broadcast_to(place, (128, 128)), 1.0, 0.0).astype(BF16)
                s_ref[base : base + 128, col * 128 : col * 128 + 128] = hot

    def table(col, i, j):
        if col == 0:
            return get(t2_ref, i * 8 + j)
        return get(lo_ref, i * 4 + j - 4) if j >= 4 else get(hi_ref, i * 4 + j)

    zero = jnp.zeros((8, 128), F32)
    for xt in range(3):
        shift = (-12.0, 1000.0, 12.0)[xt]
        for col in range(2):
            for yq in range(2):
                b = xt * 2 + yq
                t = side_of(xt) * 3 + (0 if col == 0 else 1 + yq)
                x0 = row(metas[t], 0) - 6.0 + jnp.where(right_half, shift, 0.0)
                y0 = row(metas[t], 1) - 6.0
                if col == 1:
                    y0 = y0 + (16.0 if yq == 1 else -16.0)
                js = range(8) if col == 0 else (range(0, 4) if yq == 1 else range(4, 8))
                if col == 1 or yq == 0:
                    for a in range(4):
                        for j in js:
                            moved = zero
                            for i in range(8):
                                moved = jnp.where(x0 == float(4 * xt + a - i), table(col, i, j), moved)
                            put(tx, a * 8 + j, moved)
                for a in range(4):
                    for c in range(4):
                        rows = []
                        for h in range(2):
                            y = 8 * h + 4 * yq + c
                            moved = zero
                            if col == 0 or h == yq:
                                for j in js:
                                    moved = jnp.where(y0 == float(y - j), get(tx, a * 8 + j), moved)
                            rows.append(moved)
                        for p in range(8):
                            base = ((b * 8 + p) * 16 + a * 4 + c) * 8
                            value = jnp.where(low, row(rows[0], p), row(rows[1], p))
                            q_ref[base : base + 8, col * 128 : col * 128 + 128] = value
    partial_coeffs(y_ref, q_ref, s_ref, g_ref, z_ref, acc)
    send_coeffs(flags[0], z_ref, xe_ref, xo_ref, 0)


def fold_kernel(base, flags, z_ref, xe_ref, xo_ref, out_ref, ye_ref, yo_ref):
    _, lane = iotas()
    left_half = lane < 64
    from_x = [sides(flags[0] == 1, get(xe_ref, base + t), get(xo_ref, base + t)) for t in range(3)]
    tiles = []
    for side in range(2):
        for t in range(3):
            near, far = from_x[t][side], from_x[t][1 - side]
            tiles.append(get(z_ref, side * 3 + t) + near + jnp.where(left_half, far, 0.0))
    for t in range(6):
        put(out_ref, t, tiles[t])
    for side in range(2):
        for n, (above, below) in enumerate(((2, 1), (0, 0))):
            above, below = tiles[side * 3 + above], tiles[side * 3 + below]
            put(ye_ref, side * 2 + n, jnp.where(flags[1] == 1, below, above))
            put(yo_ref, side * 2 + n, jnp.where(flags[1] == 1, above, below))


def step_kernel(
    step, flags, y_ref, prev_ref, xe_ref, xo_ref, ye_ref, yo_ref, coef_ref, q_ref, s_ref, w_ref, z_ref, ce_ref, co_ref,
    dz_ref, g_ref, *rest
):
    last = step == STEPS
    if last:
        new_ref, ex, ey, zd, acc, wp, rims = rest
    else:
        new_ref, nxe_ref, nxo_ref, nye_ref, nyo_ref, zn_ref, ex, ey, zd, acc, wp, rims = rest
    sub, _ = iotas()
    low = sub < 4
    scale = 1.0 if step == 1 else 2.0

    high, rest_part = split(y_ref[...])
    zd[...] = mm(high, dz_ref[0:NZ, :]) + mm(rest_part, dz_ref[0:NZ, :]) + mm(high, dz_ref[NZ : 2 * NZ, :])

    take(flags[0], xe_ref, xo_ref, ex, XH * 8, 0, (XH + TILES) * 8)
    take(flags[1], ye_ref, yo_ref, rims, YH * 8, 0, YH * 8)
    ex[XH * 8 : (XH + TILES) * 8, :] = y_ref[...]
    for x in range(CX):
        for yl in range(8):
            put(ey, x * 20 + HALO + yl, get(y_ref, x * 8 + yl))
        lo_rims = [get(rims, x * 3 + m) for m in range(3)]
        hi_rims = [get(rims, YH + x * 3 + m) for m in range(3)]
        for m in range(HALO):
            rim = lo_rims[m] if m < 3 else pltpu.roll(lo_rims[m - 3], 4, 0)
            put(ey, x * 20 + m, jnp.where(low, rim, pltpu.roll(get(y_ref, x * 8 + 2 + m), 4, 0)))
            rim = pltpu.roll(hi_rims[m], 4, 0) if m < 3 else hi_rims[m - 3]
            put(ey, x * 20 + HALO + 8 + m, jnp.where(low, pltpu.roll(get(y_ref, x * 8 + m), 4, 0), rim))

    def body(x, carry):
        for yl in range(8):
            r = x * 8 + yl
            center = get_at(y_ref, r)
            gx = gy = lap = None
            for k in range(1, HALO + 1):
                xp, xm = get_at(ex, (x + HALO + k) * 8 + yl), get_at(ex, (x + HALO - k) * 8 + yl)
                yp, ym = get_at(ey, x * 20 + HALO + yl + k), get_at(ey, x * 20 + HALO + yl - k)
                tx = first_coefs[k - 1] * (xp - xm)
                ty = first_coefs[k - 1] * (yp - ym)
                tl = second_coefs[k - 1] * ((xp + xm) + (yp + ym))
                gx, gy, lap = (tx, ty, tl) if k == 1 else (gx + tx, gy + ty, lap + tl)
            at = pl.ds(pl.multiple_of(r * 8, 8), 8)
            total = get_at(coef_ref, r) * (lap + zd[at, NZ:])
            total += get_at(coef_ref, TILES + r) * gx
            total += get_at(coef_ref, 2 * TILES + r) * gy
            total += get_at(coef_ref, 3 * TILES + r) * zd[at, :NZ]
            total += get_at(coef_ref, 4 * TILES + r) * center
            new_ref[at, :] = total if step == 1 else 2.0 * total - get_at(prev_ref, r)
        return carry

    lax.fori_loop(0, CX, body, 0)

    tiles = []
    for side in range(2):
        own, lo, hi = (get(z_ref, side * 3 + t) for t in range(3))
        tiles.append(own + get(ce_ref, side * 2) + get(co_ref, side * 2))
        from_lo, from_hi = sides(flags[1] == 1, get(ce_ref, side * 2 + 1), get(co_ref, side * 2 + 1))
        tiles.append(lo + from_lo)
        tiles.append(hi + from_hi)
    weights = jnp.concatenate(tiles, axis=0) * w_ref[...] * scale
    wp[...] = pick_t(weights, g_ref[...])

    for xt in range(3):
        for yq in range(2):
            b = xt * 2 + yq
            ta, tb = side_of(xt) * 3, side_of(xt) * 3 + 1 + yq
            total = None
            for p in range(8):
                weight = jnp.concatenate(
                    [wp[t * 8 : t * 8 + 8, p * 128 : p * 128 + 128] for t in (ta, tb)], axis=1
                )
                base = (b * 8 + p) * 128
                term = weight[None] * q_ref[base : base + 128, :].reshape(16, 8, 256)
                total = term if total is None else total + term
            table = s_ref[(side_of(xt) * 2 + yq) * 128 : (side_of(xt) * 2 + yq) * 128 + 128, :]
            spread = pick_t(total.reshape(128, 256), table)
            for a, t in enumerate(block_tiles(xt, yq)):
                new_ref[t * 8 : t * 8 + 32, :] += spread[a * 32 : a * 32 + 32, :]

    if not last:
        give_ends(flags[0], new_ref, nxe_ref, nxo_ref)
        pack_rims(new_ref, rims.at[pl.ds(YH * 8, YH * 8)], rims.at[pl.ds(0, YH * 8)], low)
        rows = YH * 8
        nye_ref[...] = rims[pl.ds(pl.multiple_of(jnp.where(flags[1] == 1, 0, rows), 8), rows), :]
        nyo_ref[...] = rims[pl.ds(pl.multiple_of(jnp.where(flags[1] == 1, rows, 0), 8), rows), :]
        partial_coeffs(new_ref, q_ref, s_ref, g_ref, zn_ref, acc)
        send_coeffs(flags[0], zn_ref, nxe_ref, nxo_ref, XH)


def gram_kernel(order, a0, a1, a2, a3, out_ref, held):
    for n, ref in enumerate((a0, a1, a2, a3)):
        held[order[n]] = ref[...]

    def body(x, totals):
        at = pl.ds(pl.multiple_of(x * 64, 64), 64)
        field = jnp.concatenate([held[d, at, :] for d in range(4)], axis=0)
        high, low = split(field)
        return totals[0] + mm_t(high, high), totals[1] + mm_t(high, low)

    zero = jnp.zeros((256, 256), F32)
    total, mixed = lax.fori_loop(0, CX, body, (zero, zero))
    total = total + mixed + mixed.T
    rows = lax.broadcasted_iota(jnp.int32, (256, 256), 0)
    columns = lax.broadcasted_iota(jnp.int32, (256, 256), 1)
    total = jnp.where((rows % 64) // 4 == (columns % 64) // 4, total, 0.0)
    orbital = lax.broadcasted_iota(jnp.int32, (16, 256), 0)
    held_at = lax.broadcasted_iota(jnp.int32, (16, 256), 1)
    hot = jnp.where(orbital == held_at // 64 * 4 + held_at % 4, 1.0, 0.0).astype(F32)
    first = jnp.dot(hot, total, precision=lax.Precision.HIGHEST, preferred_element_type=F32)
    small = lax.dot_general(
        first, hot, (((1,), (1,)), ((), ())), precision=lax.Precision.HIGHEST, preferred_element_type=F32
    )
    out_ref[...] = jnp.zeros((8, 128), F32)
    out_ref[:, 0:16] = small[0:8]
    out_ref[:, 16:32] = small[8:16]


def rotate_kernel(cells, order, corr_ref, a0, a1, a2, a3, out_ref, flat):
    lane = lax.broadcasted_iota(jnp.int32, (16, 128), 1)
    rows = lax.broadcasted_iota(jnp.int32, (16, 128), 0)
    packed = corr_ref[...]
    whole = jnp.concatenate([packed, pltpu.roll(packed, 112, 1)], axis=0)
    work = jnp.where(lane < 16, whole * (1.0 / cells), jnp.where(lane == rows + 16, 1.0, 0.0))
    pivots = jnp.ones((16, 128), F32)
    for k in range(16):
        pivot_row = jnp.broadcast_to(work[k : k + 1, :], (16, 128))
        pivot = jnp.broadcast_to(pivot_row[:, k : k + 1], (16, 128))
        column = jnp.broadcast_to(work[:, k : k + 1], (16, 128))
        pivots = jnp.where(rows == k, pivot, pivots)
        work = jnp.where(rows > k, work - column / pivot * pivot_row, work)
    inverse = (work / jnp.sqrt(pivots))[:, 16:32]
    me = order[0]
    own_row = lax.broadcasted_iota(jnp.int32, (64, 16), 0)
    orbital = lax.broadcasted_iota(jnp.int32, (64, 16), 1)
    left = jnp.where(orbital == me * 4 + own_row % 4, 1.0, 0.0).astype(F32)
    orbital = lax.broadcasted_iota(jnp.int32, (16, 256), 0)
    held_at = lax.broadcasted_iota(jnp.int32, (16, 256), 1)
    device = held_at // 64
    owner = jnp.where(device == 0, order[0], jnp.where(device == 1, order[1], jnp.where(device == 2, order[2], order[3])))
    right = jnp.where(orbital == owner * 4 + held_at % 4, 1.0, 0.0).astype(F32)
    exact = functools.partial(jnp.dot, precision=lax.Precision.HIGHEST, preferred_element_type=F32)
    mixing = exact(exact(left, inverse), right)
    at_row = lax.broadcasted_iota(jnp.int32, (64, 256), 0)
    at_column = lax.broadcasted_iota(jnp.int32, (64, 256), 1)
    mixing = jnp.where(at_row // 4 == at_column % 64 // 4, mixing, 0.0)
    mix_high, mix_low = split(mixing)
    for x in range(CX):
        field = jnp.concatenate([ref[x * 64 : x * 64 + 64, :] for ref in (a0, a1, a2, a3)], axis=0)
        high, low = split(field)
        flat[x * 64 : x * 64 + 64, :] = mm(mix_high, high) + mm(mix_high, low) + mm(mix_low, high)
    for o in range(ORB):
        for x in range(CX):
            for h in range(2):
                out_ref[o, x, 8 * h : 8 * h + 8, :] = flat[pl.ds(x * 64 + 4 * h + o, 8, stride=8), :]


def kernel_call(body, outs, ins, scratch=(), name=None):
    return pl.pallas_call(
        body,
        out_shape=[jax.ShapeDtypeStruct(shape, dtype) for shape, dtype in outs],
        in_specs=ins,
        out_specs=[VMEM] * len(outs),
        scratch_shapes=list(scratch),
        compiler_params=pltpu.CompilerParams(vmem_limit_bytes=LIMIT),
        name=name,
    )


def blocks(count, columns=128, dtype=F32):
    return (count * 8, columns), dtype


def exchange(even_value, odd_value, axis):
    count = lax.axis_size(axis)
    results = []
    for first, value in ((1, odd_value), (0, even_value)):
        pairs = [p for i in range(first, count - 1, 2) for p in ((i, i + 1), (i + 1, i))]
        results.append(lax.ppermute(value, axis, pairs))
    return results[1], results[0]


def spread_sum(value, axis):
    copies = jnp.broadcast_to(value[None], (lax.axis_size(axis),) + value.shape)
    return jnp.sum(lax.all_to_all(copies, axis, 0, 0, tiled=True), axis=0)


def fold(flags, z, even, odd, tile):
    return kernel_call(
        functools.partial(fold_kernel, tile), [blocks(6), blocks(4), blocks(4)], [SMEM] + [VMEM] * 3, name="fold_coeffs"
    )(flags, z, even, odd)


def shards(orbitals, potential, kinetic_mu, projectors, strengths, box_offsets, block_counts):
    dz = jnp.asarray(derivative_table())
    flags = jnp.stack([lax.axis_index("gx") % 2, lax.axis_index("gy") % 2]).astype(jnp.int32)
    mu_blocks = 2 * HALO + 17
    y, t, meta, xe, xo, ye, yo, mu, groups = kernel_call(
        prep_kernel,
        [blocks(TILES), blocks(64), blocks(1), blocks(FIRST_X), blocks(FIRST_X), blocks(FIRST_Y), blocks(FIRST_Y)]
        + [((CX, CY, NZ), F32), ((1024, 128), BF16)],
        [SMEM] * 4 + [VMEM] * 3,
        [
            pltpu.VMEM((mu_blocks * 8, 128), F32),
            pltpu.VMEM((mu_blocks * 8, 128), F32),
            pltpu.VMEM((FIRST_Y * 8, 128), F32),
            pltpu.VMEM((FIRST_Y * 8, 128), F32),
        ],
        name="prepare",
    )(flags, box_offsets.T, strengths, block_counts, orbitals, kinetic_mu, projectors)
    xe, xo = exchange(xe, xo, "gx")
    t2, metas, ye2, yo2 = kernel_call(
        widen_kernel,
        [blocks(64), blocks(2), blocks(34), blocks(34)],
        [SMEM] + [VMEM] * 4,
        [pltpu.VMEM((17 * 8, 128), F32)] * 2 + [pltpu.VMEM((34 * 8, 128), F32)] * 2,
        name="widen",
    )(flags, t, meta, xe, xo)
    ye, yo = exchange(ye, yo, "gy")
    ye2, yo2 = exchange(ye2, yo2, "gy")
    (coefs,) = kernel_call(
        coef_kernel,
        [blocks(5 * TILES)],
        [SMEM] + [VMEM] * 7,
        [pltpu.VMEM(((TILES + 2 * XH) * 8, 128), F32), pltpu.VMEM((CX * 20 * 8, 128), F32)],
        name="coefficients",
    )(flags, mu, potential, xe, xo, ye, yo, dz)
    q, s, w, z, ce, co = kernel_call(
        build_kernel,
        [blocks(6 * 8 * 16, 256), ((4 * 128, 256), BF16), blocks(6), blocks(6), blocks(3), blocks(3)],
        [SMEM] + [VMEM] * 6,
        [
            pltpu.VMEM((32 * 8, 128), F32),
            pltpu.VMEM((48, 1024), F32),
            pltpu.VMEM((34 * 8, 128), F32),
            pltpu.VMEM((34 * 8, 128), F32),
        ],
        name="build",
    )(flags, t2, metas, ye2, yo2, y, groups)
    ce, co = exchange(ce, co, "gx")
    z, ce, co = fold(flags, z, ce, co, 0)
    ce, co = exchange(ce, co, "gy")

    previous = y
    for step in range(1, STEPS + 1):
        last = step == STEPS
        outs = [blocks(TILES)]
        if not last:
            outs += [blocks(XH + 3), blocks(XH + 3), blocks(YH), blocks(YH), blocks(6)]
        result = kernel_call(
            functools.partial(step_kernel, step),
            outs,
            [SMEM] + [VMEM] * 15,
            [
                pltpu.VMEM(((TILES + 2 * XH) * 8, 128), F32),
                pltpu.VMEM((CX * 20 * 8, 128), F32),
                pltpu.VMEM((TILES * 8, 256), F32),
                pltpu.VMEM((48, 1024), F32),
                pltpu.VMEM((48, 1024), F32),
                pltpu.VMEM((2 * YH * 8, 128), F32),
            ],
            name="step",
        )(flags, y, previous, xe, xo, ye, yo, coefs, q, s, w, z, ce, co, dz, groups)
        previous = y
        if last:
            (y,) = result
        else:
            y, xe, xo, ye, yo, z = result
            ye, yo = exchange(ye, yo, "gy")
            xe, xo = exchange(xe, xo, "gx")
            z, ce, co = fold(flags, z, xe, xo, XH)
            ce, co = exchange(ce, co, "gy")

    count = lax.axis_size("orb")
    me = lax.axis_index("orb")
    even = [(i, i ^ 1) for i in range(count)]
    odd = [(i, count - 1 - i) for i in range(count)]
    one = lax.ppermute(y, "orb", even)
    other = lax.ppermute(y, "orb", odd)
    half = TILES * 4
    across_a = lax.ppermute(one[:half], "orb", odd)
    across_b = lax.ppermute(other[half:], "orb", even)
    across = jnp.concatenate([across_a, across_b], axis=0)
    order = jnp.stack([me, me ^ 1, count - 1 - me, (me + 2) % count]).astype(jnp.int32)
    (corr,) = kernel_call(
        gram_kernel,
        [blocks(1)],
        [SMEM] + [VMEM] * 4,
        [pltpu.VMEM((4, TILES * 8, 128), F32)],
        name="gram",
    )(order, y, one, other, across)
    for axis in ("gx", "gy"):
        corr = spread_sum(corr, axis)
    cells = CX * CY * NZ * lax.axis_size("gx") * lax.axis_size("gy")
    (result,) = kernel_call(
        functools.partial(rotate_kernel, cells),
        [((ORB, CX, CY, NZ), F32)],
        [SMEM] + [VMEM] * 5,
        [pltpu.VMEM((TILES * 8, 128), F32)],
        name="rotate",
    )(order, corr, y, one, other, across)
    return result


def solution(mesh):
    in_specs = (
        P("orb", "gx", "gy", None),
        P("gx", "gy", None),
        P("gx", "gy", None),
        P(("gx", "gy"), None, None),
        P(("gx", "gy"), None),
        P(("gx", "gy"), None),
        P(("gx", "gy")),
    )
    out_specs = P("orb", "gx", "gy", None)
    return jax.shard_map(shards, mesh=mesh, in_specs=in_specs, out_specs=out_specs, check_vma=False)
```

```python
import functools

import jax
import jax.numpy as jnp
import ml_dtypes
import numpy as np
from jax import lax
from jax.experimental import pallas as pl
from jax.experimental.pallas import tpu as pltpu
from jax.sharding import PartitionSpec as P

CX, CY, NZ, ORB = 12, 16, 128, 4
HALO = 6
TILES = 96
XH = HALO * 8
YH = CX * 3
STEPS = 3

first_coefs = (6.0 / 7.0, -15.0 / 56.0, 5.0 / 63.0, -1.0 / 56.0, 2.0 / 825.0, -1.0 / 5544.0)
second_coefs = (12.0 / 7.0, -15.0 / 56.0, 10.0 / 189.0, -1.0 / 112.0, 2.0 / 1925.0, -1.0 / 16632.0)
center_coef = -5369.0 / 1800.0
filter_center = 13.5
filter_half = 10.5

F32, BF16 = jnp.float32, jnp.bfloat16
VMEM = pl.BlockSpec(memory_space=pltpu.VMEM)
SMEM = pl.BlockSpec(memory_space=pltpu.SMEM)
LIMIT = 24 * 1024 * 1024


def derivative_table():
    table = np.zeros((NZ, 2 * NZ), np.float64)
    for z in range(NZ):
        table[z, NZ + z] = 3.0 * center_coef
        for k in range(1, HALO + 1):
            if z + k < NZ:
                table[z + k, z] = first_coefs[k - 1]
                table[z + k, NZ + z] = second_coefs[k - 1]
            if z - k >= 0:
                table[z - k, z] = -first_coefs[k - 1]
                table[z - k, NZ + z] = second_coefs[k - 1]
    high = table.astype(ml_dtypes.bfloat16)
    low = (table - high.astype(np.float64)).astype(ml_dtypes.bfloat16)
    return np.concatenate([high, low], axis=0)


def split(a):
    high = a.astype(BF16)
    return high, (a - high.astype(F32)).astype(BF16)


def mm(a, b):
    return jnp.dot(a, b, preferred_element_type=F32)


def mm_t(a, b):
    return lax.dot_general(a, b, (((1,), (1,)), ((), ())), preferred_element_type=F32)


def pick(a, table):
    high, low = split(a)
    return mm(high, table) + mm(low, table)


def pick_t(a, table):
    high, low = split(a)
    return mm_t(high, table) + mm_t(low, table)


def get(ref, tile):
    return ref[pl.ds(tile * 8, 8), :]


def put(ref, tile, value):
    ref[pl.ds(tile * 8, 8), :] = value


def get_at(ref, tile):
    return ref[pl.ds(pl.multiple_of(tile * 8, 8), 8), :]


def iotas():
    return (
        lax.broadcasted_iota(jnp.int32, (8, 128), 0),
        lax.broadcasted_iota(jnp.int32, (8, 128), 1),
    )


def row(value, index):
    return jnp.broadcast_to(value[index : index + 1, :], (8, 128))


def pack_rims(y_ref, hi_ref, lo_ref, low):
    for x in range(CX):
        for m in range(3):
            put(hi_ref, x * 3 + m, jnp.where(low, pltpu.roll(get(y_ref, x * 8 + 2 + m), 4, 0), get(y_ref, x * 8 + 5 + m)))
            put(lo_ref, x * 3 + m, jnp.where(low, get(y_ref, x * 8 + m), pltpu.roll(get(y_ref, x * 8 + 3 + m), 4, 0)))


def sides(odd, even_op, odd_op):
    return jnp.where(odd, even_op, odd_op), jnp.where(odd, odd_op, even_op)


def send(flag, below, above, even_ref, odd_ref, tiles, base=0):
    even_from = jnp.where(flag == 1, 0, 1)
    for t in range(tiles):
        one, two = get(below, t), get(above, t)
        put(even_ref, base + t, jnp.where(even_from == 0, one, two))
        put(odd_ref, base + t, jnp.where(even_from == 0, two, one))


def take(flag, even_ref, odd_ref, target, rows, low_at, high_at):
    even_at = pl.multiple_of(jnp.where(flag == 1, low_at, high_at), 8)
    odd_at = pl.multiple_of(jnp.where(flag == 1, high_at, low_at), 8)
    target[pl.ds(even_at, rows), :] = even_ref[0:rows, :]
    target[pl.ds(odd_at, rows), :] = odd_ref[0:rows, :]


def give_ends(flag, y_ref, even_ref, odd_ref):
    rows = XH * 8
    even_at = pl.multiple_of(jnp.where(flag == 1, 0, rows), 8)
    odd_at = pl.multiple_of(jnp.where(flag == 1, rows, 0), 8)
    even_ref[0:rows, :] = y_ref[pl.ds(even_at, rows), :]
    odd_ref[0:rows, :] = y_ref[pl.ds(odd_at, rows), :]


def prep_slots_kernel(flags, offs, strg, cnt, proj, t_ref, meta_ref, xe_ref, xo_ref, g_ref, xr_ref, xl_ref):
    at_row = lax.broadcasted_iota(jnp.int32, (1024, 128), 0)
    at_column = lax.broadcasted_iota(jnp.int32, (1024, 128), 1)
    same = (at_row % 128 // 8 == at_column // 8) & (at_row // 128 == at_column % 8)
    g_ref[...] = jnp.where(same, 1.0, 0.0).astype(BF16)
    sub, lane = iotas()
    left_half = lane < 64
    group = lane // 8
    meta = jnp.zeros((8, 128), F32)
    for s in range(8):
        for column in range(3):
            value = offs[column, s].astype(F32)
            meta = jnp.where((group == s) & (sub == column), value, meta)
        alive = jnp.where(s < cnt[0], 1.0, 0.0).astype(F32)
        for p in range(8):
            weight = strg[s, p] * alive * (1.0 / (512.0 * filter_half))
            meta = jnp.where((lane == s * 8 + p) & (sub == 3), weight, meta)
    meta_ref[...] = meta
    for i in range(8):
        for j in range(8):
            start = (i % 2) * 64 + j * 8
            total = jnp.zeros((8, 128), F32)
            for s in range(8):
                source = proj[s, :, 128 * (i // 2) : 128 * (i // 2) + 128]
                shift = (s * 8 - start) % 128
                moved = pltpu.roll(source, shift, 1) if shift else source
                total = jnp.where(group == s, moved, total)
            put(t_ref, i * 8 + j, total)
    for i in range(2):
        for j in range(8):
            for ref, first in ((xr_ref, 4), (xl_ref, 0)):
                one = get(t_ref, (first + i) * 8 + j)
                two = pltpu.roll(get(t_ref, (first + 2 + i) * 8 + j), 64, 1)
                put(ref, i * 8 + j, jnp.where(left_half, one, two))
    put(xr_ref, 16, meta)
    put(xl_ref, 16, meta)
    send(flags[0], xl_ref, xr_ref, xe_ref, xo_ref, 17)


def prep_fields_kernel(orb, mu, pot, y_ref, mu_out, pot_out):
    mu_out[...] = mu[...]
    pot_out[...] = pot[...]
    for x in range(CX):
        for o in range(ORB):
            for h in range(2):
                y_ref[pl.ds(x * 64 + 4 * h + o, 8, stride=8), :] = orb[o, x, 8 * h : 8 * h + 8, :]


X_SUMS, Y_SUMS = XH, YH
X_MU, Y_MU = XH + 3, YH + 4
X_ALL, Y_ALL = X_MU + 2 * HALO, Y_MU + CX


def send_rims(flag, y_ref, rims, ye_ref, yo_ref):
    low = iotas()[0] < 4
    rows = YH * 8
    pack_rims(y_ref, rims.at[pl.ds(rows, rows)], rims.at[pl.ds(0, rows)], low)
    ye_ref[0:rows, :] = rims[pl.ds(pl.multiple_of(jnp.where(flag == 1, 0, rows), 8), rows), :]
    yo_ref[0:rows, :] = rims[pl.ds(pl.multiple_of(jnp.where(flag == 1, rows, 0), 8), rows), :]


def widen_kernel(flags, t_ref, meta_ref, xe_ref, xo_ref, t2_ref, m_ref, ye_ref, yo_ref, fl_ref, fr_ref, hi_ref, lo_ref):
    _, lane = iotas()
    left_half = lane < 64
    base = 0
    for t in range(17):
        left, right = sides(flags[0] == 1, get(xe_ref, t), get(xo_ref, t))
        put(fl_ref, t, left)
        put(fr_ref, t, right)
    for i in range(8):
        for j in range(8):
            if i >= 4:
                other = get(fl_ref, base + (i % 2) * 8 + j)
                other = other if i >= 6 else pltpu.roll(other, 64, 1)
            else:
                other = get(fr_ref, base + (i % 2) * 8 + j)
                other = other if i >= 2 else pltpu.roll(other, 64, 1)
            both = jnp.where(left_half, get(t_ref, i * 8 + j), other)
            put(t2_ref, i * 8 + j, both)
            if j >= 4:
                put(hi_ref, i * 4 + j - 4, both)
            else:
                put(lo_ref, i * 4 + j, both)
    meta = meta_ref[...]
    for side, ref in enumerate((fl_ref, fr_ref)):
        both = jnp.where(left_half, meta, pltpu.roll(get(ref, base + 16), 64, 1))
        put(m_ref, side, both)
        put(hi_ref, 32 + side, both)
        put(lo_ref, 32 + side, both)
    send(flags[1], lo_ref, hi_ref, ye_ref, yo_ref, 34)


def coef_kernel(flags, mu, pot, xe_ref, xo_ref, ye_ref, yo_ref, dz_ref, out_ref, ex, ey):
    sub, _ = iotas()
    low = sub < 4

    def two(a, ia, b, ib):
        return jnp.where(low, row(a, ia), row(b, ib))

    ends = [sides(flags[0] == 1, get(xe_ref, X_MU + t), get(xo_ref, X_MU + t)) for t in range(2 * HALO)]
    for x in range(CX + 2 * HALO):
        if x < HALO:
            a, b = ends[2 * x][0], ends[2 * x + 1][0]
        elif x < HALO + CX:
            a, b = mu[x - HALO, 0:8, :], mu[x - HALO, 8:16, :]
        else:
            a, b = ends[2 * (x - HALO - CX)][1], ends[2 * (x - HALO - CX) + 1][1]
        for yl in range(8):
            put(ex, x * 8 + yl, two(a, yl, b, yl))
    for x in range(CX):
        lo_rim, hi_rim = sides(flags[1] == 1, get(ye_ref, Y_MU + x), get(yo_ref, Y_MU + x))
        parts = [lo_rim, mu[x, 0:8, :], mu[x, 8:16, :], hi_rim]
        for n in range(20):
            y = n - HALO
            put(ey, x * 20 + n, two(parts[(y + 8) // 8], y % 8, parts[(y + 16) // 8], y % 8))
    field = ex[XH * 8 : (XH + TILES) * 8, :]
    high, rest = split(field)
    zd = mm(high, dz_ref[0:NZ, 0:NZ]) + mm(rest, dz_ref[0:NZ, 0:NZ]) + mm(high, dz_ref[NZ : 2 * NZ, 0:NZ])
    out_ref[3 * 768 : 4 * 768, :] = zd * (-0.5 / filter_half)

    def body(x, carry):
        va, vb = pot[x, 0:8, :], pot[x, 8:16, :]
        for yl in range(8):
            gx = jnp.zeros((8, 128), F32)
            gy = jnp.zeros((8, 128), F32)
            for k in range(1, HALO + 1):
                gx += first_coefs[k - 1] * (get_at(ex, (x + HALO + k) * 8 + yl) - get_at(ex, (x + HALO - k) * 8 + yl))
                gy += first_coefs[k - 1] * (
                    get_at(ey, x * 20 + HALO + yl + k) - get_at(ey, x * 20 + HALO + yl - k)
                )
            r = x * 8 + yl
            center = get_at(ex, (x + HALO) * 8 + yl)

            def store(which, value):
                out_ref[pl.ds(pl.multiple_of((which * TILES + r) * 8, 8), 8), :] = value

            store(0, (1.0 + center) * (-0.5 / filter_half))
            store(1, gx * (-0.5 / filter_half))
            store(2, gy * (-0.5 / filter_half))
            store(4, (two(va, yl, vb, yl) - filter_center) * (1.0 / filter_half))
        return carry

    lax.fori_loop(0, CX, body, 0)


def block_tiles(xt, yq):
    return [(4 * xt + a) * 8 + 4 * yq for a in range(4)]


def side_of(xt):
    return 1 if xt == 2 else 0


def partial_coeffs(y_ref, q_ref, s_ref, g_ref, z_ref, acc):
    left_half = lax.broadcasted_iota(jnp.int32, (8, 1024), 1) % 128 < 64
    own = None
    ends = {}
    rims = [None, None]
    corners = {}
    for xt in range(3):
        for yq in range(2):
            b = xt * 2 + yq
            field = jnp.concatenate([y_ref[t * 8 : t * 8 + 32, :] for t in block_tiles(xt, yq)], axis=0)
            table = s_ref[(side_of(xt) * 2 + yq) * 128 : (side_of(xt) * 2 + yq) * 128 + 128, :]
            seen = pick(field, table).reshape(16, 8, 256)
            sums = []
            for p in range(8):
                base = (b * 8 + p) * 128
                product = seen * q_ref[base : base + 128, :].reshape(16, 8, 256)
                total = jnp.sum(product, axis=0)
                sums.append(total + pltpu.roll(total, 4, 0))
            col_a = jnp.concatenate([t[:, :128] for t in sums], axis=1)
            col_b = jnp.concatenate([t[:, 128:] for t in sums], axis=1)
            own = col_a if own is None else own + col_a
            rims[yq] = col_b if rims[yq] is None else rims[yq] + col_b
            if xt != 1:
                ends[xt] = ends[xt] + col_a if xt in ends else col_a
                corners[(xt, yq)] = col_b
    for side, xt in enumerate((0, 2)):
        acc[side * 24 : side * 24 + 8, :] = jnp.where(left_half, own, ends[xt])
        for yq in range(2):
            at = side * 24 + 8 + yq * 8
            acc[at : at + 8, :] = jnp.where(left_half, rims[yq], corners[(xt, yq)])
    z_ref[...] = pick(acc[...], g_ref[...])


def send_coeffs(flag, z_ref, ye_ref, yo_ref, base):
    for side in range(2):
        for n, (above, below) in enumerate(((2, 1), (0, 0))):
            above, below = get(z_ref, side * 3 + above), get(z_ref, side * 3 + below)
            put(ye_ref, base + side * 2 + n, jnp.where(flag == 1, below, above))
            put(yo_ref, base + side * 2 + n, jnp.where(flag == 1, above, below))


def build_kernel(
    flags, t2_ref, m_ref, ye_ref, yo_ref, y_ref, mu, g_ref,
    q_ref, s_ref, w_ref, z_ref, nye_ref, nyo_ref, tx, acc, lo_ref, hi_ref, rims
):
    for t in range(34):
        lo, hi = sides(flags[1] == 1, get(ye_ref, t), get(yo_ref, t))
        put(lo_ref, t, lo)
        put(hi_ref, t, hi)
    sub, lane = iotas()
    low = sub < 4
    right_half = lane >= 64
    metas = [get(m_ref, 0), get(lo_ref, 32), get(hi_ref, 32), get(m_ref, 1), get(lo_ref, 33), get(hi_ref, 33)]
    for t in range(6):
        put(w_ref, t, row(metas[t], 3))
    zi = lax.broadcasted_iota(jnp.int32, (128, 128), 0)
    for side in range(2):
        for yq in range(2):
            for col, t in enumerate((side * 3, side * 3 + 1 + yq)):
                place = metas[t][2:3, :].astype(jnp.int32) + lane[0:1, :] % 8
                base = (side * 2 + yq) * 128
                hot = jnp.where(zi == jnp.broadcast_to(place, (128, 128)), 1.0, 0.0).astype(BF16)
                s_ref[base : base + 128, col * 128 : col * 128 + 128] = hot

    def table(col, i, j):
        if col == 0:
            return get(t2_ref, i * 8 + j)
        return get(lo_ref, i * 4 + j - 4) if j >= 4 else get(hi_ref, i * 4 + j)

    zero = jnp.zeros((8, 128), F32)
    for xt in range(3):
        shift = (-12.0, 1000.0, 12.0)[xt]
        for col in range(2):
            for yq in range(2):
                b = xt * 2 + yq
                t = side_of(xt) * 3 + (0 if col == 0 else 1 + yq)
                x0 = row(metas[t], 0) - 6.0 + jnp.where(right_half, shift, 0.0)
                y0 = row(metas[t], 1) - 6.0
                if col == 1:
                    y0 = y0 + (16.0 if yq == 1 else -16.0)
                js = range(8) if col == 0 else (range(0, 4) if yq == 1 else range(4, 8))
                if col == 1 or yq == 0:
                    for a in range(4):
                        for j in js:
                            moved = zero
                            for i in range(8):
                                moved = jnp.where(x0 == float(4 * xt + a - i), table(col, i, j), moved)
                            put(tx, a * 8 + j, moved)
                for a in range(4):
                    for c in range(4):
                        rows = []
                        for h in range(2):
                            y = 8 * h + 4 * yq + c
                            moved = zero
                            if col == 0 or h == yq:
                                for j in js:
                                    moved = jnp.where(y0 == float(y - j), get(tx, a * 8 + j), moved)
                            rows.append(moved)
                        for p in range(8):
                            base = ((b * 8 + p) * 16 + a * 4 + c) * 8
                            value = jnp.where(low, row(rows[0], p), row(rows[1], p))
                            q_ref[base : base + 8, col * 128 : col * 128 + 128] = value
    partial_coeffs(y_ref, q_ref, s_ref, g_ref, z_ref, acc)
    send_coeffs(flags[1], z_ref, nye_ref, nyo_ref, Y_SUMS)
    send_rims(flags[1], y_ref, rims, nye_ref, nyo_ref)
    for x in range(CX):
        below, above = mu[x, 0:8, :], mu[x, 8:16, :]
        put(nye_ref, Y_MU + x, jnp.where(flags[1] == 1, below, above))
        put(nyo_ref, Y_MU + x, jnp.where(flags[1] == 1, above, below))


def fold_kernel(flags, z_ref, y_ref, ye_ref, yo_ref, *rest):
    out_ref, xe_ref, xo_ref = rest[-3:]
    give_ends(flags[0], y_ref, xe_ref, xo_ref)
    if len(rest) == 4:
        mu = rest[0]
        for x in range(HALO):
            for h in range(2):
                left, right = mu[x, 8 * h : 8 * h + 8, :], mu[CX - HALO + x, 8 * h : 8 * h + 8, :]
                put(xe_ref, X_MU + 2 * x + h, jnp.where(flags[0] == 1, left, right))
                put(xo_ref, X_MU + 2 * x + h, jnp.where(flags[0] == 1, right, left))
    base = Y_SUMS
    for side in range(2):
        own, lo, hi = (get(z_ref, side * 3 + t) for t in range(3))
        across = [(get(ye_ref, base + side * 2 + n), get(yo_ref, base + side * 2 + n)) for n in range(2)]
        from_lo, from_hi = sides(flags[1] == 1, *across[1])
        put(out_ref, side * 3, own + across[0][0] + across[0][1])
        put(out_ref, side * 3 + 1, lo + from_lo)
        put(out_ref, side * 3 + 2, hi + from_hi)
    for t in range(3):
        left, right = pltpu.roll(get(out_ref, t), 64, 1), pltpu.roll(get(out_ref, 3 + t), 64, 1)
        put(xe_ref, X_SUMS + t, jnp.where(flags[0] == 1, left, right))
        put(xo_ref, X_SUMS + t, jnp.where(flags[0] == 1, right, left))


def step_kernel(
    step, flags, y_ref, prev_ref, xe_ref, xo_ref, ye_ref, yo_ref, coef_ref, q_ref, s_ref, w_ref, z_ref,
    dz_ref, g_ref, *rest
):
    last = step == STEPS
    if last:
        first_ref, second_ref, ex, ey, zd, wp, rims, new_ref = rest
    else:
        new_ref, nye_ref, nyo_ref, zn_ref, ex, ey, zd, wp, rims, acc = rest
    sub, lane = iotas()
    low = sub < 4
    scale = 1.0 if step == 1 else 2.0

    high, rest_part = split(y_ref[...])
    zd[...] = mm(high, dz_ref[0:NZ, :]) + mm(rest_part, dz_ref[0:NZ, :]) + mm(high, dz_ref[NZ : 2 * NZ, :])

    take(flags[0], xe_ref, xo_ref, ex, XH * 8, 0, (XH + TILES) * 8)
    take(flags[1], ye_ref, yo_ref, rims, YH * 8, 0, YH * 8)
    ex[XH * 8 : (XH + TILES) * 8, :] = y_ref[...]
    for x in range(CX):
        for yl in range(8):
            put(ey, x * 20 + HALO + yl, get(y_ref, x * 8 + yl))
        lo_rims = [get(rims, x * 3 + m) for m in range(3)]
        hi_rims = [get(rims, YH + x * 3 + m) for m in range(3)]
        for m in range(HALO):
            rim = lo_rims[m] if m < 3 else pltpu.roll(lo_rims[m - 3], 4, 0)
            put(ey, x * 20 + m, jnp.where(low, rim, pltpu.roll(get(y_ref, x * 8 + 2 + m), 4, 0)))
            rim = pltpu.roll(hi_rims[m], 4, 0) if m < 3 else hi_rims[m - 3]
            put(ey, x * 20 + HALO + 8 + m, jnp.where(low, pltpu.roll(get(y_ref, x * 8 + m), 4, 0), rim))

    def body(x, carry):
        for yl in range(8):
            r = x * 8 + yl
            center = get_at(y_ref, r)
            gx = gy = lap = None
            for k in range(1, HALO + 1):
                xp, xm = get_at(ex, (x + HALO + k) * 8 + yl), get_at(ex, (x + HALO - k) * 8 + yl)
                yp, ym = get_at(ey, x * 20 + HALO + yl + k), get_at(ey, x * 20 + HALO + yl - k)
                tx = first_coefs[k - 1] * (xp - xm)
                ty = first_coefs[k - 1] * (yp - ym)
                tl = second_coefs[k - 1] * ((xp + xm) + (yp + ym))
                gx, gy, lap = (tx, ty, tl) if k == 1 else (gx + tx, gy + ty, lap + tl)
            at = pl.ds(pl.multiple_of(r * 8, 8), 8)
            total = get_at(coef_ref, r) * (lap + zd[at, NZ:])
            total += get_at(coef_ref, TILES + r) * gx
            total += get_at(coef_ref, 2 * TILES + r) * gy
            total += get_at(coef_ref, 3 * TILES + r) * zd[at, :NZ]
            total += get_at(coef_ref, 4 * TILES + r) * center
            new_ref[at, :] = total if step == 1 else 2.0 * total - get_at(prev_ref, r)
        return carry

    lax.fori_loop(0, CX, body, 0)

    left_half = lane < 64
    from_x = [sides(flags[0] == 1, get(xe_ref, X_SUMS + t), get(xo_ref, X_SUMS + t)) for t in range(3)]
    tiles = []
    for side in range(2):
        for t in range(3):
            near, far = from_x[t][side], from_x[t][1 - side]
            tiles.append(get(z_ref, side * 3 + t) + near + jnp.where(left_half, far, 0.0))
    weights = jnp.concatenate(tiles, axis=0) * w_ref[...] * scale
    wp[...] = pick_t(weights, g_ref[...])

    for xt in range(3):
        for yq in range(2):
            b = xt * 2 + yq
            ta, tb = side_of(xt) * 3, side_of(xt) * 3 + 1 + yq
            total = None
            for p in range(8):
                weight = jnp.concatenate(
                    [wp[t * 8 : t * 8 + 8, p * 128 : p * 128 + 128] for t in (ta, tb)], axis=1
                )
                base = (b * 8 + p) * 128
                term = weight[None] * q_ref[base : base + 128, :].reshape(16, 8, 256)
                total = term if total is None else total + term
            table = s_ref[(side_of(xt) * 2 + yq) * 128 : (side_of(xt) * 2 + yq) * 128 + 128, :]
            spread = pick_t(total.reshape(128, 256), table)
            for a, t in enumerate(block_tiles(xt, yq)):
                new_ref[t * 8 : t * 8 + 32, :] += spread[a * 32 : a * 32 + 32, :]

    if last:
        half = TILES * 4
        first_ref[...] = new_ref[0:half, :]
        second_ref[...] = new_ref[half : 2 * half, :]
    else:
        send_rims(flags[1], new_ref, rims, nye_ref, nyo_ref)
        partial_coeffs(new_ref, q_ref, s_ref, g_ref, zn_ref, acc)
        send_coeffs(flags[1], zn_ref, nye_ref, nyo_ref, Y_SUMS)


def gram_kernel(order, *refs):
    out_ref, held = refs[8:]
    for n in range(4):
        for h in range(2):
            held[order[n], h * TILES * 4 : (h + 1) * TILES * 4, :] = refs[2 * n + h][...]

    def body(x, totals):
        at = pl.ds(pl.multiple_of(x * 64, 64), 64)
        field = jnp.concatenate([held[d, at, :] for d in range(4)], axis=0)
        high, low = split(field)
        return totals[0] + mm_t(high, high), totals[1] + mm_t(high, low)

    zero = jnp.zeros((256, 256), F32)
    total, mixed = lax.fori_loop(0, CX, body, (zero, zero))
    total = total + mixed + mixed.T
    rows = lax.broadcasted_iota(jnp.int32, (256, 256), 0)
    columns = lax.broadcasted_iota(jnp.int32, (256, 256), 1)
    total = jnp.where((rows % 64) // 4 == (columns % 64) // 4, total, 0.0)
    orbital = lax.broadcasted_iota(jnp.int32, (16, 256), 0)
    held_at = lax.broadcasted_iota(jnp.int32, (16, 256), 1)
    hot = jnp.where(orbital == held_at // 64 * 4 + held_at % 4, 1.0, 0.0).astype(F32)
    first = jnp.dot(hot, total, precision=lax.Precision.HIGHEST, preferred_element_type=F32)
    small = lax.dot_general(
        first, hot, (((1,), (1,)), ((), ())), precision=lax.Precision.HIGHEST, preferred_element_type=F32
    )
    out_ref[...] = jnp.zeros((8, 128), F32)
    out_ref[:, 0:16] = small[0:8]
    out_ref[:, 16:32] = small[8:16]


def rotate_kernel(cells, order, corr_ref, *refs):
    out_ref, flat = refs[8:]
    lane = lax.broadcasted_iota(jnp.int32, (16, 128), 1)
    rows = lax.broadcasted_iota(jnp.int32, (16, 128), 0)
    packed = corr_ref[...]
    whole = jnp.concatenate([packed, pltpu.roll(packed, 112, 1)], axis=0)
    work = jnp.where(lane < 16, whole * (1.0 / cells), jnp.where(lane == rows + 16, 1.0, 0.0))
    pivots = jnp.ones((16, 128), F32)
    for k in range(16):
        pivot_row = jnp.broadcast_to(work[k : k + 1, :], (16, 128))
        pivot = jnp.broadcast_to(pivot_row[:, k : k + 1], (16, 128))
        column = jnp.broadcast_to(work[:, k : k + 1], (16, 128))
        pivots = jnp.where(rows == k, pivot, pivots)
        work = jnp.where(rows > k, work - column / pivot * pivot_row, work)
    inverse = (work / jnp.sqrt(pivots))[:, 16:32]
    me = order[0]
    own_row = lax.broadcasted_iota(jnp.int32, (64, 16), 0)
    orbital = lax.broadcasted_iota(jnp.int32, (64, 16), 1)
    left = jnp.where(orbital == me * 4 + own_row % 4, 1.0, 0.0).astype(F32)
    orbital = lax.broadcasted_iota(jnp.int32, (16, 256), 0)
    held_at = lax.broadcasted_iota(jnp.int32, (16, 256), 1)
    device = held_at // 64
    owner = jnp.where(device == 0, order[0], jnp.where(device == 1, order[1], jnp.where(device == 2, order[2], order[3])))
    right = jnp.where(orbital == owner * 4 + held_at % 4, 1.0, 0.0).astype(F32)
    exact = functools.partial(jnp.dot, precision=lax.Precision.HIGHEST, preferred_element_type=F32)
    mixing = exact(exact(left, inverse), right)
    at_row = lax.broadcasted_iota(jnp.int32, (64, 256), 0)
    at_column = lax.broadcasted_iota(jnp.int32, (64, 256), 1)
    mixing = jnp.where(at_row // 4 == at_column % 64 // 4, mixing, 0.0)
    mix_high, mix_low = split(mixing)
    for x in range(CX):
        at = x % (CX // 2) * 64
        field = jnp.concatenate([refs[2 * n + x // (CX // 2)][at : at + 64, :] for n in range(4)], axis=0)
        high, low = split(field)
        flat[x * 64 : x * 64 + 64, :] = mm(mix_high, high) + mm(mix_high, low) + mm(mix_low, high)
    for o in range(ORB):
        for x in range(CX):
            for h in range(2):
                out_ref[o, x, 8 * h : 8 * h + 8, :] = flat[pl.ds(x * 64 + 4 * h + o, 8, stride=8), :]


def kernel_call(body, outs, ins, scratch=(), name=None):
    return pl.pallas_call(
        body,
        out_shape=[jax.ShapeDtypeStruct(shape, dtype) for shape, dtype in outs],
        in_specs=ins,
        out_specs=[VMEM] * len(outs),
        scratch_shapes=list(scratch),
        compiler_params=pltpu.CompilerParams(vmem_limit_bytes=LIMIT),
        name=name,
    )


def blocks(count, columns=128, dtype=F32):
    return (count * 8, columns), dtype


def exchange(even_value, odd_value, axis):
    count = lax.axis_size(axis)
    results = []
    for first, value in ((1, odd_value), (0, even_value)):
        pairs = [p for i in range(first, count - 1, 2) for p in ((i, i + 1), (i + 1, i))]
        results.append(lax.ppermute(value, axis, pairs))
    return results[1], results[0]


def spread_sum(value, axis):
    copies = jnp.broadcast_to(value[None], (lax.axis_size(axis),) + value.shape)
    return jnp.sum(lax.all_to_all(copies, axis, 0, 0, tiled=True), axis=0)


def fold(flags, z, y, even, odd, *mu):
    count = X_ALL if mu else X_MU
    return kernel_call(
        fold_kernel, [blocks(6), blocks(count), blocks(count)], [SMEM] + [VMEM] * (4 + len(mu)), name="fold_coeffs"
    )(flags, z, y, even, odd, *mu)


def shards(orbitals, potential, kinetic_mu, projectors, strengths, box_offsets, block_counts):
    dz = jnp.asarray(derivative_table())
    flags = jnp.stack([lax.axis_index("gx") % 2, lax.axis_index("gy") % 2]).astype(jnp.int32)
    t, meta, xte, xto, groups = kernel_call(
        prep_slots_kernel,
        [blocks(64), blocks(1), blocks(17), blocks(17), ((1024, 128), BF16)],
        [SMEM] * 4 + [VMEM],
        [pltpu.VMEM((17 * 8, 128), F32)] * 2,
        name="prepare_slots",
    )(flags, box_offsets.T, strengths, block_counts, projectors)
    orbitals, xte, xto = lax.optimization_barrier((orbitals, xte, xto))
    xte, xto = exchange(xte, xto, "gx")
    y, mu, pot = kernel_call(
        prep_fields_kernel,
        [blocks(TILES), ((CX, CY, NZ), F32), ((CX, CY, NZ), F32)],
        [VMEM] * 3,
        name="prepare_fields",
    )(orbitals, kinetic_mu, potential)
    t2, metas, ye2, yo2 = kernel_call(
        widen_kernel,
        [blocks(64), blocks(2), blocks(34), blocks(34)],
        [SMEM] + [VMEM] * 4,
        [pltpu.VMEM((17 * 8, 128), F32)] * 2 + [pltpu.VMEM((34 * 8, 128), F32)] * 2,
        name="widen",
    )(flags, t, meta, xte, xto)
    ye2, yo2 = exchange(ye2, yo2, "gy")
    q, s, w, z, ye, yo = kernel_call(
        build_kernel,
        [blocks(6 * 8 * 16, 256), ((4 * 128, 256), BF16), blocks(6), blocks(6), blocks(Y_ALL), blocks(Y_ALL)],
        [SMEM] + [VMEM] * 7,
        [
            pltpu.VMEM((32 * 8, 128), F32),
            pltpu.VMEM((48, 1024), F32),
            pltpu.VMEM((34 * 8, 128), F32),
            pltpu.VMEM((34 * 8, 128), F32),
            pltpu.VMEM((2 * YH * 8, 128), F32),
        ],
        name="build",
    )(flags, t2, metas, ye2, yo2, y, mu, groups)
    ye, yo = exchange(ye, yo, "gy")
    z, xe, xo = fold(flags, z, y, ye, yo, mu)
    xe, xo = exchange(xe, xo, "gx")
    (coefs,) = kernel_call(
        coef_kernel,
        [blocks(5 * TILES)],
        [SMEM] + [VMEM] * 7,
        [pltpu.VMEM(((TILES + 2 * XH) * 8, 128), F32), pltpu.VMEM((CX * 20 * 8, 128), F32)],
        name="coefficients",
    )(flags, mu, pot, xe, xo, ye, yo, dz)

    previous = y
    for step in range(1, STEPS + 1):
        last = step == STEPS
        if last:
            outs = [blocks(TILES // 2), blocks(TILES // 2)]
        else:
            outs = [blocks(TILES), blocks(Y_MU), blocks(Y_MU), blocks(6)]
        result = kernel_call(
            functools.partial(step_kernel, step),
            outs,
            [SMEM] + [VMEM] * 13,
            [
                pltpu.VMEM(((TILES + 2 * XH) * 8, 128), F32),
                pltpu.VMEM((CX * 20 * 8, 128), F32),
                pltpu.VMEM((TILES * 8, 256), F32),
                pltpu.VMEM((48, 1024), F32),
                pltpu.VMEM((2 * YH * 8, 128), F32),
                pltpu.VMEM((TILES * 8, 128) if last else (48, 1024), F32),
            ],
            name="step",
        )(flags, y, previous, xe, xo, ye, yo, coefs, q, s, w, z, dz, groups)
        previous = y
        if not last:
            y, ye, yo, z = result
            ye, yo = exchange(ye, yo, "gy")
            z, xe, xo = fold(flags, z, y, ye, yo)
            xe, xo = exchange(xe, xo, "gx")

    count = lax.axis_size("orb")
    me = lax.axis_index("orb")
    even = [(i, i ^ 1) for i in range(count)]
    odd = [(i, count - 1 - i) for i in range(count)]
    parts = result
    one_a, other_b = lax.ppermute(parts[0], "orb", even), lax.ppermute(parts[1], "orb", odd)
    one_b, other_a = lax.ppermute(parts[1], "orb", even), lax.ppermute(parts[0], "orb", odd)
    across_a, across_b = lax.ppermute(one_a, "orb", odd), lax.ppermute(other_b, "orb", even)
    gathered = (parts[0], parts[1], one_a, one_b, other_a, other_b, across_a, across_b)
    order = jnp.stack([me, me ^ 1, count - 1 - me, (me + 2) % count]).astype(jnp.int32)
    (corr,) = kernel_call(
        gram_kernel,
        [blocks(1)],
        [SMEM] + [VMEM] * 8,
        [pltpu.VMEM((4, TILES * 8, 128), F32)],
        name="gram",
    )(order, *gathered)
    for axis in ("gx", "gy"):
        corr = spread_sum(corr, axis)
    cells = CX * CY * NZ * lax.axis_size("gx") * lax.axis_size("gy")
    (result,) = kernel_call(
        functools.partial(rotate_kernel, cells),
        [((ORB, CX, CY, NZ), F32)],
        [SMEM] + [VMEM] * 9,
        [pltpu.VMEM((TILES * 8, 128), F32)],
        name="rotate",
    )(order, corr, *gathered)
    return result


def solution(mesh):
    in_specs = (
        P("orb", "gx", "gy", None),
        P("gx", "gy", None),
        P("gx", "gy", None),
        P(("gx", "gy"), None, None),
        P(("gx", "gy"), None),
        P(("gx", "gy"), None),
        P(("gx", "gy")),
    )
    out_specs = P("orb", "gx", "gy", None)
    return jax.shard_map(shards, mesh=mesh, in_specs=in_specs, out_specs=out_specs, check_vma=False)
```

```python
import functools

import jax
import jax.numpy as jnp
import ml_dtypes
import numpy as np
from jax import lax
from jax.experimental import pallas as pl
from jax.experimental.pallas import tpu as pltpu
from jax.sharding import PartitionSpec as P

CX, CY, NZ, ORB = 12, 16, 128, 4
HALO = 6
TILES = 96
XH = HALO * 8
YH = CX * 3
STEPS = 3

first_coefs = (6.0 / 7.0, -15.0 / 56.0, 5.0 / 63.0, -1.0 / 56.0, 2.0 / 825.0, -1.0 / 5544.0)
second_coefs = (12.0 / 7.0, -15.0 / 56.0, 10.0 / 189.0, -1.0 / 112.0, 2.0 / 1925.0, -1.0 / 16632.0)
center_coef = -5369.0 / 1800.0
filter_center = 13.5
filter_half = 10.5

F32, BF16 = jnp.float32, jnp.bfloat16
VMEM = pl.BlockSpec(memory_space=pltpu.VMEM)
SMEM = pl.BlockSpec(memory_space=pltpu.SMEM)
LIMIT = 24 * 1024 * 1024


def derivative_table():
    table = np.zeros((NZ, 2 * NZ), np.float64)
    for z in range(NZ):
        table[z, NZ + z] = 3.0 * center_coef
        for k in range(1, HALO + 1):
            if z + k < NZ:
                table[z + k, z] = first_coefs[k - 1]
                table[z + k, NZ + z] = second_coefs[k - 1]
            if z - k >= 0:
                table[z - k, z] = -first_coefs[k - 1]
                table[z - k, NZ + z] = second_coefs[k - 1]
    high = table.astype(ml_dtypes.bfloat16)
    low = (table - high.astype(np.float64)).astype(ml_dtypes.bfloat16)
    return np.concatenate([high, low], axis=0)


def split(a):
    high = a.astype(BF16)
    return high, (a - high.astype(F32)).astype(BF16)


def mm(a, b):
    return jnp.dot(a, b, preferred_element_type=F32)


def mm_t(a, b):
    return lax.dot_general(a, b, (((1,), (1,)), ((), ())), preferred_element_type=F32)


def pick(a, table):
    high, low = split(a)
    return mm(high, table) + mm(low, table)


def pick_t(a, table):
    high, low = split(a)
    return mm_t(high, table) + mm_t(low, table)


def get(ref, tile):
    return ref[pl.ds(tile * 8, 8), :]


def put(ref, tile, value):
    ref[pl.ds(tile * 8, 8), :] = value


def get_at(ref, tile):
    return ref[pl.ds(pl.multiple_of(tile * 8, 8), 8), :]


def iotas():
    return (
        lax.broadcasted_iota(jnp.int32, (8, 128), 0),
        lax.broadcasted_iota(jnp.int32, (8, 128), 1),
    )


def row(value, index):
    return jnp.broadcast_to(value[index : index + 1, :], (8, 128))


def pack_rims(y_ref, hi_ref, lo_ref, low):
    for x in range(CX):
        for m in range(3):
            put(hi_ref, x * 3 + m, jnp.where(low, pltpu.roll(get(y_ref, x * 8 + 2 + m), 4, 0), get(y_ref, x * 8 + 5 + m)))
            put(lo_ref, x * 3 + m, jnp.where(low, get(y_ref, x * 8 + m), pltpu.roll(get(y_ref, x * 8 + 3 + m), 4, 0)))


def sides(odd, even_op, odd_op):
    return jnp.where(odd, even_op, odd_op), jnp.where(odd, odd_op, even_op)


def send(flag, below, above, even_ref, odd_ref, tiles, base=0):
    even_from = jnp.where(flag == 1, 0, 1)
    for t in range(tiles):
        one, two = get(below, t), get(above, t)
        put(even_ref, base + t, jnp.where(even_from == 0, one, two))
        put(odd_ref, base + t, jnp.where(even_from == 0, two, one))


def take(flag, even_ref, odd_ref, target, rows, low_at, high_at):
    even_at = pl.multiple_of(jnp.where(flag == 1, low_at, high_at), 8)
    odd_at = pl.multiple_of(jnp.where(flag == 1, high_at, low_at), 8)
    target[pl.ds(even_at, rows), :] = even_ref[0:rows, :]
    target[pl.ds(odd_at, rows), :] = odd_ref[0:rows, :]


def give_ends(flag, y_ref, even_ref, odd_ref):
    rows = XH * 8
    even_at = pl.multiple_of(jnp.where(flag == 1, 0, rows), 8)
    odd_at = pl.multiple_of(jnp.where(flag == 1, rows, 0), 8)
    even_ref[0:rows, :] = y_ref[pl.ds(even_at, rows), :]
    odd_ref[0:rows, :] = y_ref[pl.ds(odd_at, rows), :]


def prep_slots_kernel(flags, offs, strg, cnt, proj, mu, t_ref, meta_ref, xe_ref, xo_ref, g_ref, mu_out, xr_ref, xl_ref):
    mu_out[...] = mu[...]
    at_row = lax.broadcasted_iota(jnp.int32, (1024, 128), 0)
    at_column = lax.broadcasted_iota(jnp.int32, (1024, 128), 1)
    same = (at_row % 128 // 8 == at_column // 8) & (at_row // 128 == at_column % 8)
    g_ref[...] = jnp.where(same, 1.0, 0.0).astype(BF16)
    sub, lane = iotas()
    left_half = lane < 64
    group = lane // 8
    meta = jnp.zeros((8, 128), F32)
    for s in range(8):
        for column in range(3):
            value = offs[column, s].astype(F32)
            meta = jnp.where((group == s) & (sub == column), value, meta)
        alive = jnp.where(s < cnt[0], 1.0, 0.0).astype(F32)
        for p in range(8):
            weight = strg[s, p] * alive * (1.0 / (512.0 * filter_half))
            meta = jnp.where((lane == s * 8 + p) & (sub == 3), weight, meta)
    meta_ref[...] = meta
    for i in range(8):
        for j in range(8):
            start = (i % 2) * 64 + j * 8
            total = jnp.zeros((8, 128), F32)
            for s in range(8):
                source = proj[s, :, 128 * (i // 2) : 128 * (i // 2) + 128]
                shift = (s * 8 - start) % 128
                moved = pltpu.roll(source, shift, 1) if shift else source
                total = jnp.where(group == s, moved, total)
            put(t_ref, i * 8 + j, total)
    for i in range(2):
        for j in range(8):
            for ref, first in ((xr_ref, 4), (xl_ref, 0)):
                one = get(t_ref, (first + i) * 8 + j)
                two = pltpu.roll(get(t_ref, (first + 2 + i) * 8 + j), 64, 1)
                put(ref, i * 8 + j, jnp.where(left_half, one, two))
    put(xr_ref, 16, meta)
    put(xl_ref, 16, meta)
    send(flags[0], xl_ref, xr_ref, xe_ref, xo_ref, 17)
    for x in range(HALO):
        for h in range(2):
            left, right = mu[x, 8 * h : 8 * h + 8, :], mu[CX - HALO + x, 8 * h : 8 * h + 8, :]
            put(xe_ref, 17 + 2 * x + h, jnp.where(flags[0] == 1, left, right))
            put(xo_ref, 17 + 2 * x + h, jnp.where(flags[0] == 1, right, left))


def prep_fields_kernel(orb, pot, y_ref, pot_out):
    pot_out[...] = pot[...]
    for x in range(CX):
        for o in range(ORB):
            for h in range(2):
                y_ref[pl.ds(x * 64 + 4 * h + o, 8, stride=8), :] = orb[o, x, 8 * h : 8 * h + 8, :]


X_SUMS, Y_SUMS = XH, YH
X_ALL, Y_MU = XH + 3, YH + 4
Y_ALL = Y_MU + CX


def send_rims(flag, y_ref, rims, ye_ref, yo_ref):
    low = iotas()[0] < 4
    rows = YH * 8
    pack_rims(y_ref, rims.at[pl.ds(rows, rows)], rims.at[pl.ds(0, rows)], low)
    ye_ref[0:rows, :] = rims[pl.ds(pl.multiple_of(jnp.where(flag == 1, 0, rows), 8), rows), :]
    yo_ref[0:rows, :] = rims[pl.ds(pl.multiple_of(jnp.where(flag == 1, rows, 0), 8), rows), :]


def widen_kernel(flags, t_ref, meta_ref, xe_ref, xo_ref, t2_ref, m_ref, ye_ref, yo_ref, fl_ref, fr_ref, hi_ref, lo_ref):
    _, lane = iotas()
    left_half = lane < 64
    base = 0
    for t in range(17):
        left, right = sides(flags[0] == 1, get(xe_ref, t), get(xo_ref, t))
        put(fl_ref, t, left)
        put(fr_ref, t, right)
    for i in range(8):
        for j in range(8):
            if i >= 4:
                other = get(fl_ref, base + (i % 2) * 8 + j)
                other = other if i >= 6 else pltpu.roll(other, 64, 1)
            else:
                other = get(fr_ref, base + (i % 2) * 8 + j)
                other = other if i >= 2 else pltpu.roll(other, 64, 1)
            both = jnp.where(left_half, get(t_ref, i * 8 + j), other)
            put(t2_ref, i * 8 + j, both)
            if j >= 4:
                put(hi_ref, i * 4 + j - 4, both)
            else:
                put(lo_ref, i * 4 + j, both)
    meta = meta_ref[...]
    for side, ref in enumerate((fl_ref, fr_ref)):
        both = jnp.where(left_half, meta, pltpu.roll(get(ref, base + 16), 64, 1))
        put(m_ref, side, both)
        put(hi_ref, 32 + side, both)
        put(lo_ref, 32 + side, both)
    send(flags[1], lo_ref, hi_ref, ye_ref, yo_ref, 34)


def coef_kernel(flags, mu, pot, xe_ref, xo_ref, ye_ref, yo_ref, dz_ref, out_ref, ex, ey):
    sub, _ = iotas()
    low = sub < 4

    def two(a, ia, b, ib):
        return jnp.where(low, row(a, ia), row(b, ib))

    ends = [sides(flags[0] == 1, get(xe_ref, 17 + t), get(xo_ref, 17 + t)) for t in range(2 * HALO)]
    for x in range(CX + 2 * HALO):
        if x < HALO:
            a, b = ends[2 * x][0], ends[2 * x + 1][0]
        elif x < HALO + CX:
            a, b = mu[x - HALO, 0:8, :], mu[x - HALO, 8:16, :]
        else:
            a, b = ends[2 * (x - HALO - CX)][1], ends[2 * (x - HALO - CX) + 1][1]
        for yl in range(8):
            put(ex, x * 8 + yl, two(a, yl, b, yl))
    for x in range(CX):
        lo_rim, hi_rim = sides(flags[1] == 1, get(ye_ref, Y_MU + x), get(yo_ref, Y_MU + x))
        parts = [lo_rim, mu[x, 0:8, :], mu[x, 8:16, :], hi_rim]
        for n in range(20):
            y = n - HALO
            put(ey, x * 20 + n, two(parts[(y + 8) // 8], y % 8, parts[(y + 16) // 8], y % 8))
    field = ex[XH * 8 : (XH + TILES) * 8, :]
    high, rest = split(field)
    zd = mm(high, dz_ref[0:NZ, 0:NZ]) + mm(rest, dz_ref[0:NZ, 0:NZ]) + mm(high, dz_ref[NZ : 2 * NZ, 0:NZ])
    out_ref[3 * 768 : 4 * 768, :] = zd * (-0.5 / filter_half)

    def body(x, carry):
        va, vb = pot[x, 0:8, :], pot[x, 8:16, :]
        for yl in range(8):
            gx = jnp.zeros((8, 128), F32)
            gy = jnp.zeros((8, 128), F32)
            for k in range(1, HALO + 1):
                gx += first_coefs[k - 1] * (get_at(ex, (x + HALO + k) * 8 + yl) - get_at(ex, (x + HALO - k) * 8 + yl))
                gy += first_coefs[k - 1] * (
                    get_at(ey, x * 20 + HALO + yl + k) - get_at(ey, x * 20 + HALO + yl - k)
                )
            r = x * 8 + yl
            center = get_at(ex, (x + HALO) * 8 + yl)

            def store(which, value):
                out_ref[pl.ds(pl.multiple_of((which * TILES + r) * 8, 8), 8), :] = value

            store(0, (1.0 + center) * (-0.5 / filter_half))
            store(1, gx * (-0.5 / filter_half))
            store(2, gy * (-0.5 / filter_half))
            store(4, (two(va, yl, vb, yl) - filter_center) * (1.0 / filter_half))
        return carry

    lax.fori_loop(0, CX, body, 0)


def block_tiles(xt, yq):
    return [(4 * xt + a) * 8 + 4 * yq for a in range(4)]


def side_of(xt):
    return 1 if xt == 2 else 0


def partial_coeffs(y_ref, q_ref, s_ref, g_ref, z_ref, acc):
    left_half = lax.broadcasted_iota(jnp.int32, (8, 1024), 1) % 128 < 64
    own = None
    ends = {}
    rims = [None, None]
    corners = {}
    for xt in range(3):
        for yq in range(2):
            b = xt * 2 + yq
            field = jnp.concatenate([y_ref[t * 8 : t * 8 + 32, :] for t in block_tiles(xt, yq)], axis=0)
            table = s_ref[(side_of(xt) * 2 + yq) * 128 : (side_of(xt) * 2 + yq) * 128 + 128, :]
            seen = pick(field, table).reshape(16, 8, 256)
            sums = []
            for p in range(8):
                base = (b * 8 + p) * 128
                product = seen * q_ref[base : base + 128, :].reshape(16, 8, 256)
                total = jnp.sum(product, axis=0)
                sums.append(total + pltpu.roll(total, 4, 0))
            col_a = jnp.concatenate([t[:, :128] for t in sums], axis=1)
            col_b = jnp.concatenate([t[:, 128:] for t in sums], axis=1)
            own = col_a if own is None else own + col_a
            rims[yq] = col_b if rims[yq] is None else rims[yq] + col_b
            if xt != 1:
                ends[xt] = ends[xt] + col_a if xt in ends else col_a
                corners[(xt, yq)] = col_b
    for side, xt in enumerate((0, 2)):
        acc[side * 24 : side * 24 + 8, :] = jnp.where(left_half, own, ends[xt])
        for yq in range(2):
            at = side * 24 + 8 + yq * 8
            acc[at : at + 8, :] = jnp.where(left_half, rims[yq], corners[(xt, yq)])
    z_ref[...] = pick(acc[...], g_ref[...])


def send_coeffs(flag, z_ref, ye_ref, yo_ref, base):
    for side in range(2):
        for n, (above, below) in enumerate(((2, 1), (0, 0))):
            above, below = get(z_ref, side * 3 + above), get(z_ref, side * 3 + below)
            put(ye_ref, base + side * 2 + n, jnp.where(flag == 1, below, above))
            put(yo_ref, base + side * 2 + n, jnp.where(flag == 1, above, below))


def build_kernel(
    flags, t2_ref, m_ref, ye_ref, yo_ref, y_ref, mu, g_ref,
    q_ref, s_ref, w_ref, z_ref, nye_ref, nyo_ref, tx, acc, lo_ref, hi_ref, rims
):
    for t in range(34):
        lo, hi = sides(flags[1] == 1, get(ye_ref, t), get(yo_ref, t))
        put(lo_ref, t, lo)
        put(hi_ref, t, hi)
    sub, lane = iotas()
    low = sub < 4
    right_half = lane >= 64
    metas = [get(m_ref, 0), get(lo_ref, 32), get(hi_ref, 32), get(m_ref, 1), get(lo_ref, 33), get(hi_ref, 33)]
    for t in range(6):
        put(w_ref, t, row(metas[t], 3))
    zi = lax.broadcasted_iota(jnp.int32, (128, 128), 0)
    for side in range(2):
        for yq in range(2):
            for col, t in enumerate((side * 3, side * 3 + 1 + yq)):
                place = metas[t][2:3, :].astype(jnp.int32) + lane[0:1, :] % 8
                base = (side * 2 + yq) * 128
                hot = jnp.where(zi == jnp.broadcast_to(place, (128, 128)), 1.0, 0.0).astype(BF16)
                s_ref[base : base + 128, col * 128 : col * 128 + 128] = hot

    def table(col, i, j):
        if col == 0:
            return get(t2_ref, i * 8 + j)
        return get(lo_ref, i * 4 + j - 4) if j >= 4 else get(hi_ref, i * 4 + j)

    zero = jnp.zeros((8, 128), F32)
    for xt in range(3):
        shift = (-12.0, 1000.0, 12.0)[xt]
        for col in range(2):
            for yq in range(2):
                b = xt * 2 + yq
                t = side_of(xt) * 3 + (0 if col == 0 else 1 + yq)
                x0 = row(metas[t], 0) - 6.0 + jnp.where(right_half, shift, 0.0)
                y0 = row(metas[t], 1) - 6.0
                if col == 1:
                    y0 = y0 + (16.0 if yq == 1 else -16.0)
                js = range(8) if col == 0 else (range(0, 4) if yq == 1 else range(4, 8))
                if col == 1 or yq == 0:
                    for a in range(4):
                        for j in js:
                            moved = zero
                            for i in range(8):
                                moved = jnp.where(x0 == float(4 * xt + a - i), table(col, i, j), moved)
                            put(tx, a * 8 + j, moved)
                for a in range(4):
                    for c in range(4):
                        rows = []
                        for h in range(2):
                            y = 8 * h + 4 * yq + c
                            moved = zero
                            if col == 0 or h == yq:
                                for j in js:
                                    moved = jnp.where(y0 == float(y - j), get(tx, a * 8 + j), moved)
                            rows.append(moved)
                        for p in range(8):
                            base = ((b * 8 + p) * 16 + a * 4 + c) * 8
                            value = jnp.where(low, row(rows[0], p), row(rows[1], p))
                            q_ref[base : base + 8, col * 128 : col * 128 + 128] = value
    partial_coeffs(y_ref, q_ref, s_ref, g_ref, z_ref, acc)
    send_coeffs(flags[1], z_ref, nye_ref, nyo_ref, Y_SUMS)
    send_rims(flags[1], y_ref, rims, nye_ref, nyo_ref)
    for x in range(CX):
        below, above = mu[x, 0:8, :], mu[x, 8:16, :]
        put(nye_ref, Y_MU + x, jnp.where(flags[1] == 1, below, above))
        put(nyo_ref, Y_MU + x, jnp.where(flags[1] == 1, above, below))


def fold_kernel(flags, z_ref, y_ref, ye_ref, yo_ref, out_ref, xe_ref, xo_ref):
    give_ends(flags[0], y_ref, xe_ref, xo_ref)
    base = Y_SUMS
    for side in range(2):
        own, lo, hi = (get(z_ref, side * 3 + t) for t in range(3))
        across = [(get(ye_ref, base + side * 2 + n), get(yo_ref, base + side * 2 + n)) for n in range(2)]
        from_lo, from_hi = sides(flags[1] == 1, *across[1])
        put(out_ref, side * 3, own + across[0][0] + across[0][1])
        put(out_ref, side * 3 + 1, lo + from_lo)
        put(out_ref, side * 3 + 2, hi + from_hi)
    for t in range(3):
        left, right = pltpu.roll(get(out_ref, t), 64, 1), pltpu.roll(get(out_ref, 3 + t), 64, 1)
        put(xe_ref, X_SUMS + t, jnp.where(flags[0] == 1, left, right))
        put(xo_ref, X_SUMS + t, jnp.where(flags[0] == 1, right, left))


def step_kernel(
    step, flags, y_ref, prev_ref, xe_ref, xo_ref, ye_ref, yo_ref, coef_ref, q_ref, s_ref, w_ref, z_ref,
    dz_ref, g_ref, *rest
):
    last = step == STEPS
    if last:
        first_ref, second_ref, ex, ey, zd, wp, rims, new_ref = rest
    else:
        new_ref, nye_ref, nyo_ref, zn_ref, ex, ey, zd, wp, rims, acc = rest
    sub, lane = iotas()
    low = sub < 4
    scale = 1.0 if step == 1 else 2.0

    high, rest_part = split(y_ref[...])
    zd[...] = mm(high, dz_ref[0:NZ, :]) + mm(rest_part, dz_ref[0:NZ, :]) + mm(high, dz_ref[NZ : 2 * NZ, :])

    take(flags[0], xe_ref, xo_ref, ex, XH * 8, 0, (XH + TILES) * 8)
    take(flags[1], ye_ref, yo_ref, rims, YH * 8, 0, YH * 8)
    ex[XH * 8 : (XH + TILES) * 8, :] = y_ref[...]
    for x in range(CX):
        for yl in range(8):
            put(ey, x * 20 + HALO + yl, get(y_ref, x * 8 + yl))
        lo_rims = [get(rims, x * 3 + m) for m in range(3)]
        hi_rims = [get(rims, YH + x * 3 + m) for m in range(3)]
        for m in range(HALO):
            rim = lo_rims[m] if m < 3 else pltpu.roll(lo_rims[m - 3], 4, 0)
            put(ey, x * 20 + m, jnp.where(low, rim, pltpu.roll(get(y_ref, x * 8 + 2 + m), 4, 0)))
            rim = pltpu.roll(hi_rims[m], 4, 0) if m < 3 else hi_rims[m - 3]
            put(ey, x * 20 + HALO + 8 + m, jnp.where(low, pltpu.roll(get(y_ref, x * 8 + m), 4, 0), rim))

    def body(x, carry):
        for yl in range(8):
            r = x * 8 + yl
            center = get_at(y_ref, r)
            gx = gy = lap = None
            for k in range(1, HALO + 1):
                xp, xm = get_at(ex, (x + HALO + k) * 8 + yl), get_at(ex, (x + HALO - k) * 8 + yl)
                yp, ym = get_at(ey, x * 20 + HALO + yl + k), get_at(ey, x * 20 + HALO + yl - k)
                tx = first_coefs[k - 1] * (xp - xm)
                ty = first_coefs[k - 1] * (yp - ym)
                tl = second_coefs[k - 1] * ((xp + xm) + (yp + ym))
                gx, gy, lap = (tx, ty, tl) if k == 1 else (gx + tx, gy + ty, lap + tl)
            at = pl.ds(pl.multiple_of(r * 8, 8), 8)
            total = get_at(coef_ref, r) * (lap + zd[at, NZ:])
            total += get_at(coef_ref, TILES + r) * gx
            total += get_at(coef_ref, 2 * TILES + r) * gy
            total += get_at(coef_ref, 3 * TILES + r) * zd[at, :NZ]
            total += get_at(coef_ref, 4 * TILES + r) * center
            new_ref[at, :] = total if step == 1 else 2.0 * total - get_at(prev_ref, r)
        return carry

    lax.fori_loop(0, CX, body, 0)

    left_half = lane < 64
    from_x = [sides(flags[0] == 1, get(xe_ref, X_SUMS + t), get(xo_ref, X_SUMS + t)) for t in range(3)]
    tiles = []
    for side in range(2):
        for t in range(3):
            near, far = from_x[t][side], from_x[t][1 - side]
            tiles.append(get(z_ref, side * 3 + t) + near + jnp.where(left_half, far, 0.0))
    weights = jnp.concatenate(tiles, axis=0) * w_ref[...] * scale
    wp[...] = pick_t(weights, g_ref[...])

    for xt in range(3):
        for yq in range(2):
            b = xt * 2 + yq
            ta, tb = side_of(xt) * 3, side_of(xt) * 3 + 1 + yq
            total = None
            for p in range(8):
                weight = jnp.concatenate(
                    [wp[t * 8 : t * 8 + 8, p * 128 : p * 128 + 128] for t in (ta, tb)], axis=1
                )
                base = (b * 8 + p) * 128
                term = weight[None] * q_ref[base : base + 128, :].reshape(16, 8, 256)
                total = term if total is None else total + term
            table = s_ref[(side_of(xt) * 2 + yq) * 128 : (side_of(xt) * 2 + yq) * 128 + 128, :]
            spread = pick_t(total.reshape(128, 256), table)
            for a, t in enumerate(block_tiles(xt, yq)):
                new_ref[t * 8 : t * 8 + 32, :] += spread[a * 32 : a * 32 + 32, :]

    if last:
        half = TILES * 4
        first_ref[...] = new_ref[0:half, :]
        second_ref[...] = new_ref[half : 2 * half, :]
    else:
        send_rims(flags[1], new_ref, rims, nye_ref, nyo_ref)
        partial_coeffs(new_ref, q_ref, s_ref, g_ref, zn_ref, acc)
        send_coeffs(flags[1], zn_ref, nye_ref, nyo_ref, Y_SUMS)


def two_layers(refs, x):
    half, at = x // (CX // 2), x % (CX // 2) * 64
    sides = [[refs[2 * n + half][a : a + 64, :] for n in range(4)] for a in (at, at + 64)]
    return jnp.concatenate([jnp.concatenate(side, axis=0) for side in sides], axis=1)


def ring_orbitals(order):
    orbital = lax.broadcasted_iota(jnp.int32, (16, 256), 0)
    held_at = lax.broadcasted_iota(jnp.int32, (16, 256), 1)
    device = held_at // 64
    owner = jnp.where(device == 0, order[0], jnp.where(device == 1, order[1], jnp.where(device == 2, order[2], order[3])))
    return jnp.where(orbital == owner * 4 + held_at % 4, 1.0, 0.0).astype(F32)


def gram_kernel(order, *refs):
    out_ref = refs[8]
    total = mixed = None
    for x in range(0, CX, 2):
        high, low = split(two_layers(refs, x))
        one, two = mm_t(high, high), mm_t(high, low)
        total, mixed = (one, two) if x == 0 else (total + one, mixed + two)
    total = total + mixed + mixed.T
    rows = lax.broadcasted_iota(jnp.int32, (256, 256), 0)
    columns = lax.broadcasted_iota(jnp.int32, (256, 256), 1)
    total = jnp.where((rows % 64) // 4 == (columns % 64) // 4, total, 0.0)
    hot = ring_orbitals(order)
    first = jnp.dot(hot, total, precision=lax.Precision.HIGHEST, preferred_element_type=F32)
    small = lax.dot_general(
        first, hot, (((1,), (1,)), ((), ())), precision=lax.Precision.HIGHEST, preferred_element_type=F32
    )
    out_ref[...] = jnp.zeros((8, 128), F32)
    out_ref[:, 0:16] = small[0:8]
    out_ref[:, 16:32] = small[8:16]


def rotate_kernel(cells, order, corr_ref, *refs):
    out_ref, flat = refs[8:]
    lane = lax.broadcasted_iota(jnp.int32, (16, 128), 1)
    rows = lax.broadcasted_iota(jnp.int32, (16, 128), 0)
    packed = corr_ref[...]
    whole = jnp.concatenate([packed, pltpu.roll(packed, 112, 1)], axis=0)
    work = jnp.where(lane < 16, whole * (1.0 / cells), jnp.where(lane == rows + 16, 1.0, 0.0))
    pivots = jnp.ones((16, 128), F32)
    for k in range(16):
        pivot_row = jnp.broadcast_to(work[k : k + 1, :], (16, 128))
        pivot = jnp.broadcast_to(pivot_row[:, k : k + 1], (16, 128))
        column = jnp.broadcast_to(work[:, k : k + 1], (16, 128))
        pivots = jnp.where(rows == k, pivot, pivots)
        work = jnp.where(rows > k, work - column / pivot * pivot_row, work)
    inverse = (work / jnp.sqrt(pivots))[:, 16:32]
    me = order[0]
    own_row = lax.broadcasted_iota(jnp.int32, (64, 16), 0)
    orbital = lax.broadcasted_iota(jnp.int32, (64, 16), 1)
    left = jnp.where(orbital == me * 4 + own_row % 4, 1.0, 0.0).astype(F32)
    right = ring_orbitals(order)
    exact = functools.partial(jnp.dot, precision=lax.Precision.HIGHEST, preferred_element_type=F32)
    mixing = exact(exact(left, inverse), right)
    at_row = lax.broadcasted_iota(jnp.int32, (64, 256), 0)
    at_column = lax.broadcasted_iota(jnp.int32, (64, 256), 1)
    mixing = jnp.where(at_row // 4 == at_column % 64 // 4, mixing, 0.0)
    mix_high, mix_low = split(mixing)
    for x in range(0, CX, 2):
        high, low = split(two_layers(refs, x))
        both = mm(mix_high, high) + mm(mix_high, low) + mm(mix_low, high)
        flat[x * 64 : x * 64 + 64, :] = both[:, :NZ]
        flat[x * 64 + 64 : x * 64 + 128, :] = both[:, NZ:]
    for o in range(ORB):
        for x in range(CX):
            for h in range(2):
                out_ref[o, x, 8 * h : 8 * h + 8, :] = flat[pl.ds(x * 64 + 4 * h + o, 8, stride=8), :]


def kernel_call(body, outs, ins, scratch=(), name=None):
    return pl.pallas_call(
        body,
        out_shape=[jax.ShapeDtypeStruct(shape, dtype) for shape, dtype in outs],
        in_specs=ins,
        out_specs=[VMEM] * len(outs),
        scratch_shapes=list(scratch),
        compiler_params=pltpu.CompilerParams(vmem_limit_bytes=LIMIT),
        name=name,
    )


def blocks(count, columns=128, dtype=F32):
    return (count * 8, columns), dtype


def exchange(even_value, odd_value, axis):
    count = lax.axis_size(axis)
    results = []
    for first, value in ((1, odd_value), (0, even_value)):
        pairs = [p for i in range(first, count - 1, 2) for p in ((i, i + 1), (i + 1, i))]
        results.append(lax.ppermute(value, axis, pairs))
    return results[1], results[0]


def spread_sum(value, axis):
    copies = jnp.broadcast_to(value[None], (lax.axis_size(axis),) + value.shape)
    return jnp.sum(lax.all_to_all(copies, axis, 0, 0, tiled=True), axis=0)


def fold(flags, z, y, even, odd):
    return kernel_call(
        fold_kernel, [blocks(6), blocks(X_ALL), blocks(X_ALL)], [SMEM] + [VMEM] * 4, name="fold_coeffs"
    )(flags, z, y, even, odd)


def shards(orbitals, potential, kinetic_mu, projectors, strengths, box_offsets, block_counts):
    dz = jnp.asarray(derivative_table())
    flags = jnp.stack([lax.axis_index("gx") % 2, lax.axis_index("gy") % 2]).astype(jnp.int32)
    t, meta, xte, xto, groups, mu = kernel_call(
        prep_slots_kernel,
        [blocks(64), blocks(1), blocks(17 + 2 * HALO), blocks(17 + 2 * HALO)]
        + [((1024, 128), BF16), ((CX, CY, NZ), F32)],
        [SMEM] * 4 + [VMEM] * 2,
        [pltpu.VMEM((17 * 8, 128), F32)] * 2,
        name="prepare_slots",
    )(flags, box_offsets.T, strengths, block_counts, projectors, kinetic_mu)
    orbitals, xte, xto = lax.optimization_barrier((orbitals, xte, xto))
    xte, xto = exchange(xte, xto, "gx")
    y, pot = kernel_call(
        prep_fields_kernel,
        [blocks(TILES), ((CX, CY, NZ), F32)],
        [VMEM] * 2,
        name="prepare_fields",
    )(orbitals, potential)
    t2, metas, ye2, yo2 = kernel_call(
        widen_kernel,
        [blocks(64), blocks(2), blocks(34), blocks(34)],
        [SMEM] + [VMEM] * 4,
        [pltpu.VMEM((17 * 8, 128), F32)] * 2 + [pltpu.VMEM((34 * 8, 128), F32)] * 2,
        name="widen",
    )(flags, t, meta, xte, xto)
    ye2, yo2 = exchange(ye2, yo2, "gy")
    q, s, w, z, ye, yo = kernel_call(
        build_kernel,
        [blocks(6 * 8 * 16, 256), ((4 * 128, 256), BF16), blocks(6), blocks(6), blocks(Y_ALL), blocks(Y_ALL)],
        [SMEM] + [VMEM] * 7,
        [
            pltpu.VMEM((32 * 8, 128), F32),
            pltpu.VMEM((48, 1024), F32),
            pltpu.VMEM((34 * 8, 128), F32),
            pltpu.VMEM((34 * 8, 128), F32),
            pltpu.VMEM((2 * YH * 8, 128), F32),
        ],
        name="build",
    )(flags, t2, metas, ye2, yo2, y, mu, groups)
    ye, yo = exchange(ye, yo, "gy")
    z, xe, xo = fold(flags, z, y, ye, yo)
    xe, xo = exchange(xe, xo, "gx")
    (coefs,) = kernel_call(
        coef_kernel,
        [blocks(5 * TILES)],
        [SMEM] + [VMEM] * 7,
        [pltpu.VMEM(((TILES + 2 * XH) * 8, 128), F32), pltpu.VMEM((CX * 20 * 8, 128), F32)],
        name="coefficients",
    )(flags, mu, pot, xte, xto, ye, yo, dz)

    previous = y
    for step in range(1, STEPS + 1):
        last = step == STEPS
        if last:
            outs = [blocks(TILES // 2), blocks(TILES // 2)]
        else:
            outs = [blocks(TILES), blocks(Y_MU), blocks(Y_MU), blocks(6)]
        result = kernel_call(
            functools.partial(step_kernel, step),
            outs,
            [SMEM] + [VMEM] * 13,
            [
                pltpu.VMEM(((TILES + 2 * XH) * 8, 128), F32),
                pltpu.VMEM((CX * 20 * 8, 128), F32),
                pltpu.VMEM((TILES * 8, 256), F32),
                pltpu.VMEM((48, 1024), F32),
                pltpu.VMEM((2 * YH * 8, 128), F32),
                pltpu.VMEM((TILES * 8, 128) if last else (48, 1024), F32),
            ],
            name="step",
        )(flags, y, previous, xe, xo, ye, yo, coefs, q, s, w, z, dz, groups)
        previous = y
        if not last:
            y, ye, yo, z = result
            ye, yo = exchange(ye, yo, "gy")
            z, xe, xo = fold(flags, z, y, ye, yo)
            xe, xo = exchange(xe, xo, "gx")

    count = lax.axis_size("orb")
    me = lax.axis_index("orb")
    even = [(i, i ^ 1) for i in range(count)]
    odd = [(i, count - 1 - i) for i in range(count)]
    parts = result
    one_a, other_b = lax.ppermute(parts[0], "orb", even), lax.ppermute(parts[1], "orb", odd)
    one_b, other_a = lax.ppermute(parts[1], "orb", even), lax.ppermute(parts[0], "orb", odd)
    across_a, across_b = lax.ppermute(one_a, "orb", odd), lax.ppermute(other_b, "orb", even)
    gathered = (parts[0], parts[1], one_a, one_b, other_a, other_b, across_a, across_b)
    order = jnp.stack([me, me ^ 1, count - 1 - me, (me + 2) % count]).astype(jnp.int32)
    (corr,) = kernel_call(
        gram_kernel,
        [blocks(1)],
        [SMEM] + [VMEM] * 8,
        name="gram",
    )(order, *gathered)
    for axis in ("gx", "gy"):
        corr = spread_sum(corr, axis)
    cells = CX * CY * NZ * lax.axis_size("gx") * lax.axis_size("gy")
    (result,) = kernel_call(
        functools.partial(rotate_kernel, cells),
        [((ORB, CX, CY, NZ), F32)],
        [SMEM] + [VMEM] * 9,
        [pltpu.VMEM((TILES * 8, 128), F32)],
        name="rotate",
    )(order, corr, *gathered)
    return result


def solution(mesh):
    in_specs = (
        P("orb", "gx", "gy", None),
        P("gx", "gy", None),
        P("gx", "gy", None),
        P(("gx", "gy"), None, None),
        P(("gx", "gy"), None),
        P(("gx", "gy"), None),
        P(("gx", "gy")),
    )
    out_specs = P("orb", "gx", "gy", None)
    return jax.shard_map(shards, mesh=mesh, in_specs=in_specs, out_specs=out_specs, check_vma=False)
```

```python
import functools

import jax
import jax.numpy as jnp
import ml_dtypes
import numpy as np
from jax import lax
from jax.experimental import pallas as pl
from jax.experimental.pallas import tpu as pltpu
from jax.sharding import PartitionSpec as P

CX, CY, NZ, ORB = 12, 16, 128, 4
HALO = 6
TILES = 96
XH = HALO * 8
YH = CX * 3
STEPS = 3

first_coefs = (6.0 / 7.0, -15.0 / 56.0, 5.0 / 63.0, -1.0 / 56.0, 2.0 / 825.0, -1.0 / 5544.0)
second_coefs = (12.0 / 7.0, -15.0 / 56.0, 10.0 / 189.0, -1.0 / 112.0, 2.0 / 1925.0, -1.0 / 16632.0)
center_coef = -5369.0 / 1800.0
filter_center = 13.5
filter_half = 10.5

F32, BF16 = jnp.float32, jnp.bfloat16
VMEM = pl.BlockSpec(memory_space=pltpu.VMEM)
SMEM = pl.BlockSpec(memory_space=pltpu.SMEM)
LIMIT = 24 * 1024 * 1024


def derivative_table():
    table = np.zeros((NZ, 2 * NZ), np.float64)
    for z in range(NZ):
        table[z, NZ + z] = 3.0 * center_coef
        for k in range(1, HALO + 1):
            if z + k < NZ:
                table[z + k, z] = first_coefs[k - 1]
                table[z + k, NZ + z] = second_coefs[k - 1]
            if z - k >= 0:
                table[z - k, z] = -first_coefs[k - 1]
                table[z - k, NZ + z] = second_coefs[k - 1]
    high = table.astype(ml_dtypes.bfloat16)
    low = (table - high.astype(np.float64)).astype(ml_dtypes.bfloat16)
    return np.concatenate([high, low], axis=0)


def split(a):
    high = a.astype(BF16)
    return high, (a - high.astype(F32)).astype(BF16)


def mm(a, b):
    return jnp.dot(a, b, preferred_element_type=F32)


def mm_t(a, b):
    return lax.dot_general(a, b, (((1,), (1,)), ((), ())), preferred_element_type=F32)


def pick(a, table):
    high, low = split(a)
    return mm(high, table) + mm(low, table)


def pick_t(a, table):
    high, low = split(a)
    return mm_t(high, table) + mm_t(low, table)


def get(ref, tile):
    return ref[pl.ds(tile * 8, 8), :]


def put(ref, tile, value):
    ref[pl.ds(tile * 8, 8), :] = value


def get_at(ref, tile):
    return ref[pl.ds(pl.multiple_of(tile * 8, 8), 8), :]


def iotas():
    return (
        lax.broadcasted_iota(jnp.int32, (8, 128), 0),
        lax.broadcasted_iota(jnp.int32, (8, 128), 1),
    )


def row(value, index):
    return jnp.broadcast_to(value[index : index + 1, :], (8, 128))


def pack_rims(y_ref, hi_ref, lo_ref, low):
    for x in range(CX):
        for m in range(3):
            put(hi_ref, x * 3 + m, jnp.where(low, pltpu.roll(get(y_ref, x * 8 + 2 + m), 4, 0), get(y_ref, x * 8 + 5 + m)))
            put(lo_ref, x * 3 + m, jnp.where(low, get(y_ref, x * 8 + m), pltpu.roll(get(y_ref, x * 8 + 3 + m), 4, 0)))


def sides(odd, even_op, odd_op):
    return jnp.where(odd, even_op, odd_op), jnp.where(odd, odd_op, even_op)


def send(flag, below, above, even_ref, odd_ref, tiles, base=0):
    even_from = jnp.where(flag == 1, 0, 1)
    for t in range(tiles):
        one, two = get(below, t), get(above, t)
        put(even_ref, base + t, jnp.where(even_from == 0, one, two))
        put(odd_ref, base + t, jnp.where(even_from == 0, two, one))


def take(flag, even_ref, odd_ref, target, rows, low_at, high_at):
    even_at = pl.multiple_of(jnp.where(flag == 1, low_at, high_at), 8)
    odd_at = pl.multiple_of(jnp.where(flag == 1, high_at, low_at), 8)
    target[pl.ds(even_at, rows), :] = even_ref[0:rows, :]
    target[pl.ds(odd_at, rows), :] = odd_ref[0:rows, :]


def give_ends(flag, y_ref, even_ref, odd_ref):
    rows = XH * 8
    even_at = pl.multiple_of(jnp.where(flag == 1, 0, rows), 8)
    odd_at = pl.multiple_of(jnp.where(flag == 1, rows, 0), 8)
    even_ref[0:rows, :] = y_ref[pl.ds(even_at, rows), :]
    odd_ref[0:rows, :] = y_ref[pl.ds(odd_at, rows), :]


def prep_slots_kernel(flags, offs, strg, cnt, proj, mu, t_ref, meta_ref, xe_ref, xo_ref, g_ref, mu_out, xr_ref, xl_ref):
    mu_out[...] = mu[...]
    at_row = lax.broadcasted_iota(jnp.int32, (1024, 128), 0)
    at_column = lax.broadcasted_iota(jnp.int32, (1024, 128), 1)
    same = (at_row % 128 // 8 == at_column // 8) & (at_row // 128 == at_column % 8)
    g_ref[...] = jnp.where(same, 1.0, 0.0).astype(BF16)
    sub, lane = iotas()
    left_half = lane < 64
    group = lane // 8
    meta = jnp.zeros((8, 128), F32)
    for s in range(8):
        for column in range(3):
            value = offs[column, s].astype(F32)
            meta = jnp.where((group == s) & (sub == column), value, meta)
        alive = jnp.where(s < cnt[0], 1.0, 0.0).astype(F32)
        for p in range(8):
            weight = strg[s, p] * alive * (1.0 / (512.0 * filter_half))
            meta = jnp.where((lane == s * 8 + p) & (sub == 3), weight, meta)
    meta_ref[...] = meta
    for i in range(8):
        for j in range(8):
            start = (i % 2) * 64 + j * 8
            total = jnp.zeros((8, 128), F32)
            for s in range(8):
                source = proj[s, :, 128 * (i // 2) : 128 * (i // 2) + 128]
                shift = (s * 8 - start) % 128
                moved = pltpu.roll(source, shift, 1) if shift else source
                total = jnp.where(group == s, moved, total)
            put(t_ref, i * 8 + j, total)
    for i in range(2):
        for j in range(8):
            for ref, first in ((xr_ref, 4), (xl_ref, 0)):
                one = get(t_ref, (first + i) * 8 + j)
                two = pltpu.roll(get(t_ref, (first + 2 + i) * 8 + j), 64, 1)
                put(ref, i * 8 + j, jnp.where(left_half, one, two))
    put(xr_ref, 16, meta)
    put(xl_ref, 16, meta)
    send(flags[0], xl_ref, xr_ref, xe_ref, xo_ref, 17)
    for x in range(HALO):
        for h in range(2):
            left, right = mu[x, 8 * h : 8 * h + 8, :], mu[CX - HALO + x, 8 * h : 8 * h + 8, :]
            put(xe_ref, 17 + 2 * x + h, jnp.where(flags[0] == 1, left, right))
            put(xo_ref, 17 + 2 * x + h, jnp.where(flags[0] == 1, right, left))


def prep_fields_kernel(orb, pot, y_ref, pot_out):
    pot_out[...] = pot[...]
    for x in range(CX):
        for o in range(ORB):
            for h in range(2):
                y_ref[pl.ds(x * 64 + 4 * h + o, 8, stride=8), :] = orb[o, x, 8 * h : 8 * h + 8, :]


X_SUMS, Y_SUMS = XH, YH
X_ALL, Y_MU = XH + 3, YH + 4
Y_ALL = Y_MU + CX


def send_rims(flag, y_ref, rims, ye_ref, yo_ref):
    low = iotas()[0] < 4
    rows = YH * 8
    pack_rims(y_ref, rims.at[pl.ds(rows, rows)], rims.at[pl.ds(0, rows)], low)
    ye_ref[0:rows, :] = rims[pl.ds(pl.multiple_of(jnp.where(flag == 1, 0, rows), 8), rows), :]
    yo_ref[0:rows, :] = rims[pl.ds(pl.multiple_of(jnp.where(flag == 1, rows, 0), 8), rows), :]


def widen_kernel(flags, t_ref, meta_ref, xo_ref, xe_ref, t2_ref, m_ref, ye_ref, yo_ref, fl_ref, fr_ref, hi_ref, lo_ref):
    _, lane = iotas()
    left_half = lane < 64
    base = 0
    for t in range(17):
        left, right = sides(flags[0] == 1, get(xe_ref, t), get(xo_ref, t))
        put(fl_ref, t, left)
        put(fr_ref, t, right)
    for i in range(8):
        for j in range(8):
            if i >= 4:
                other = get(fl_ref, base + (i % 2) * 8 + j)
                other = other if i >= 6 else pltpu.roll(other, 64, 1)
            else:
                other = get(fr_ref, base + (i % 2) * 8 + j)
                other = other if i >= 2 else pltpu.roll(other, 64, 1)
            both = jnp.where(left_half, get(t_ref, i * 8 + j), other)
            put(t2_ref, i * 8 + j, both)
            if j >= 4:
                put(hi_ref, i * 4 + j - 4, both)
            else:
                put(lo_ref, i * 4 + j, both)
    meta = meta_ref[...]
    for side, ref in enumerate((fl_ref, fr_ref)):
        both = jnp.where(left_half, meta, pltpu.roll(get(ref, base + 16), 64, 1))
        put(m_ref, side, both)
        put(hi_ref, 32 + side, both)
        put(lo_ref, 32 + side, both)
    send(flags[1], lo_ref, hi_ref, ye_ref, yo_ref, 34)


def coef_kernel(flags, mu, pot, xe_ref, xo_ref, ye_ref, yo_ref, dz_ref, out_ref, ex, ey):
    sub, _ = iotas()
    low = sub < 4

    def two(a, ia, b, ib):
        return jnp.where(low, row(a, ia), row(b, ib))

    ends = [sides(flags[0] == 1, get(xe_ref, 17 + t), get(xo_ref, 17 + t)) for t in range(2 * HALO)]
    for x in range(CX + 2 * HALO):
        if x < HALO:
            a, b = ends[2 * x][0], ends[2 * x + 1][0]
        elif x < HALO + CX:
            a, b = mu[x - HALO, 0:8, :], mu[x - HALO, 8:16, :]
        else:
            a, b = ends[2 * (x - HALO - CX)][1], ends[2 * (x - HALO - CX) + 1][1]
        for yl in range(8):
            put(ex, x * 8 + yl, two(a, yl, b, yl))
    for x in range(CX):
        lo_rim, hi_rim = sides(flags[1] == 1, get(ye_ref, Y_MU + x), get(yo_ref, Y_MU + x))
        parts = [lo_rim, mu[x, 0:8, :], mu[x, 8:16, :], hi_rim]
        for n in range(20):
            y = n - HALO
            put(ey, x * 20 + n, two(parts[(y + 8) // 8], y % 8, parts[(y + 16) // 8], y % 8))
    field = ex[XH * 8 : (XH + TILES) * 8, :]
    high, rest = split(field)
    zd = mm(high, dz_ref[0:NZ, 0:NZ]) + mm(rest, dz_ref[0:NZ, 0:NZ]) + mm(high, dz_ref[NZ : 2 * NZ, 0:NZ])
    out_ref[3 * 768 : 4 * 768, :] = zd * (-0.5 / filter_half)

    def body(x, carry):
        va, vb = pot[x, 0:8, :], pot[x, 8:16, :]
        for yl in range(8):
            gx = jnp.zeros((8, 128), F32)
            gy = jnp.zeros((8, 128), F32)
            for k in range(1, HALO + 1):
                gx += first_coefs[k - 1] * (get_at(ex, (x + HALO + k) * 8 + yl) - get_at(ex, (x + HALO - k) * 8 + yl))
                gy += first_coefs[k - 1] * (
                    get_at(ey, x * 20 + HALO + yl + k) - get_at(ey, x * 20 + HALO + yl - k)
                )
            r = x * 8 + yl
            center = get_at(ex, (x + HALO) * 8 + yl)

            def store(which, value):
                out_ref[pl.ds(pl.multiple_of((which * TILES + r) * 8, 8), 8), :] = value

            store(0, (1.0 + center) * (-0.5 / filter_half))
            store(1, gx * (-0.5 / filter_half))
            store(2, gy * (-0.5 / filter_half))
            store(4, (two(va, yl, vb, yl) - filter_center) * (1.0 / filter_half))
        return carry

    lax.fori_loop(0, CX, body, 0)


def block_tiles(xt, yq):
    return [(4 * xt + a) * 8 + 4 * yq for a in range(4)]


def side_of(xt):
    return 1 if xt == 2 else 0


def partial_coeffs(y_ref, q_ref, s_ref, g_ref, z_ref, acc):
    left_half = lax.broadcasted_iota(jnp.int32, (8, 1024), 1) % 128 < 64
    own = None
    ends = {}
    rims = [None, None]
    corners = {}
    for xt in range(3):
        for yq in range(2):
            b = xt * 2 + yq
            field = jnp.concatenate([y_ref[t * 8 : t * 8 + 32, :] for t in block_tiles(xt, yq)], axis=0)
            table = s_ref[(side_of(xt) * 2 + yq) * 128 : (side_of(xt) * 2 + yq) * 128 + 128, :]
            seen = pick(field, table).reshape(16, 8, 256)
            sums = []
            for p in range(8):
                base = (b * 8 + p) * 128
                product = seen * q_ref[base : base + 128, :].reshape(16, 8, 256)
                total = jnp.sum(product, axis=0)
                sums.append(total + pltpu.roll(total, 4, 0))
            col_a = jnp.concatenate([t[:, :128] for t in sums], axis=1)
            col_b = jnp.concatenate([t[:, 128:] for t in sums], axis=1)
            own = col_a if own is None else own + col_a
            rims[yq] = col_b if rims[yq] is None else rims[yq] + col_b
            if xt != 1:
                ends[xt] = ends[xt] + col_a if xt in ends else col_a
                corners[(xt, yq)] = col_b
    for side, xt in enumerate((0, 2)):
        acc[side * 24 : side * 24 + 8, :] = jnp.where(left_half, own, ends[xt])
        for yq in range(2):
            at = side * 24 + 8 + yq * 8
            acc[at : at + 8, :] = jnp.where(left_half, rims[yq], corners[(xt, yq)])
    z_ref[...] = pick(acc[...], g_ref[...])


def send_coeffs(flag, z_ref, ye_ref, yo_ref, base):
    for side in range(2):
        for n, (above, below) in enumerate(((2, 1), (0, 0))):
            above, below = get(z_ref, side * 3 + above), get(z_ref, side * 3 + below)
            put(ye_ref, base + side * 2 + n, jnp.where(flag == 1, below, above))
            put(yo_ref, base + side * 2 + n, jnp.where(flag == 1, above, below))


def build_kernel(
    flags, t2_ref, m_ref, yo_ref, ye_ref, y_ref, mu, g_ref,
    q_ref, s_ref, w_ref, z_ref, nye_ref, nyo_ref, tx, acc, lo_ref, hi_ref, rims
):
    for t in range(34):
        lo, hi = sides(flags[1] == 1, get(ye_ref, t), get(yo_ref, t))
        put(lo_ref, t, lo)
        put(hi_ref, t, hi)
    sub, lane = iotas()
    low = sub < 4
    right_half = lane >= 64
    metas = [get(m_ref, 0), get(lo_ref, 32), get(hi_ref, 32), get(m_ref, 1), get(lo_ref, 33), get(hi_ref, 33)]
    for t in range(6):
        put(w_ref, t, row(metas[t], 3))
    zi = lax.broadcasted_iota(jnp.int32, (128, 128), 0)
    for side in range(2):
        for yq in range(2):
            for col, t in enumerate((side * 3, side * 3 + 1 + yq)):
                place = metas[t][2:3, :].astype(jnp.int32) + lane[0:1, :] % 8
                base = (side * 2 + yq) * 128
                hot = jnp.where(zi == jnp.broadcast_to(place, (128, 128)), 1.0, 0.0).astype(BF16)
                s_ref[base : base + 128, col * 128 : col * 128 + 128] = hot

    def table(col, i, j):
        if col == 0:
            return get(t2_ref, i * 8 + j)
        return get(lo_ref, i * 4 + j - 4) if j >= 4 else get(hi_ref, i * 4 + j)

    zero = jnp.zeros((8, 128), F32)
    for xt in range(3):
        shift = (-12.0, 1000.0, 12.0)[xt]
        for col in range(2):
            for yq in range(2):
                b = xt * 2 + yq
                t = side_of(xt) * 3 + (0 if col == 0 else 1 + yq)
                x0 = row(metas[t], 0) - 6.0 + jnp.where(right_half, shift, 0.0)
                y0 = row(metas[t], 1) - 6.0
                if col == 1:
                    y0 = y0 + (16.0 if yq == 1 else -16.0)
                js = range(8) if col == 0 else (range(0, 4) if yq == 1 else range(4, 8))
                if col == 1 or yq == 0:
                    for a in range(4):
                        for j in js:
                            moved = zero
                            for i in range(8):
                                moved = jnp.where(x0 == float(4 * xt + a - i), table(col, i, j), moved)
                            put(tx, a * 8 + j, moved)
                for a in range(4):
                    for c in range(4):
                        rows = []
                        for h in range(2):
                            y = 8 * h + 4 * yq + c
                            moved = zero
                            if col == 0 or h == yq:
                                for j in js:
                                    moved = jnp.where(y0 == float(y - j), get(tx, a * 8 + j), moved)
                            rows.append(moved)
                        for p in range(8):
                            base = ((b * 8 + p) * 16 + a * 4 + c) * 8
                            value = jnp.where(low, row(rows[0], p), row(rows[1], p))
                            q_ref[base : base + 8, col * 128 : col * 128 + 128] = value
    partial_coeffs(y_ref, q_ref, s_ref, g_ref, z_ref, acc)
    send_coeffs(flags[1], z_ref, nye_ref, nyo_ref, Y_SUMS)
    send_rims(flags[1], y_ref, rims, nye_ref, nyo_ref)
    for x in range(CX):
        below, above = mu[x, 0:8, :], mu[x, 8:16, :]
        put(nye_ref, Y_MU + x, jnp.where(flags[1] == 1, below, above))
        put(nyo_ref, Y_MU + x, jnp.where(flags[1] == 1, above, below))


def fold_kernel(flags, z_ref, y_ref, yo_ref, ye_ref, out_ref, xe_ref, xo_ref):
    give_ends(flags[0], y_ref, xe_ref, xo_ref)
    base = Y_SUMS
    for side in range(2):
        own, lo, hi = (get(z_ref, side * 3 + t) for t in range(3))
        across = [(get(ye_ref, base + side * 2 + n), get(yo_ref, base + side * 2 + n)) for n in range(2)]
        from_lo, from_hi = sides(flags[1] == 1, *across[1])
        put(out_ref, side * 3, own + across[0][0] + across[0][1])
        put(out_ref, side * 3 + 1, lo + from_lo)
        put(out_ref, side * 3 + 2, hi + from_hi)
    for t in range(3):
        left, right = pltpu.roll(get(out_ref, t), 64, 1), pltpu.roll(get(out_ref, 3 + t), 64, 1)
        put(xe_ref, X_SUMS + t, jnp.where(flags[0] == 1, left, right))
        put(xo_ref, X_SUMS + t, jnp.where(flags[0] == 1, right, left))


def step_kernel(
    step, flags, y_ref, prev_ref, xo_ref, xe_ref, yo_ref, ye_ref, coef_ref, q_ref, s_ref, w_ref, z_ref,
    dz_ref, g_ref, *rest
):
    last = step == STEPS
    if last:
        first_ref, second_ref, ex, ey, zd, wp, rims, new_ref = rest
    else:
        new_ref, nye_ref, nyo_ref, zn_ref, ex, ey, zd, wp, rims, acc = rest
    sub, lane = iotas()
    low = sub < 4
    scale = 1.0 if step == 1 else 2.0

    high, rest_part = split(y_ref[...])
    zd[...] = mm(high, dz_ref[0:NZ, :]) + mm(rest_part, dz_ref[0:NZ, :]) + mm(high, dz_ref[NZ : 2 * NZ, :])

    take(flags[0], xe_ref, xo_ref, ex, XH * 8, 0, (XH + TILES) * 8)
    take(flags[1], ye_ref, yo_ref, rims, YH * 8, 0, YH * 8)
    ex[XH * 8 : (XH + TILES) * 8, :] = y_ref[...]
    for x in range(CX):
        for yl in range(8):
            put(ey, x * 20 + HALO + yl, get(y_ref, x * 8 + yl))
        lo_rims = [get(rims, x * 3 + m) for m in range(3)]
        hi_rims = [get(rims, YH + x * 3 + m) for m in range(3)]
        for m in range(HALO):
            rim = lo_rims[m] if m < 3 else pltpu.roll(lo_rims[m - 3], 4, 0)
            put(ey, x * 20 + m, jnp.where(low, rim, pltpu.roll(get(y_ref, x * 8 + 2 + m), 4, 0)))
            rim = pltpu.roll(hi_rims[m], 4, 0) if m < 3 else hi_rims[m - 3]
            put(ey, x * 20 + HALO + 8 + m, jnp.where(low, pltpu.roll(get(y_ref, x * 8 + m), 4, 0), rim))

    def body(x, carry):
        for yl in range(8):
            r = x * 8 + yl
            center = get_at(y_ref, r)
            gx = gy = lap = None
            for k in range(1, HALO + 1):
                xp, xm = get_at(ex, (x + HALO + k) * 8 + yl), get_at(ex, (x + HALO - k) * 8 + yl)
                yp, ym = get_at(ey, x * 20 + HALO + yl + k), get_at(ey, x * 20 + HALO + yl - k)
                tx = first_coefs[k - 1] * (xp - xm)
                ty = first_coefs[k - 1] * (yp - ym)
                tl = second_coefs[k - 1] * ((xp + xm) + (yp + ym))
                gx, gy, lap = (tx, ty, tl) if k == 1 else (gx + tx, gy + ty, lap + tl)
            at = pl.ds(pl.multiple_of(r * 8, 8), 8)
            total = get_at(coef_ref, r) * (lap + zd[at, NZ:])
            total += get_at(coef_ref, TILES + r) * gx
            total += get_at(coef_ref, 2 * TILES + r) * gy
            total += get_at(coef_ref, 3 * TILES + r) * zd[at, :NZ]
            total += get_at(coef_ref, 4 * TILES + r) * center
            new_ref[at, :] = total if step == 1 else 2.0 * total - get_at(prev_ref, r)
        return carry

    lax.fori_loop(0, CX, body, 0)

    left_half = lane < 64
    from_x = [sides(flags[0] == 1, get(xe_ref, X_SUMS + t), get(xo_ref, X_SUMS + t)) for t in range(3)]
    tiles = []
    for side in range(2):
        for t in range(3):
            near, far = from_x[t][side], from_x[t][1 - side]
            tiles.append(get(z_ref, side * 3 + t) + near + jnp.where(left_half, far, 0.0))
    weights = jnp.concatenate(tiles, axis=0) * w_ref[...] * scale
    wp[...] = pick_t(weights, g_ref[...])

    for xt in range(3):
        for yq in range(2):
            b = xt * 2 + yq
            ta, tb = side_of(xt) * 3, side_of(xt) * 3 + 1 + yq
            total = None
            for p in range(8):
                weight = jnp.concatenate(
                    [wp[t * 8 : t * 8 + 8, p * 128 : p * 128 + 128] for t in (ta, tb)], axis=1
                )
                base = (b * 8 + p) * 128
                term = weight[None] * q_ref[base : base + 128, :].reshape(16, 8, 256)
                total = term if total is None else total + term
            table = s_ref[(side_of(xt) * 2 + yq) * 128 : (side_of(xt) * 2 + yq) * 128 + 128, :]
            spread = pick_t(total.reshape(128, 256), table)
            for a, t in enumerate(block_tiles(xt, yq)):
                new_ref[t * 8 : t * 8 + 32, :] += spread[a * 32 : a * 32 + 32, :]

    if last:
        half = TILES * 4
        first_ref[...] = new_ref[0:half, :]
        second_ref[...] = new_ref[half : 2 * half, :]
    else:
        send_rims(flags[1], new_ref, rims, nye_ref, nyo_ref)
        partial_coeffs(new_ref, q_ref, s_ref, g_ref, zn_ref, acc)
        send_coeffs(flags[1], zn_ref, nye_ref, nyo_ref, Y_SUMS)


def two_layers(refs, x):
    half, at = x // (CX // 2), x % (CX // 2) * 64
    sides = [[refs[2 * n + half][a : a + 64, :] for n in range(4)] for a in (at, at + 64)]
    return jnp.concatenate([jnp.concatenate(side, axis=0) for side in sides], axis=1)


def ring_orbitals(order):
    orbital = lax.broadcasted_iota(jnp.int32, (16, 256), 0)
    held_at = lax.broadcasted_iota(jnp.int32, (16, 256), 1)
    device = held_at // 64
    owner = jnp.where(device == 0, order[0], jnp.where(device == 1, order[1], jnp.where(device == 2, order[2], order[3])))
    return jnp.where(orbital == owner * 4 + held_at % 4, 1.0, 0.0).astype(F32)


def gram_kernel(order, *refs):
    out_ref = refs[8]
    total = mixed = None
    for x in range(0, CX, 2):
        high, low = split(two_layers(refs, x))
        one, two = mm_t(high, high), mm_t(high, low)
        total, mixed = (one, two) if x == 0 else (total + one, mixed + two)
    total = total + mixed + mixed.T
    rows = lax.broadcasted_iota(jnp.int32, (256, 256), 0)
    columns = lax.broadcasted_iota(jnp.int32, (256, 256), 1)
    total = jnp.where((rows % 64) // 4 == (columns % 64) // 4, total, 0.0)
    hot = ring_orbitals(order)
    first = jnp.dot(hot, total, precision=lax.Precision.HIGHEST, preferred_element_type=F32)
    small = lax.dot_general(
        first, hot, (((1,), (1,)), ((), ())), precision=lax.Precision.HIGHEST, preferred_element_type=F32
    )
    out_ref[...] = jnp.zeros((8, 128), F32)
    out_ref[:, 0:16] = small[0:8]
    out_ref[:, 16:32] = small[8:16]


def rotate_kernel(cells, order, corr_ref, *refs):
    out_ref, flat = refs[8:]
    lane = lax.broadcasted_iota(jnp.int32, (16, 128), 1)
    rows = lax.broadcasted_iota(jnp.int32, (16, 128), 0)
    packed = corr_ref[...]
    whole = jnp.concatenate([packed, pltpu.roll(packed, 112, 1)], axis=0)
    work = jnp.where(lane < 16, whole * (1.0 / cells), jnp.where(lane == rows + 16, 1.0, 0.0))
    pivots = jnp.ones((16, 128), F32)
    for k in range(16):
        pivot_row = jnp.broadcast_to(work[k : k + 1, :], (16, 128))
        column = jnp.broadcast_to(work[:, k : k + 1], (16, 128))
        pivot = jnp.broadcast_to(column[k : k + 1, :], (16, 128))
        pivots = jnp.where(rows == k, pivot, pivots)
        work = jnp.where(rows > k, work - column / pivot * pivot_row, work)
    inverse = (work / jnp.sqrt(pivots))[:, 16:32]
    me = order[0]
    own_row = lax.broadcasted_iota(jnp.int32, (64, 16), 0)
    orbital = lax.broadcasted_iota(jnp.int32, (64, 16), 1)
    left = jnp.where(orbital == me * 4 + own_row % 4, 1.0, 0.0).astype(F32)
    right = ring_orbitals(order)
    exact = functools.partial(jnp.dot, precision=lax.Precision.HIGHEST, preferred_element_type=F32)
    mixing = exact(exact(left, inverse), right)
    at_row = lax.broadcasted_iota(jnp.int32, (64, 256), 0)
    at_column = lax.broadcasted_iota(jnp.int32, (64, 256), 1)
    mixing = jnp.where(at_row // 4 == at_column % 64 // 4, mixing, 0.0)
    mix_high, mix_low = split(mixing)
    for x in range(0, CX, 2):
        high, low = split(two_layers(refs, x))
        both = mm(mix_high, high) + mm(mix_high, low) + mm(mix_low, high)
        flat[x * 64 : x * 64 + 64, :] = both[:, :NZ]
        flat[x * 64 + 64 : x * 64 + 128, :] = both[:, NZ:]
    for o in range(ORB):
        for x in range(CX):
            for h in range(2):
                out_ref[o, x, 8 * h : 8 * h + 8, :] = flat[pl.ds(x * 64 + 4 * h + o, 8, stride=8), :]


def kernel_call(body, outs, ins, scratch=(), name=None):
    return pl.pallas_call(
        body,
        out_shape=[jax.ShapeDtypeStruct(shape, dtype) for shape, dtype in outs],
        in_specs=ins,
        out_specs=[VMEM] * len(outs),
        scratch_shapes=list(scratch),
        compiler_params=pltpu.CompilerParams(vmem_limit_bytes=LIMIT),
        name=name,
    )


def blocks(count, columns=128, dtype=F32):
    return (count * 8, columns), dtype


def exchange(even_value, odd_value, axis):
    count = lax.axis_size(axis)
    results = []
    for first, value in ((1, odd_value), (0, even_value)):
        pairs = [p for i in range(first, count - 1, 2) for p in ((i, i + 1), (i + 1, i))]
        results.append(lax.ppermute(value, axis, pairs))
    return results[1], results[0]


def spread_sum(value, axis):
    copies = jnp.broadcast_to(value[None], (lax.axis_size(axis),) + value.shape)
    return jnp.sum(lax.all_to_all(copies, axis, 0, 0, tiled=True), axis=0)


def fold(flags, z, y, even, odd):
    return kernel_call(
        fold_kernel, [blocks(6), blocks(X_ALL), blocks(X_ALL)], [SMEM] + [VMEM] * 4, name="fold_coeffs"
    )(flags, z, y, odd, even)


def shards(orbitals, potential, kinetic_mu, projectors, strengths, box_offsets, block_counts):
    dz = jnp.asarray(derivative_table())
    flags = jnp.stack([lax.axis_index("gx") % 2, lax.axis_index("gy") % 2]).astype(jnp.int32)
    t, meta, xte, xto, groups, mu = kernel_call(
        prep_slots_kernel,
        [blocks(64), blocks(1), blocks(17 + 2 * HALO), blocks(17 + 2 * HALO)]
        + [((1024, 128), BF16), ((CX, CY, NZ), F32)],
        [SMEM] * 4 + [VMEM] * 2,
        [pltpu.VMEM((17 * 8, 128), F32)] * 2,
        name="prepare_slots",
    )(flags, box_offsets.T, strengths, block_counts, projectors, kinetic_mu)
    orbitals, xte, xto = lax.optimization_barrier((orbitals, xte, xto))
    xte, xto = exchange(xte, xto, "gx")
    y, pot = kernel_call(
        prep_fields_kernel,
        [blocks(TILES), ((CX, CY, NZ), F32)],
        [VMEM] * 2,
        name="prepare_fields",
    )(orbitals, potential)
    t2, metas, ye2, yo2 = kernel_call(
        widen_kernel,
        [blocks(64), blocks(2), blocks(34), blocks(34)],
        [SMEM] + [VMEM] * 4,
        [pltpu.VMEM((17 * 8, 128), F32)] * 2 + [pltpu.VMEM((34 * 8, 128), F32)] * 2,
        name="widen",
    )(flags, t, meta, xto, xte)
    ye2, yo2 = exchange(ye2, yo2, "gy")
    q, s, w, z, ye, yo = kernel_call(
        build_kernel,
        [blocks(6 * 8 * 16, 256), ((4 * 128, 256), BF16), blocks(6), blocks(6), blocks(Y_ALL), blocks(Y_ALL)],
        [SMEM] + [VMEM] * 7,
        [
            pltpu.VMEM((32 * 8, 128), F32),
            pltpu.VMEM((48, 1024), F32),
            pltpu.VMEM((34 * 8, 128), F32),
            pltpu.VMEM((34 * 8, 128), F32),
            pltpu.VMEM((2 * YH * 8, 128), F32),
        ],
        name="build",
    )(flags, t2, metas, yo2, ye2, y, mu, groups)
    ye, yo = exchange(ye, yo, "gy")
    z, xe, xo = fold(flags, z, y, ye, yo)
    xe, xo = exchange(xe, xo, "gx")
    (coefs,) = kernel_call(
        coef_kernel,
        [blocks(5 * TILES)],
        [SMEM] + [VMEM] * 7,
        [pltpu.VMEM(((TILES + 2 * XH) * 8, 128), F32), pltpu.VMEM((CX * 20 * 8, 128), F32)],
        name="coefficients",
    )(flags, mu, pot, xte, xto, ye, yo, dz)

    previous = y
    for step in range(1, STEPS + 1):
        last = step == STEPS
        if last:
            outs = [blocks(TILES // 2), blocks(TILES // 2)]
        else:
            outs = [blocks(TILES), blocks(Y_MU), blocks(Y_MU), blocks(6)]
        result = kernel_call(
            functools.partial(step_kernel, step),
            outs,
            [SMEM] + [VMEM] * 13,
            [
                pltpu.VMEM(((TILES + 2 * XH) * 8, 128), F32),
                pltpu.VMEM((CX * 20 * 8, 128), F32),
                pltpu.VMEM((TILES * 8, 256), F32),
                pltpu.VMEM((48, 1024), F32),
                pltpu.VMEM((2 * YH * 8, 128), F32),
                pltpu.VMEM((TILES * 8, 128) if last else (48, 1024), F32),
            ],
            name="step",
        )(flags, y, previous, xo, xe, yo, ye, coefs, q, s, w, z, dz, groups)
        previous = y
        if not last:
            y, ye, yo, z = result
            ye, yo = exchange(ye, yo, "gy")
            z, xe, xo = fold(flags, z, y, ye, yo)
            xe, xo = exchange(xe, xo, "gx")

    count = lax.axis_size("orb")
    me = lax.axis_index("orb")
    even = [(i, i ^ 1) for i in range(count)]
    odd = [(i, count - 1 - i) for i in range(count)]
    parts = result
    one_a, other_b = lax.ppermute(parts[0], "orb", even), lax.ppermute(parts[1], "orb", odd)
    one_b, other_a = lax.ppermute(parts[1], "orb", even), lax.ppermute(parts[0], "orb", odd)
    across_a, across_b = lax.ppermute(one_a, "orb", odd), lax.ppermute(other_b, "orb", even)
    gathered = (parts[0], parts[1], one_a, one_b, other_a, other_b, across_a, across_b)
    order = jnp.stack([me, me ^ 1, count - 1 - me, (me + 2) % count]).astype(jnp.int32)
    (corr,) = kernel_call(
        gram_kernel,
        [blocks(1)],
        [SMEM] + [VMEM] * 8,
        name="gram",
    )(order, *gathered)
    for axis in ("gx", "gy"):
        corr = spread_sum(corr, axis)
    cells = CX * CY * NZ * lax.axis_size("gx") * lax.axis_size("gy")
    (result,) = kernel_call(
        functools.partial(rotate_kernel, cells),
        [((ORB, CX, CY, NZ), F32)],
        [SMEM] + [VMEM] * 9,
        [pltpu.VMEM((TILES * 8, 128), F32)],
        name="rotate",
    )(order, corr, *gathered)
    return result


def solution(mesh):
    in_specs = (
        P("orb", "gx", "gy", None),
        P("gx", "gy", None),
        P("gx", "gy", None),
        P(("gx", "gy"), None, None),
        P(("gx", "gy"), None),
        P(("gx", "gy"), None),
        P(("gx", "gy")),
    )
    out_specs = P("orb", "gx", "gy", None)
    return jax.shard_map(shards, mesh=mesh, in_specs=in_specs, out_specs=out_specs, check_vma=False)
```
